256 devices in a mesh: seq: 16 (over z_lo, x), ri: 4 (over z_hi, core), rj: 4 (over y).
Axes of the slice: x: 4, y: 4, z: 8 (z_hi: 2, z_lo: 4; z = z_hi * 4 + z_lo), core: 2. Of those that a mesh axis runs over, the one named last changes fastest.
Arguments:
- homolog_embedding: bfloat16 [256, 512, 256], P('seq', 'ri'), may hold values from -6 to 6
- pairwise_state: bfloat16 [512, 512, 128], P('ri', ('seq', 'rj')), may hold values from -6 to 6
- residue_mask: int32 [512], replicated, may hold values 0 or 1
- alignment_row_mask: int32 [256], replicated, may hold values 0 or 1
- focus_layer_scale: float32 [256], replicated, may hold values from 0.25 to 1.75
- asking_projector: bfloat16 [256, 256], P(None, 'rj'), may hold values from -1 to 1
- lookup_projector: bfloat16 [256, 256], P(None, 'rj'), may hold values from -1 to 1
- content_projector: bfloat16 [256, 256], P(None, 'rj'), may hold values from -0.375 to 0.375
- sigmoid_projector: bfloat16 [256, 256], P(None, 'rj'), may hold values from -0.375 to 0.375
- gate_offset_bias: float32 [256], replicated, may hold values from -4 to 4
- final_projector: bfloat16 [256, 256], P('rj'), may hold values from -1.5 to 1.5
- pairwise_norm_gain: float32 [128], replicated, may hold values from 0.25 to 1.75
- bias_weight: bfloat16 [128, 8], replicated, may hold values from -5 to 5
- cross_layer_scale: float32 [256], replicated, may hold values from 0.25 to 1.75
- first_cross_projector: bfloat16 [256, 32], replicated, may hold values from -0.375 to 0.375
- second_cross_projector: bfloat16 [256, 32], replicated, may hold values from -0.375 to 0.375
- outer_weight: bfloat16 [1024, 128], replicated, may hold values from -3 to 3
Outputs:
- alignment_output: bfloat16 [256, 512, 256], P('seq', 'ri')
- pairwise_output: bfloat16 [512, 512, 128], P('ri', ('seq', 'rj'))
The draws below stay inside these ranges and needn't reach their ends.
All inputs are finite; a program needn't handle non-finite values.
Results may differ from the reference program's by a relative error of at most 0.015.
The reference program's roundings to bfloat16 on the way count: a program that leaves them out, or rounds other values in their place, can miss the bound.
Values may be sent and summed in bfloat16 or wider, within the bound.
A program may use at most 64 MiB of HBM per device.

```python
import jax
import jax.numpy as jnp
from jax import lax

FEATURE_DEPTH = 256
CZ = 128
FOCUS_SPLITS = 8
SPLIT_DEPTH = 32
CROSS_FEATURES = 32
RES_BLK = 128
HOMOLOG_TOTAL = 256
AMINO_TOTAL = 512
N_RI = 4


def draw_bias_weight(key, part):
    key = jax.random.fold_in(key, 11)
    sample = jnp.clip(jax.random.normal(key, (CZ, FOCUS_SPLITS), jnp.float32) * 5.0 * CZ ** (-0.5), -5.0, 5.0)
    return sample.astype(jnp.bfloat16)


def with_ends(entries, rng, low, top_value):
    place = [jax.random.randint(jax.random.fold_in(rng, axis), (), 0, length) for axis, length in enumerate(entries.shape)]
    main_axis = entries.shape.index(max(entries.shape))
    beside = place[:main_axis] + [(place[main_axis] + 1) % entries.shape[main_axis]] + place[main_axis + 1:]
    return entries.at[tuple(place)].set(low).at[tuple(beside)].set(top_value)


def levels(rng, dims, shards, least, largest):
    def one(dim, parts):
        heights = jax.random.uniform(jax.random.fold_in(jax.random.fold_in(rng, 6), dim), (parts,), jnp.float32, least / len(shards), largest / len(shards))
        return jnp.repeat(jnp.exp(heights), dims[dim] // parts).reshape((-1,) + (1,) * (len(dims) - dim - 1))

    level = one(*shards[0])
    for cut in shards[1:]:
        level = level * one(*cut)
    return level


def gaussian(key, dims, deviation, most, pieces=(), kind=jnp.bfloat16):
    drawn = jax.random.normal(key, dims, jnp.float32) * deviation
    if len(pieces) > 0:
        drawn = levels(key, dims, pieces, -0.22, 0.18) * drawn
    return jnp.clip(drawn, min=-most, max=most).astype(kind)


def setup_inputs(seed: int = 0) -> dict:
    key_list = jax.random.split(jax.random.key(seed), 18)
    homolog_embedding = gaussian(key_list[0], (HOMOLOG_TOTAL, AMINO_TOTAL, FEATURE_DEPTH), 1.0, 6.0, ((0, 16), (1, 4)))
    pairwise_state = gaussian(key_list[1], (AMINO_TOTAL, AMINO_TOTAL, CZ), 1.0, 6.0, ((0, 4), (1, 64)))
    residue_mask = with_ends((jax.random.randint(key_list[2], (AMINO_TOTAL,), 0, 8) < 7).astype(jnp.int32), jax.random.fold_in(key_list[2], 1), 0, 1)
    alignment_row_mask = with_ends((jax.random.randint(key_list[3], (HOMOLOG_TOTAL,), 0, 4) < 3).astype(jnp.int32), jax.random.fold_in(key_list[3], 1), 0, 1)
    focus_layer_scale = jnp.clip(1.0 + 0.15 * jax.random.normal(key_list[4], (FEATURE_DEPTH,), jnp.float32), 0.25, 1.75)
    asking_projector = gaussian(key_list[5], (FEATURE_DEPTH, FOCUS_SPLITS * SPLIT_DEPTH), (FEATURE_DEPTH // 8) ** -0.5, 1.0, ((1, 4),))
    lookup_projector = gaussian(key_list[6], (FEATURE_DEPTH, FOCUS_SPLITS * SPLIT_DEPTH), (FEATURE_DEPTH // 8) ** -0.5, 1.0, ((1, 4),))
    content_projector = gaussian(key_list[7], (FEATURE_DEPTH, FOCUS_SPLITS * SPLIT_DEPTH), FEATURE_DEPTH ** -0.5, 0.375, ((1, 4),))
    sigmoid_projector = gaussian(key_list[8], (FEATURE_DEPTH, FOCUS_SPLITS * SPLIT_DEPTH), FEATURE_DEPTH ** -0.5, 0.375, ((1, 4),))
    gate_offset_bias = gaussian(key_list[9], (FOCUS_SPLITS * SPLIT_DEPTH,), 1.0, 4.0, (), jnp.float32)
    final_projector = gaussian(key_list[10], (FOCUS_SPLITS * SPLIT_DEPTH, FEATURE_DEPTH), (FOCUS_SPLITS * SPLIT_DEPTH // 16) ** -0.5, 1.5, ((0, 4),))
    pairwise_norm_gain = jnp.clip(1.0 + 0.15 * jax.random.normal(key_list[11], (CZ,), jnp.float32), 0.25, 1.75)
    bias_weight = draw_bias_weight(jax.random.fold_in(key_list[17], 71), 0)
    cross_layer_scale = jnp.clip(1.0 + 0.15 * jax.random.normal(key_list[13], (FEATURE_DEPTH,), jnp.float32), 0.25, 1.75)
    first_cross_projector = gaussian(key_list[14], (FEATURE_DEPTH, CROSS_FEATURES), FEATURE_DEPTH ** -0.5, 0.375)
    second_cross_projector = gaussian(key_list[15], (FEATURE_DEPTH, CROSS_FEATURES), FEATURE_DEPTH ** -0.5, 0.375)
    outer_weight = gaussian(key_list[16], (CROSS_FEATURES * CROSS_FEATURES, CZ), 0.5, 3.0)
    return dict(homolog_embedding=homolog_embedding, pairwise_state=pairwise_state, residue_mask=residue_mask, alignment_row_mask=alignment_row_mask, focus_layer_scale=focus_layer_scale, asking_projector=asking_projector, lookup_projector=lookup_projector, content_projector=content_projector, sigmoid_projector=sigmoid_projector, gate_offset_bias=gate_offset_bias, final_projector=final_projector, pairwise_norm_gain=pairwise_norm_gain, bias_weight=bias_weight, cross_layer_scale=cross_layer_scale, first_cross_projector=first_cross_projector, second_cross_projector=second_cross_projector, outer_weight=outer_weight)


def normed_rows(values, gain):
    values = values.astype(jnp.float32)
    centre = values - lax.optimization_barrier(jnp.mean(values, -1, keepdims=True))
    spread = lax.optimization_barrier(jnp.mean(centre * centre, -1, keepdims=True))
    return centre * lax.rsqrt(spread + 1e-05) * gain.astype(jnp.float32)

def reference(homolog_embedding, pairwise_state, residue_mask, alignment_row_mask, focus_layer_scale, asking_projector, lookup_projector, content_projector, sigmoid_projector, gate_offset_bias, final_projector, pairwise_norm_gain, bias_weight, cross_layer_scale, first_cross_projector, second_cross_projector, outer_weight):
    highest = lax.Precision.HIGHEST
    alignment_normed = normed_rows(homolog_embedding, focus_layer_scale).astype(jnp.bfloat16)
    query_matrix = (jnp.dot(alignment_normed, asking_projector, preferred_element_type=jnp.float32) * SPLIT_DEPTH ** (-0.5)).astype(jnp.bfloat16)
    key_matrix = jnp.dot(alignment_normed, lookup_projector, preferred_element_type=jnp.float32).astype(jnp.bfloat16)
    value_matrix = jnp.dot(alignment_normed, content_projector, preferred_element_type=jnp.float32).astype(jnp.bfloat16)
    gate_values = jax.nn.sigmoid(jnp.dot(alignment_normed, sigmoid_projector, preferred_element_type=jnp.float32) + gate_offset_bias.astype(jnp.float32))
    pair_norm = normed_rows(pairwise_state, pairwise_norm_gain).astype(jnp.bfloat16)
    pair_bias = jnp.einsum('ijc,ch->hij', pair_norm.astype(jnp.float32), bias_weight.astype(jnp.float32), precision=highest).astype(jnp.bfloat16)
    res_float = residue_mask.astype(jnp.float32)
    row_float = alignment_row_mask.astype(jnp.float32)
    key_bias = 1000000000.0 * (res_float - 1.0)
    query_heads = query_matrix.reshape(HOMOLOG_TOTAL, AMINO_TOTAL, FOCUS_SPLITS, SPLIT_DEPTH).transpose(2, 0, 1, 3)
    key_heads = key_matrix.reshape(HOMOLOG_TOTAL, AMINO_TOTAL, FOCUS_SPLITS, SPLIT_DEPTH).transpose(2, 0, 1, 3)
    value_heads = value_matrix.reshape(HOMOLOG_TOTAL, AMINO_TOTAL, FOCUS_SPLITS, SPLIT_DEPTH).transpose(2, 0, 1, 3)

    def one_head(items):
        query_h, key_h, value_h, bias_h = items
        logits = jnp.einsum('sid,sjd->sij', query_h.astype(jnp.float32), key_h.astype(jnp.float32), precision=highest)
        logits = logits + bias_h.astype(jnp.float32)[None] + key_bias[None, None, :]
        weights = jax.nn.softmax(logits, axis=-1)
        return jnp.einsum('sij,sjd->sid', weights, value_h.astype(jnp.float32), precision=highest)
    heads_out = lax.map(one_head, (query_heads, key_heads, value_heads, pair_bias))
    heads_out = heads_out.transpose(1, 2, 0, 3).reshape(HOMOLOG_TOTAL, AMINO_TOTAL, FOCUS_SPLITS * SPLIT_DEPTH)
    attended_values = (heads_out * gate_values).astype(jnp.bfloat16)
    alignment_output = (homolog_embedding.astype(jnp.float32) + jnp.dot(attended_values, final_projector, preferred_element_type=jnp.float32)).astype(jnp.bfloat16)
    product_normed = normed_rows(alignment_output, cross_layer_scale).astype(jnp.bfloat16)
    weight_mask = (row_float[:, None] * res_float[None, :])[:, None, :]
    left = (jnp.einsum('src,ck->skr', product_normed.astype(jnp.float32), first_cross_projector.astype(jnp.float32), precision=highest) * weight_mask).astype(jnp.bfloat16)
    right = (jnp.einsum('src,ck->skr', product_normed.astype(jnp.float32), second_cross_projector.astype(jnp.float32), precision=highest) * weight_mask).astype(jnp.bfloat16)
    w_cube = outer_weight.astype(jnp.float32).reshape(CROSS_FEATURES, CROSS_FEATURES, CZ)
    right_float = right.astype(jnp.float32)

    def row_block(left_block):
        outer = jnp.einsum('ski,slj->ijkl', left_block.astype(jnp.float32), right_float, precision=highest)
        return jnp.einsum('ijkl,klz->ijz', outer, w_cube, precision=highest)
    blocks = left.reshape(HOMOLOG_TOTAL, CROSS_FEATURES, N_RI, RES_BLK).transpose(2, 0, 1, 3)
    update = lax.map(row_block, blocks).reshape(AMINO_TOTAL, AMINO_TOTAL, CZ)
    row_total = jnp.sum(row_float)
    count = jnp.maximum(res_float[:, None] * res_float[None, :] * row_total, 1.0)
    pairwise_output = (pairwise_state.astype(jnp.float32) + update / count[:, :, None]).astype(jnp.bfloat16)
    return (alignment_output, pairwise_output)
```

```python
import jax
import jax.numpy as jnp
from jax import lax
from jax.experimental import pallas as pl
from jax.experimental.pallas import tpu as pltpu
from jax.sharding import PartitionSpec as P

F32 = jnp.float32
BF = jnp.bfloat16
NT = (((1,), (1,)), ((), ()))

XZ, XM, XF = 0, 4, 8
WT, BZ, BY, BX = 12, 15, 18, 21
AL, A2 = 24, 36
LZ, LX = 39, 42
R2, R4 = 54, 58
UP = 70
COUNT = 73


def nt(a, b):
    return lax.dot_general(a, b, NT, preferred_element_type=F32)


def mm(a, b):
    return jnp.dot(a, b, preferred_element_type=F32)


def norm(values, gain):
    centre = values - jnp.mean(values, -1, keepdims=True)
    spread = jnp.mean(centre * centre, -1, keepdims=True)
    return centre * lax.rsqrt(spread + 1e-5) * gain


def eye(n):
    row = lax.broadcasted_iota(jnp.int32, (n, n), 0)
    col = lax.broadcasted_iota(jnp.int32, (n, n), 1)
    return (row == col).astype(F32).astype(BF)


def kernel(
    hom, pair, resm, rows, rowv, fscale, wq, wk, wv, wg, gb, wo, pgain, bw, cscale, p1, p2, ow,
    out_al, out_pair,
    xin, xn, wbuf, pn, bt, bg, biasf, gbt, cm, wst, al, sndf, snd, rcv, scr, lb, rst, rb,
    bscr, ub, ubf, urecv,
    ssem, rsem, xsem, osem,
):
    seq = lax.axis_index("seq")
    ri = lax.axis_index("ri")
    rj = lax.axis_index("rj")
    zl, x = lax.div(seq, 4), lax.rem(seq, 4)
    mate = ri + 1 - 2 * lax.rem(ri, 2)
    opp = lax.rem(ri + 2, 4)
    oppmate = lax.rem(mate + 2, 4)

    def ahead(v, d):
        return lax.rem(v + d, 4)

    def behind(v, d):
        return lax.rem(v + 4 - d, 4)

    ypeer = [{"rj": ahead(rj, d)} for d in (1, 2, 3)]
    xpeer = [{"seq": zl * 4 + ahead(x, d)} for d in (1, 2, 3)]
    zpeer = [{"seq": ahead(zl, d) * 4 + x} for d in (1, 2, 3)]
    rdest = [{"seq": ri * 4 + rj, "ri": t, "rj": x} for t in range(4)]
    rsrc = [{"seq": t * 4 + rj, "ri": zl, "rj": x} for t in range(4)]
    diagonal = jnp.logical_and(zl == ri, x == rj)

    def rcopy(src, dst, k, dev, send=None):
        return pltpu.make_async_remote_copy(
            src_ref=src,
            dst_ref=dst,
            send_sem=ssem.at[k if send is None else send],
            recv_sem=rsem.at[k],
            device_id=dev,
            device_id_type=pl.DeviceIdType.MESH,
        )

    def arrived(ref, k):
        pltpu.make_async_copy(ref, ref, rsem.at[k]).wait()

    def left_here(ref, k):
        pltpu.make_async_copy(ref, ref, ssem.at[k]).wait()

    barrier = pltpu.get_barrier_semaphore()

    def greet(dev):
        pl.semaphore_signal(barrier, inc=1, device_id=dev, device_id_type=pl.DeviceIdType.MESH)

    for dev in ypeer + xpeer + zpeer + [{"ri": mate}, {"ri": opp}]:
        greet(dev)
    for t in range(4):

        @pl.when(jnp.logical_not(jnp.logical_and(diagonal, ri == t)))
        def _():
            greet(rdest[t])

        @pl.when(jnp.logical_not(jnp.logical_and(diagonal, zl == t)))
        def _():
            greet(rsrc[t])

    xcopy = pltpu.make_async_copy(hom.at[pl.ds(rj * 4, 4)], xin, xsem)
    xcopy.start()

    pn[...] = norm(pair[...].astype(F32), pgain[...]).astype(BF).astype(F32)
    bwt = bw[...]
    for j in range(8):
        tile = pn[pl.ds(j, 128, stride=8), :].astype(BF)
        bt[pl.ds(j, 8, stride=8), :] = nt(bwt, tile)
    bg[zl, x, rj] = bt[...].astype(BF)

    for k, w in enumerate((wq, wk, wv, wg)):
        wbuf[rj, pl.ds(k * 64, 64), :] = w[...]
    wbuf[rj, pl.ds(256, 64), :] = wo[...]

    pl.semaphore_wait(barrier, 19 - 2 * diagonal.astype(jnp.int32))

    for d in (1, 2, 3):
        rcopy(bg.at[zl, x, rj], bg.at[zl, x, rj], BZ + d - 1, zpeer[d - 1]).start()

    xcopy.wait()

    def norm_x(s, carry):
        xn[s, ri] = norm(xin[s].astype(F32), fscale[...]).astype(BF)
        rcopy(xn.at[s, ri], xn.at[s, ri], XZ + s, {"ri": opp}).start()
        rcopy(xn.at[s, ri], xn.at[s, ri], XM + s, {"ri": mate}).start()
        return carry

    lax.fori_loop(0, 4, norm_x, 0)
    for d in (1, 2, 3):
        rcopy(wbuf.at[rj], wbuf.at[rj], WT + d - 1, ypeer[d - 1]).start()

    for d in (1, 2, 3):
        arrived(bg.at[behind(zl, d), x, rj], BZ + d - 1)
    for d in (1, 2, 3):
        rcopy(bg.at[:, x, rj], bg.at[:, x, rj], BY + d - 1, ypeer[d - 1]).start()

    row128 = lax.broadcasted_iota(jnp.int32, (128, 128), 0)
    col128 = lax.broadcasted_iota(jnp.int32, (128, 128), 1)
    ones = jnp.ones((128, 128), BF)
    for b in range(4):
        res = resm[pl.ds(b, 1), :].astype(F32)
        spread = jnp.where(row128 == col128, jnp.broadcast_to(res, (128, 128)), 0.0).astype(BF)
        cm[b] = mm(spread, ones)
    for b in range(2):
        gbt[pl.ds(b * 128, 128), :] = jnp.transpose(
            jnp.broadcast_to(gb[:, pl.ds(b * 128, 128)], (128, 128))
        )
    e128 = eye(128)
    for k in range(4):
        wst[pl.ds(k * 128, 128), :] = nt(e128, ow[pl.ds(k * 256, 256), :]).astype(BF)
    pick = (
        lax.broadcasted_iota(jnp.int32, (32, 128), 0)
        == lax.rem(lax.broadcasted_iota(jnp.int32, (32, 128), 1), 32)
    ).astype(F32).astype(BF)
    p1t = p1[...]
    p2r = jnp.concatenate([p2[...]] * 4, 0)
    total = jnp.maximum(jnp.sum(rowv[...].astype(F32)), 1.0)

    for d in (1, 2, 3):
        arrived(bg.at[:, x, behind(rj, d)], BY + d - 1)
    for d in (1, 2, 3):
        rcopy(bg.at[:, x], bg.at[:, x], BX + d - 1, xpeer[d - 1]).start()

    def forward(s):
        arrived(xn.at[s, opp], XZ + s)
        rcopy(xn.at[s, opp], xn.at[s, opp], XF + s, {"ri": mate}).start()

    forward(0)
    for d in (1, 2, 3):
        arrived(wbuf.at[behind(rj, d)], WT + d - 1)
    for d in (1, 2, 3):
        arrived(bg.at[:, behind(x, d)], BX + d - 1)

    keymask = (jnp.concatenate([cm[b] for b in range(4)], 0) - 1.0) * 1e9
    for hp in range(4):
        two = bg[:, :, :, pl.ds(hp * 16, 16), :].astype(F32).reshape(64, 2, 8, 128)
        for h in range(2):
            biasf[hp * 2 + h] = two[:, h].reshape(512, 128) + keymask

    def weight(k):
        return wbuf[:, pl.ds(k * 64, 64), :].reshape(256, 256)

    lane8 = lax.div(lax.broadcasted_iota(jnp.int32, (8, 128), 1), 32)

    def attend(s, carry):
        @pl.when(s < 3)
        def _():
            forward(s + 1)

        arrived(xn.at[s, mate], XM + s)
        arrived(xn.at[s, oppmate], XF + s)
        every = xn[s].reshape(512, 256)
        own = xn[s, ri]
        key = nt(every, weight(1)).astype(BF)
        value = nt(weight(2), every).astype(BF)
        query = (nt(weight(0), own) * 32 ** -0.5).astype(BF)
        gate = jax.nn.sigmoid(nt(weight(3), own) + gbt[...])
        parts = []
        for h in range(8):
            g, r = h // 4, h % 4
            pieces = [jnp.zeros((32, 128), BF)] * 4
            pieces[r] = query[h * 32 : h * 32 + 32]
            logits = mm(key[:, g * 128 : g * 128 + 128], jnp.concatenate(pieces, 0)) + biasf[h]
            top = jnp.max(logits, 0, keepdims=True)
            probs = jnp.exp(logits - top)
            denom = jnp.sum(probs, 0, keepdims=True)
            head = mm(value[h * 32 : h * 32 + 32], probs.astype(BF))
            parts.append(head * (1.0 / denom))
        attended = (jnp.concatenate(parts, 0) * gate).astype(BF)
        attended = nt(e128, attended).astype(BF)
        result = (xin[s].astype(F32) + mm(attended, weight(4))).astype(BF)
        al[s] = result
        pltpu.make_async_copy(al.at[s], out_al.at[rj * 4 + s], osem.at[s]).start()
        for d in (1, 2, 3):
            rcopy(al.at[s], out_al.at[rj * 4 + s], AL + s * 3 + d - 1, ypeer[d - 1]).start()
        on = norm(result.astype(F32), cscale[...])
        keep = cm[ri] * rows[seq * 16 + rj * 4 + s].astype(F32)
        on = (on * jnp.concatenate([keep, keep], 1)).astype(BF)
        left = nt(p1t, on)
        right = nt(on, p2r)
        for y in range(4):
            ltile = jnp.zeros((8, 128), F32)
            rtile = jnp.zeros((8, 128), F32)
            for k in range(4):
                piece = left[k * 8 : k * 8 + 8]
                if k != y:
                    piece = pltpu.roll(piece, (32 * (k - y)) % 128, 1)
                ltile = jnp.where(lane8 == k, piece, ltile)
                rtile = jnp.where(lane8 == k, right[y * 32 + k * 8 : y * 32 + k * 8 + 8], rtile)
            sndf[y, pl.ds(pl.multiple_of(s * 8, 8), 8), :] = ltile
            sndf[y, pl.ds(pl.multiple_of(32 + s * 8, 8), 8), :] = rtile
        return carry

    lax.fori_loop(0, 4, attend, 0)

    snd[...] = sndf[...].astype(BF)
    for d in (1, 2, 3):
        rcopy(snd.at[ahead(rj, d)], rcv.at[rj], A2 + d - 1, ypeer[d - 1]).start()
    rcv[rj] = snd[rj]
    for d in (1, 2, 3):
        arrived(rcv.at[behind(rj, d)], A2 + d - 1)
    for y in range(4):
        block = rcv[y].astype(F32)
        for side in range(2):
            for s in range(4):
                r = side * 32 + s * 8
                scr[side, pl.ds(y * 4 + s, 8, stride=16), :] = block[r : r + 8]
    lb[:, pl.ds(seq, 1)] = scr[0].astype(BF).reshape(8, 1, 16, 128)
    rblock = scr[1].astype(BF).reshape(8, 16, 128)
    rst[...] = rblock

    @pl.when(diagonal)
    def _():
        rb[:, pl.ds(seq, 1)] = rblock.reshape(8, 1, 16, 128)

    for d in (1, 2, 3):
        rcopy(lb.at[:, seq], lb.at[:, seq], LZ + d - 1, zpeer[d - 1]).start()

    def rfirst(t):
        return rcopy(rst, rb.at[:, seq], R2 + zl, rdest[t], R2 + t)

    for t in range(4):

        @pl.when(jnp.logical_not(jnp.logical_and(diagonal, ri == t)))
        def _():
            rfirst(t).start()

    for b in range(4):
        src = behind(zl, b) * 4 + x
        if b > 0:
            arrived(lb.at[:, src], LZ + b - 1)
        for d in (1, 2, 3):
            rcopy(lb.at[:, src], lb.at[:, src], LX + b * 3 + d - 1, xpeer[d - 1]).start()
        came = b * 4 + rj

        @pl.when(jnp.logical_not(jnp.logical_and(diagonal, zl == b)))
        def _():
            arrived(rb.at[:, came], R2 + b)

        for d in (1, 2, 3):
            rcopy(rb.at[:, came], rb.at[:, came], R4 + b * 3 + d - 1, ypeer[d - 1]).start()

    for b in range(4):
        for d in (1, 2, 3):
            arrived(lb.at[:, behind(zl, b) * 4 + behind(x, d)], LX + b * 3 + d - 1)
            arrived(rb.at[:, b * 4 + behind(rj, d)], R4 + b * 3 + d - 1)

    lane128 = lax.div(lax.broadcasted_iota(jnp.int32, (128, 128), 1), 32)

    def product(q, carry):
        right = nt(e128, rb[q].reshape(256, 128)).astype(BF)
        for k in range(8):
            outer = mm(right, lb[k].reshape(256, 128)).astype(BF)
            for j in range(4):
                bscr[j // 2, pl.ds(k * 32, 32), pl.ds((j % 2) * 128, 128)] = outer[
                    j * 32 : j * 32 + 32
                ]
        for jp in range(2):
            wide = mm(wst[...], bscr[jp])
            for half in range(2):
                c = half * 128
                mixed = wide[0:128, c : c + 128]
                for k in range(1, 4):
                    mixed = jnp.where(
                        lane128 == k, wide[k * 128 : k * 128 + 128, c : c + 128], mixed
                    )
                ub[jp * 2 + half, pl.ds(q, 32, stride=8), :] = nt(pick, mixed.astype(BF))
        return carry

    lax.fori_loop(0, 8, product, 0)
    ubf[...] = ub[...].astype(BF)
    for d in (1, 2, 3):
        rcopy(ubf.at[ahead(rj, d)], urecv.at[rj], UP + d - 1, ypeer[d - 1]).start()
    urecv[rj] = ubf[rj]
    scale = 1.0 / total
    for d in (1, 2, 3):
        arrived(urecv.at[behind(rj, d)], UP + d - 1)
    out_pair[...] = (
        pair[...].astype(F32) + urecv[...].reshape(1024, 128).astype(F32) * scale
    ).astype(BF)

    for s in range(4):
        pltpu.make_async_copy(al.at[s], out_al.at[rj * 4 + s], osem.at[s]).wait()
        left_here(xn.at[s, ri], XZ + s)
        left_here(xn.at[s, ri], XM + s)
        left_here(xn.at[s, opp], XF + s)
        for d in (1, 2, 3):
            left_here(al.at[s], AL + s * 3 + d - 1)
            arrived(out_al.at[behind(rj, d) * 4 + s], AL + s * 3 + d - 1)
    for d in (1, 2, 3):
        left_here(wbuf.at[rj], WT + d - 1)
        left_here(bg.at[zl, x, rj], BZ + d - 1)
        left_here(bg.at[:, x, rj], BY + d - 1)
        left_here(bg.at[:, x], BX + d - 1)
        left_here(snd.at[ahead(rj, d)], A2 + d - 1)
        left_here(lb.at[:, seq], LZ + d - 1)
        left_here(ubf.at[ahead(rj, d)], UP + d - 1)
        for b in range(4):
            left_here(lb.at[:, behind(zl, b) * 4 + x], LX + b * 3 + d - 1)
            left_here(rb.at[:, b * 4 + rj], R4 + b * 3 + d - 1)
    for t in range(4):

        @pl.when(jnp.logical_not(jnp.logical_and(diagonal, ri == t)))
        def _():
            left_here(rst, R2 + t)


def on_device(
    homolog_embedding,
    pairwise_state,
    residue_mask,
    alignment_row_mask,
    focus_layer_scale,
    asking_projector,
    lookup_projector,
    content_projector,
    sigmoid_projector,
    gate_offset_bias,
    final_projector,
    pairwise_norm_gain,
    bias_weight,
    cross_layer_scale,
    first_cross_projector,
    second_cross_projector,
    outer_weight,
):
    vmem = pl.BlockSpec(memory_space=pltpu.VMEM)
    smem = pl.BlockSpec(memory_space=pltpu.SMEM)
    hbm = pl.BlockSpec(memory_space=pl.ANY)
    alignment_output, pair_rows = pl.pallas_call(
        kernel,
        out_shape=(
            jax.ShapeDtypeStruct((16, 128, 256), BF),
            jax.ShapeDtypeStruct((1024, 128), BF),
        ),
        in_specs=[hbm, vmem, vmem, smem] + [vmem] * 14,
        out_specs=(hbm, vmem),
        scratch_shapes=[
            pltpu.VMEM((4, 128, 256), BF),
            pltpu.VMEM((4, 4, 128, 256), BF),
            pltpu.VMEM((4, 320, 256), BF),
            pltpu.VMEM((1024, 128), F32),
            pltpu.VMEM((64, 128), F32),
            pltpu.VMEM((4, 4, 4, 64, 128), BF),
            pltpu.VMEM((8, 512, 128), F32),
            pltpu.VMEM((256, 128), F32),
            pltpu.VMEM((4, 128, 128), F32),
            pltpu.VMEM((512, 256), BF),
            pltpu.VMEM((4, 128, 256), BF),
            pltpu.VMEM((4, 64, 128), F32),
            pltpu.VMEM((4, 64, 128), BF),
            pltpu.VMEM((4, 64, 128), BF),
            pltpu.VMEM((2, 128, 128), F32),
            pltpu.VMEM((8, 16, 16, 128), BF),
            pltpu.VMEM((8, 16, 128), BF),
            pltpu.VMEM((8, 16, 16, 128), BF),
            pltpu.VMEM((2, 256, 256), BF),
            pltpu.VMEM((4, 256, 128), F32),
            pltpu.VMEM((4, 256, 128), BF),
            pltpu.VMEM((4, 256, 128), BF),
            pltpu.SemaphoreType.DMA((COUNT,)),
            pltpu.SemaphoreType.DMA((COUNT,)),
            pltpu.SemaphoreType.DMA,
            pltpu.SemaphoreType.DMA((4,)),
        ],
        compiler_params=pltpu.CompilerParams(
            collective_id=0, has_side_effects=True, vmem_limit_bytes=40 * 1024 * 1024
        ),
        cost_estimate=pl.CostEstimate(
            flops=4_000_000_000, bytes_accessed=4_000_000, transcendentals=2_000_000
        ),
    )(
        homolog_embedding,
        pairwise_state.reshape(1024, 128),
        residue_mask.reshape(4, 128),
        alignment_row_mask,
        alignment_row_mask.reshape(2, 128),
        focus_layer_scale.reshape(1, 256),
        asking_projector.T,
        lookup_projector.T,
        content_projector.T,
        sigmoid_projector.T,
        gate_offset_bias.reshape(1, 256),
        final_projector,
        pairwise_norm_gain.reshape(1, 128),
        bias_weight.T,
        cross_layer_scale.reshape(1, 256),
        first_cross_projector.T,
        second_cross_projector.T,
        outer_weight,
    )
    return alignment_output, pair_rows.reshape(128, 8, 128)


def solution(mesh):
    placed = (
        P("seq", "ri", None),
        P("ri", ("seq", "rj"), None),
        P(),
        P(),
        P(),
        P(None, "rj"),
        P(None, "rj"),
        P(None, "rj"),
        P(None, "rj"),
        P(),
        P("rj", None),
        P(),
        P(),
        P(),
        P(),
        P(),
        P(),
    )
    return jax.shard_map(
        on_device,
        mesh=mesh,
        in_specs=placed,
        out_specs=(P("seq", "ri", None), P("ri", ("seq", "rj"), None)),
        check_vma=False,
    )
```

```python
import jax
import jax.numpy as jnp
from jax import lax
from jax.experimental import pallas as pl
from jax.experimental.pallas import tpu as pltpu
from jax.sharding import PartitionSpec as P

F32 = jnp.float32
BF = jnp.bfloat16
NT = (((1,), (1,)), ((), ()))

XZ, XM, XF = 0, 4, 8
WT, BZ, BY, BX = 12, 16, 19, 23
AL, A2 = 27, 43
LZ, LX = 46, 49
R2, R4 = 65, 69
UP = 85
COUNT = 88


def nt(a, b):
    return lax.dot_general(a, b, NT, preferred_element_type=F32)


def mm(a, b):
    return jnp.dot(a, b, preferred_element_type=F32)


def norm(values, gain):
    centre = values - jnp.mean(values, -1, keepdims=True)
    spread = jnp.mean(centre * centre, -1, keepdims=True)
    return centre * lax.rsqrt(spread + 1e-5) * gain


def eye(n):
    row = lax.broadcasted_iota(jnp.int32, (n, n), 0)
    col = lax.broadcasted_iota(jnp.int32, (n, n), 1)
    return (row == col).astype(F32).astype(BF)


def kernel(
    hom, pair_in, resm_in, rows_in, rowv_in, fscale_in, wq, wk, wv, wg, gb_in, wo, pgain_in, bw_in,
    cscale_in, p1_in, p2_in, ow_in,
    out_al, out_pair,
    xin, pair, resm, rows, rowv, fscale, gb, pgain, bw, cscale, p1, p2, ow,
    xn, wbuf, pn, bt, bg, biasf, gbt, cm, wst, al, sndf, snd, rcv, scr, lb, rst, rb,
    bscr, ub, ubf, urecv,
    ssem, rsem, lsem, osem,
):
    seq = lax.axis_index("seq")
    ri = lax.axis_index("ri")
    rj = lax.axis_index("rj")
    zl, x = lax.div(seq, 4), lax.rem(seq, 4)
    mate = ri + 1 - 2 * lax.rem(ri, 2)
    opp = lax.rem(ri + 2, 4)
    oppmate = lax.rem(mate + 2, 4)

    def ahead(v, d):
        return lax.rem(v + d, 4)

    def behind(v, d):
        return lax.rem(v + 4 - d, 4)

    plus_y, minus_y = {"rj": ahead(rj, 1)}, {"rj": behind(rj, 1)}
    plus_x, minus_x = {"seq": zl * 4 + ahead(x, 1)}, {"seq": zl * 4 + behind(x, 1)}
    ypeer = [{"rj": ahead(rj, d)} for d in (1, 2, 3)]
    xpeer = [{"seq": zl * 4 + ahead(x, d)} for d in (1, 2, 3)]
    zpeer = [{"seq": ahead(zl, d) * 4 + x} for d in (1, 2, 3)]
    rdest = [{"seq": ri * 4 + rj, "ri": t, "rj": x} for t in range(4)]
    rsrc = [{"seq": t * 4 + rj, "ri": zl, "rj": x} for t in range(4)]
    diagonal = jnp.logical_and(zl == ri, x == rj)

    def rcopy(src, dst, k, dev, send=None):
        return pltpu.make_async_remote_copy(
            src_ref=src,
            dst_ref=dst,
            send_sem=ssem.at[k if send is None else send],
            recv_sem=rsem.at[k],
            device_id=dev,
            device_id_type=pl.DeviceIdType.MESH,
        )

    def arrived(ref, k):
        pltpu.make_async_copy(ref, ref, rsem.at[k]).wait()

    def left_here(ref, k):
        pltpu.make_async_copy(ref, ref, ssem.at[k]).wait()

    def ring_start(own, k, plus, minus):
        rcopy(own, own, k, plus).start()
        rcopy(own, own, k + 1, minus).start()

    def ring_pass(before, after, lower, upper, k, plus, minus):
        arrived(before, k)
        rcopy(lower(before), lower(before), k + 2, plus).start()
        arrived(after, k + 1)
        rcopy(upper(after), upper(after), k + 3, minus).start()

    def ring_end(far, lower, upper, k):
        arrived(lower(far), k + 2)
        arrived(upper(far), k + 3)

    def ring_sent(own, lower, upper, k):
        left_here(own, k)
        left_here(own, k + 1)
        left_here(lower(own), k + 2)
        left_here(upper(own), k + 3)

    def first(n):
        return lambda ref: ref.at[pl.ds(0, n)]

    def second(n):
        return lambda ref: ref.at[pl.ds(n, n)]

    inward = [
        (hom.at[pl.ds(rj * 4, 4)], xin),
        (fscale_in, fscale),
        (pair_in, pair),
        (pgain_in, pgain),
        (bw_in, bw),
        (wq, wbuf.at[rj, pl.ds(0, 64)]),
        (wk, wbuf.at[rj, pl.ds(64, 64)]),
        (wv, wbuf.at[rj, pl.ds(128, 64)]),
        (wg, wbuf.at[rj, pl.ds(192, 64)]),
        (wo, wbuf.at[rj, pl.ds(256, 64)]),
        (resm_in, resm),
        (rows_in, rows),
        (rowv_in, rowv),
        (gb_in, gb),
        (cscale_in, cscale),
        (p1_in, p1),
        (p2_in, p2),
        (ow_in, ow),
    ]

    def local(k):
        return pltpu.make_async_copy(inward[k][0], inward[k][1], lsem.at[k])

    for k in range(len(inward)):
        local(k).start()

    barrier = pltpu.get_barrier_semaphore()

    def greet(dev):
        pl.semaphore_signal(barrier, inc=1, device_id=dev, device_id_type=pl.DeviceIdType.MESH)

    for dev in ypeer + xpeer + zpeer + [{"ri": mate}, {"ri": opp}]:
        greet(dev)
    for t in range(4):

        @pl.when(jnp.logical_not(jnp.logical_and(diagonal, ri == t)))
        def _():
            greet(rdest[t])

        @pl.when(jnp.logical_not(jnp.logical_and(diagonal, zl == t)))
        def _():
            greet(rsrc[t])

    local(0).wait()
    local(1).wait()

    def norm_x(s, carry):
        xn[s, ri] = norm(xin[s].astype(F32), fscale[...]).astype(BF)
        return carry

    lax.fori_loop(0, 4, norm_x, 0)

    pl.semaphore_wait(barrier, 19 - 2 * diagonal.astype(jnp.int32))

    def send_x(s):
        rcopy(xn.at[s, ri], xn.at[s, ri], XZ + s, {"ri": opp}).start()
        rcopy(xn.at[s, ri], xn.at[s, ri], XM + s, {"ri": mate}).start()

    send_x(0)
    for k in range(5, 10):
        local(k).wait()
    w_lower, w_upper = first(160), second(160)
    ring_start(wbuf.at[rj], WT, plus_y, minus_y)

    for k in range(2, 5):
        local(k).wait()
    pn[...] = norm(pair[...].astype(F32), pgain[...]).astype(BF).astype(F32)
    for j in range(8):
        tile = pn[pl.ds(j, 128, stride=8), :].astype(BF)
        bt[pl.ds(j, 8, stride=8), :] = nt(bw[...], tile)
    bg[zl, x, rj] = bt[...].astype(BF)
    for d in (1, 2, 3):
        rcopy(bg.at[zl, x, rj], bg.at[zl, x, rj], BZ + d - 1, zpeer[d - 1]).start()
    for s in range(1, 4):
        send_x(s)

    for k in range(10, len(inward)):
        local(k).wait()
    ring_pass(
        wbuf.at[behind(rj, 1)], wbuf.at[ahead(rj, 1)], w_lower, w_upper, WT, plus_y, minus_y
    )
    for d in (1, 2, 3):
        arrived(bg.at[behind(zl, d), x, rj], BZ + d - 1)
    b_lower, b_upper = first(2), second(2)
    ring_start(bg.at[:, x, rj], BY, plus_y, minus_y)

    row128 = lax.broadcasted_iota(jnp.int32, (128, 128), 0)
    col128 = lax.broadcasted_iota(jnp.int32, (128, 128), 1)
    ones = jnp.ones((128, 128), BF)
    for b in range(4):
        res = resm[pl.ds(b, 1), :].astype(F32)
        spread = jnp.where(row128 == col128, jnp.broadcast_to(res, (128, 128)), 0.0).astype(BF)
        cm[b] = mm(spread, ones)
    for b in range(2):
        gbt[pl.ds(b * 128, 128), :] = jnp.transpose(
            jnp.broadcast_to(gb[:, pl.ds(b * 128, 128)], (128, 128))
        )
    e128 = eye(128)
    for k in range(4):
        wst[pl.ds(k * 128, 128), :] = nt(e128, ow[pl.ds(k * 256, 256), :]).astype(BF)
    pick = (
        lax.broadcasted_iota(jnp.int32, (32, 128), 0)
        == lax.rem(lax.broadcasted_iota(jnp.int32, (32, 128), 1), 32)
    ).astype(F32).astype(BF)
    p1t = p1[...]
    p2r = jnp.concatenate([p2[...]] * 4, 0)
    total = jnp.maximum(jnp.sum(rowv[...].astype(F32)), 1.0)

    ring_pass(
        bg.at[:, x, behind(rj, 1)], bg.at[:, x, ahead(rj, 1)], b_lower, b_upper, BY, plus_y, minus_y
    )
    ring_end(bg.at[:, x, ahead(rj, 2)], b_lower, b_upper, BY)
    ring_start(bg.at[:, x], BX, plus_x, minus_x)

    def forward(s):
        arrived(xn.at[s, opp], XZ + s)
        rcopy(xn.at[s, opp], xn.at[s, opp], XF + s, {"ri": mate}).start()

    ring_pass(bg.at[:, behind(x, 1)], bg.at[:, ahead(x, 1)], b_lower, b_upper, BX, plus_x, minus_x)
    forward(0)
    ring_end(wbuf.at[ahead(rj, 2)], w_lower, w_upper, WT)
    ring_end(bg.at[:, ahead(x, 2)], b_lower, b_upper, BX)

    keymask = (jnp.concatenate([cm[b] for b in range(4)], 0) - 1.0) * 1e9
    for hp in range(4):
        two = bg[:, :, :, pl.ds(hp * 16, 16), :].astype(F32).reshape(64, 2, 8, 128)
        for h in range(2):
            biasf[hp * 2 + h] = two[:, h].reshape(512, 128) + keymask

    def weight(k):
        return wbuf[:, pl.ds(k * 64, 64), :].reshape(256, 256)

    lane8 = lax.div(lax.broadcasted_iota(jnp.int32, (8, 128), 1), 32)

    def attend(s, carry):
        @pl.when(s < 3)
        def _():
            forward(s + 1)

        arrived(xn.at[s, mate], XM + s)
        arrived(xn.at[s, oppmate], XF + s)
        every = xn[s].reshape(512, 256)
        own = xn[s, ri]
        key = nt(every, weight(1)).astype(BF)
        value = nt(weight(2), every).astype(BF)
        query = (nt(weight(0), own) * 32 ** -0.5).astype(BF)
        gate = jax.nn.sigmoid(nt(weight(3), own) + gbt[...])
        parts = []
        for h in range(8):
            g, r = h // 4, h % 4
            pieces = [jnp.zeros((32, 128), BF)] * 4
            pieces[r] = query[h * 32 : h * 32 + 32]
            logits = mm(key[:, g * 128 : g * 128 + 128], jnp.concatenate(pieces, 0)) + biasf[h]
            top = jnp.max(logits, 0, keepdims=True)
            probs = jnp.exp(logits - top)
            denom = jnp.sum(probs, 0, keepdims=True)
            head = mm(value[h * 32 : h * 32 + 32], probs.astype(BF))
            parts.append(head * (1.0 / denom))
        attended = (jnp.concatenate(parts, 0) * gate).astype(BF)
        attended = nt(e128, attended).astype(BF)
        result = (xin[s].astype(F32) + mm(attended, weight(4))).astype(BF)
        al[s] = result
        pltpu.make_async_copy(al.at[s], out_al.at[rj * 4 + s], osem.at[s]).start()
        rcopy(al.at[s], out_al.at[rj * 4 + s], AL + s * 4, plus_y).start()
        rcopy(al.at[s], out_al.at[rj * 4 + s], AL + s * 4 + 1, minus_y).start()
        on = norm(result.astype(F32), cscale[...])
        keep = cm[ri] * rows[seq * 16 + rj * 4 + s].astype(F32)
        on = (on * jnp.concatenate([keep, keep], 1)).astype(BF)
        left = nt(p1t, on)
        right = nt(on, p2r)
        for y in range(4):
            ltile = jnp.zeros((8, 128), F32)
            rtile = jnp.zeros((8, 128), F32)
            for k in range(4):
                piece = left[k * 8 : k * 8 + 8]
                if k != y:
                    piece = pltpu.roll(piece, (32 * (k - y)) % 128, 1)
                ltile = jnp.where(lane8 == k, piece, ltile)
                rtile = jnp.where(lane8 == k, right[y * 32 + k * 8 : y * 32 + k * 8 + 8], rtile)
            sndf[y, pl.ds(pl.multiple_of(s * 8, 8), 8), :] = ltile
            sndf[y, pl.ds(pl.multiple_of(32 + s * 8, 8), 8), :] = rtile

        @pl.when(s > 0)
        def _():
            pass_out(s - 1)

        return carry

    a_lower, a_upper = first(64), second(64)

    def pass_out(s):
        ring_pass(
            out_al.at[behind(rj, 1) * 4 + s],
            out_al.at[ahead(rj, 1) * 4 + s],
            a_lower,
            a_upper,
            AL + s * 4,
            plus_y,
            minus_y,
        )

    lax.fori_loop(0, 4, attend, 0)

    snd[...] = sndf[...].astype(BF)
    for d in (1, 2, 3):
        rcopy(snd.at[ahead(rj, d)], rcv.at[rj], A2 + d - 1, ypeer[d - 1]).start()
    rcv[rj] = snd[rj]
    for d in (1, 2, 3):
        arrived(rcv.at[behind(rj, d)], A2 + d - 1)
    for y in range(4):
        block = rcv[y].astype(F32)
        for side in range(2):
            for s in range(4):
                r = side * 32 + s * 8
                scr[side, pl.ds(y * 4 + s, 8, stride=16), :] = block[r : r + 8]
    lb[:, pl.ds(seq, 1)] = scr[0].astype(BF).reshape(8, 1, 16, 128)
    rblock = scr[1].astype(BF).reshape(8, 16, 128)
    rst[...] = rblock

    @pl.when(diagonal)
    def _():
        rb[:, pl.ds(seq, 1)] = rblock.reshape(8, 1, 16, 128)

    for d in (1, 2, 3):
        rcopy(lb.at[:, seq], lb.at[:, seq], LZ + d - 1, zpeer[d - 1]).start()

    def rfirst(t):
        return rcopy(rst, rb.at[:, seq], R2 + zl, rdest[t], R2 + t)

    for t in range(4):

        @pl.when(jnp.logical_not(jnp.logical_and(diagonal, ri == t)))
        def _():
            rfirst(t).start()

    q_lower, q_upper = first(4), second(4)
    for b in range(4):
        src = behind(zl, b) * 4 + x
        if b > 0:
            arrived(lb.at[:, src], LZ + b - 1)
        ring_start(lb.at[:, src], LX + b * 4, plus_x, minus_x)
        came = b * 4 + rj

        @pl.when(jnp.logical_not(jnp.logical_and(diagonal, zl == b)))
        def _():
            arrived(rb.at[:, came], R2 + b)

        ring_start(rb.at[:, came], R4 + b * 4, plus_y, minus_y)
    for b in range(4):
        z4 = behind(zl, b) * 4
        ring_pass(
            lb.at[:, z4 + behind(x, 1)], lb.at[:, z4 + ahead(x, 1)], q_lower, q_upper,
            LX + b * 4, plus_x, minus_x,
        )
        ring_pass(
            rb.at[:, b * 4 + behind(rj, 1)], rb.at[:, b * 4 + ahead(rj, 1)], q_lower, q_upper,
            R4 + b * 4, plus_y, minus_y,
        )
    for b in range(4):
        ring_end(lb.at[:, behind(zl, b) * 4 + ahead(x, 2)], q_lower, q_upper, LX + b * 4)
        ring_end(rb.at[:, b * 4 + ahead(rj, 2)], q_lower, q_upper, R4 + b * 4)
    pass_out(3)

    lane128 = lax.div(lax.broadcasted_iota(jnp.int32, (128, 128), 1), 32)

    def product(q, carry):
        right = nt(e128, rb[q].reshape(256, 128)).astype(BF)
        for k in range(8):
            outer = mm(right, lb[k].reshape(256, 128)).astype(BF)
            for j in range(4):
                bscr[j // 2, pl.ds(k * 32, 32), pl.ds((j % 2) * 128, 128)] = outer[
                    j * 32 : j * 32 + 32
                ]
        for jp in range(2):
            wide = mm(wst[...], bscr[jp])
            for half in range(2):
                c = half * 128
                mixed = wide[0:128, c : c + 128]
                for k in range(1, 4):
                    mixed = jnp.where(
                        lane128 == k, wide[k * 128 : k * 128 + 128, c : c + 128], mixed
                    )
                ub[jp * 2 + half, pl.ds(q, 32, stride=8), :] = nt(pick, mixed.astype(BF))
        return carry

    lax.fori_loop(0, 8, product, 0)
    ubf[...] = ub[...].astype(BF)
    for d in (1, 2, 3):
        rcopy(ubf.at[ahead(rj, d)], urecv.at[rj], UP + d - 1, ypeer[d - 1]).start()
    urecv[rj] = ubf[rj]
    scale = 1.0 / total
    for d in (1, 2, 3):
        arrived(urecv.at[behind(rj, d)], UP + d - 1)
    out_pair[...] = (
        pair[...].astype(F32) + urecv[...].reshape(1024, 128).astype(F32) * scale
    ).astype(BF)

    for s in range(4):
        pltpu.make_async_copy(al.at[s], out_al.at[rj * 4 + s], osem.at[s]).wait()
        left_here(xn.at[s, ri], XZ + s)
        left_here(xn.at[s, ri], XM + s)
        left_here(xn.at[s, opp], XF + s)
        ring_end(out_al.at[ahead(rj, 2) * 4 + s], a_lower, a_upper, AL + s * 4)
        ring_sent(al.at[s], a_lower, a_upper, AL + s * 4)
    ring_sent(wbuf.at[rj], w_lower, w_upper, WT)
    ring_sent(bg.at[:, x, rj], b_lower, b_upper, BY)
    ring_sent(bg.at[:, x], b_lower, b_upper, BX)
    for d in (1, 2, 3):
        left_here(bg.at[zl, x, rj], BZ + d - 1)
        left_here(snd.at[ahead(rj, d)], A2 + d - 1)
        left_here(lb.at[:, seq], LZ + d - 1)
        left_here(ubf.at[ahead(rj, d)], UP + d - 1)
    for b in range(4):
        ring_sent(lb.at[:, behind(zl, b) * 4 + x], q_lower, q_upper, LX + b * 4)
        ring_sent(rb.at[:, b * 4 + rj], q_lower, q_upper, R4 + b * 4)
    for t in range(4):

        @pl.when(jnp.logical_not(jnp.logical_and(diagonal, ri == t)))
        def _():
            left_here(rst, R2 + t)


def on_device(
    homolog_embedding,
    pairwise_state,
    residue_mask,
    alignment_row_mask,
    focus_layer_scale,
    asking_projector,
    lookup_projector,
    content_projector,
    sigmoid_projector,
    gate_offset_bias,
    final_projector,
    pairwise_norm_gain,
    bias_weight,
    cross_layer_scale,
    first_cross_projector,
    second_cross_projector,
    outer_weight,
):
    vmem = pl.BlockSpec(memory_space=pltpu.VMEM)
    hbm = pl.BlockSpec(memory_space=pl.ANY)
    alignment_output, pair_rows = pl.pallas_call(
        kernel,
        out_shape=(
            jax.ShapeDtypeStruct((16, 128, 256), BF),
            jax.ShapeDtypeStruct((1024, 128), BF),
        ),
        in_specs=[hbm] * 18,
        out_specs=(hbm, vmem),
        scratch_shapes=[
            pltpu.VMEM((4, 128, 256), BF),
            pltpu.VMEM((1024, 128), BF),
            pltpu.VMEM((4, 128), jnp.int32),
            pltpu.SMEM((256,), jnp.int32),
            pltpu.VMEM((2, 128), jnp.int32),
            pltpu.VMEM((1, 256), F32),
            pltpu.VMEM((1, 256), F32),
            pltpu.VMEM((1, 128), F32),
            pltpu.VMEM((8, 128), BF),
            pltpu.VMEM((1, 256), F32),
            pltpu.VMEM((32, 256), BF),
            pltpu.VMEM((32, 256), BF),
            pltpu.VMEM((1024, 128), BF),
            pltpu.VMEM((4, 4, 128, 256), BF),
            pltpu.VMEM((4, 320, 256), BF),
            pltpu.VMEM((1024, 128), F32),
            pltpu.VMEM((64, 128), F32),
            pltpu.VMEM((4, 4, 4, 64, 128), BF),
            pltpu.VMEM((8, 512, 128), F32),
            pltpu.VMEM((256, 128), F32),
            pltpu.VMEM((4, 128, 128), F32),
            pltpu.VMEM((512, 256), BF),
            pltpu.VMEM((4, 128, 256), BF),
            pltpu.VMEM((4, 64, 128), F32),
            pltpu.VMEM((4, 64, 128), BF),
            pltpu.VMEM((4, 64, 128), BF),
            pltpu.VMEM((2, 128, 128), F32),
            pltpu.VMEM((8, 16, 16, 128), BF),
            pltpu.VMEM((8, 16, 128), BF),
            pltpu.VMEM((8, 16, 16, 128), BF),
            pltpu.VMEM((2, 256, 256), BF),
            pltpu.VMEM((4, 256, 128), F32),
            pltpu.VMEM((4, 256, 128), BF),
            pltpu.VMEM((4, 256, 128), BF),
            pltpu.SemaphoreType.DMA((COUNT,)),
            pltpu.SemaphoreType.DMA((COUNT,)),
            pltpu.SemaphoreType.DMA((18,)),
            pltpu.SemaphoreType.DMA((4,)),
        ],
        compiler_params=pltpu.CompilerParams(
            collective_id=0, has_side_effects=True, vmem_limit_bytes=60 * 1024 * 1024
        ),
        cost_estimate=pl.CostEstimate(
            flops=4_000_000_000, bytes_accessed=4_000_000, transcendentals=2_000_000
        ),
    )(
        homolog_embedding,
        pairwise_state.reshape(1024, 128),
        residue_mask.reshape(4, 128),
        alignment_row_mask,
        alignment_row_mask.reshape(2, 128),
        focus_layer_scale.reshape(1, 256),
        asking_projector.T,
        lookup_projector.T,
        content_projector.T,
        sigmoid_projector.T,
        gate_offset_bias.reshape(1, 256),
        final_projector,
        pairwise_norm_gain.reshape(1, 128),
        bias_weight.T,
        cross_layer_scale.reshape(1, 256),
        first_cross_projector.T,
        second_cross_projector.T,
        outer_weight,
    )
    return alignment_output, pair_rows.reshape(128, 8, 128)


def solution(mesh):
    placed = (
        P("seq", "ri", None),
        P("ri", ("seq", "rj"), None),
        P(),
        P(),
        P(),
        P(None, "rj"),
        P(None, "rj"),
        P(None, "rj"),
        P(None, "rj"),
        P(),
        P("rj", None),
        P(),
        P(),
        P(),
        P(),
        P(),
        P(),
    )
    return jax.shard_map(
        on_device,
        mesh=mesh,
        in_specs=placed,
        out_specs=(P("seq", "ri", None), P("ri", ("seq", "rj"), None)),
        check_vma=False,
    )
```

```python
import jax
import jax.numpy as jnp
from jax import lax
from jax.experimental import pallas as pl
from jax.experimental.pallas import tpu as pltpu
from jax.sharding import PartitionSpec as P

F32 = jnp.float32
BF = jnp.bfloat16
NT = (((1,), (1,)), ((), ()))

RZ, XZ, XM, XF = 0, 8, 16, 20
WT, BZ = 24, 28
AY, AX, BX, BY = 31, 35, 39, 43
AL, A2 = 47, 63
LZ, LX = 66, 69
R2, R4 = 85, 89
UP = 105
COUNT = 108


def nt(a, b):
    return lax.dot_general(a, b, NT, preferred_element_type=F32)


def mm(a, b):
    return jnp.dot(a, b, preferred_element_type=F32)


def norm(values, gain):
    centre = values - jnp.mean(values, -1, keepdims=True)
    spread = jnp.mean(centre * centre, -1, keepdims=True)
    return centre * lax.rsqrt(spread + 1e-5) * gain


def eye(n):
    row = lax.broadcasted_iota(jnp.int32, (n, n), 0)
    col = lax.broadcasted_iota(jnp.int32, (n, n), 1)
    return (row == col).astype(F32).astype(BF)


def kernel(
    hom, pair_in, resm_in, rows_in, rowv_in, fscale_in, wq, wk, wv, wg, gb_in, wo, pgain_in, bw_in,
    cscale_in, p1_in, p2_in, ow_in,
    out_al, out_pair,
    xin, pair, resm, rows, rowv, fscale, gb, pgain, bw, cscale, p1, p2, ow,
    xn, relay, wbuf, pn, bt, bg, biasf, gbt, cm, wst, al, right, sndf, snd, rcv, scr, lb, rst, rb,
    bscr, ub, ubf, urecv,
    ssem, rsem, lsem, osem,
):
    seq = lax.axis_index("seq")
    ri = lax.axis_index("ri")
    rj = lax.axis_index("rj")
    zl, x = lax.div(seq, 4), lax.rem(seq, 4)
    mate = ri + 1 - 2 * lax.rem(ri, 2)
    opp = lax.rem(ri + 2, 4)
    oppmate = lax.rem(mate + 2, 4)

    def ahead(v, d):
        return lax.rem(v + d, 4)

    def behind(v, d):
        return lax.rem(v + 4 - d, 4)

    plus_y, minus_y = {"rj": ahead(rj, 1)}, {"rj": behind(rj, 1)}
    plus_x, minus_x = {"seq": zl * 4 + ahead(x, 1)}, {"seq": zl * 4 + behind(x, 1)}
    core, z = lax.rem(ri, 2), lax.div(ri, 2) * 4 + zl

    def along_z(step):
        to = lax.rem(z + step, 8)
        return lax.div(to, 4) * 2 + core, {
            "seq": lax.rem(to, 4) * 4 + x,
            "ri": lax.div(to, 4) * 2 + core,
        }

    ri_up, up = along_z(2)
    ri_down, down = along_z(6)
    ypeer = [{"rj": ahead(rj, d)} for d in (1, 2, 3)]
    zpeer = [{"seq": ahead(zl, d) * 4 + x} for d in (1, 2, 3)]
    rdest = [{"seq": ri * 4 + rj, "ri": t, "rj": x} for t in range(4)]
    rsrc = [{"seq": t * 4 + rj, "ri": zl, "rj": x} for t in range(4)]
    diagonal = jnp.logical_and(zl == ri, x == rj)

    def rcopy(src, dst, k, dev, send=None):
        return pltpu.make_async_remote_copy(
            src_ref=src,
            dst_ref=dst,
            send_sem=ssem.at[k if send is None else send],
            recv_sem=rsem.at[k],
            device_id=dev,
            device_id_type=pl.DeviceIdType.MESH,
        )

    def arrived(ref, k):
        pltpu.make_async_copy(ref, ref, rsem.at[k]).wait()

    def left_here(ref, k):
        pltpu.make_async_copy(ref, ref, ssem.at[k]).wait()

    def ring_start(own, k, plus, minus):
        rcopy(own, own, k, plus).start()
        rcopy(own, own, k + 1, minus).start()

    def ring_pass(before, after, lower, upper, k, plus, minus):
        arrived(before, k)
        rcopy(lower(before), lower(before), k + 2, plus).start()
        arrived(after, k + 1)
        rcopy(upper(after), upper(after), k + 3, minus).start()

    def ring_end(far, lower, upper, k):
        arrived(lower(far), k + 2)
        arrived(upper(far), k + 3)

    def ring_sent(own, lower, upper, k):
        left_here(own, k)
        left_here(own, k + 1)
        left_here(lower(own), k + 2)
        left_here(upper(own), k + 3)

    def first(n):
        return lambda ref: ref.at[pl.ds(0, n)]

    def second(n):
        return lambda ref: ref.at[pl.ds(n, n)]

    inward = [
        (hom.at[pl.ds(rj * 4, 4)], xin),
        (fscale_in, fscale),
        (pair_in, pair),
        (pgain_in, pgain),
        (bw_in, bw),
        (wq, wbuf.at[rj, pl.ds(0, 64)]),
        (wk, wbuf.at[rj, pl.ds(64, 64)]),
        (wv, wbuf.at[rj, pl.ds(128, 64)]),
        (wg, wbuf.at[rj, pl.ds(192, 64)]),
        (wo, wbuf.at[rj, pl.ds(256, 64)]),
        (resm_in, resm),
        (rows_in, rows),
        (rowv_in, rowv),
        (gb_in, gb),
        (cscale_in, cscale),
        (p1_in, p1),
        (p2_in, p2),
        (ow_in, ow),
    ]

    def local(k):
        return pltpu.make_async_copy(inward[k][0], inward[k][1], lsem.at[k])

    for k in range(len(inward)):
        local(k).start()

    barrier = pltpu.get_barrier_semaphore()

    def greet(dev):
        pl.semaphore_signal(barrier, inc=1, device_id=dev, device_id_type=pl.DeviceIdType.MESH)

    for dev in ypeer + [plus_x, minus_x] + zpeer + [{"ri": mate}, up, down]:
        greet(dev)
    for t in range(4):

        @pl.when(jnp.logical_not(jnp.logical_and(diagonal, ri == t)))
        def _():
            greet(rdest[t])

        @pl.when(jnp.logical_not(jnp.logical_and(diagonal, zl == t)))
        def _():
            greet(rsrc[t])

    local(0).wait()
    local(1).wait()

    def norm_x(s, carry):
        xn[s, ri] = norm(xin[s].astype(F32), fscale[...]).astype(BF)
        return carry

    lax.fori_loop(0, 4, norm_x, 0)

    pl.semaphore_wait(barrier, 19 - 2 * diagonal.astype(jnp.int32))

    def send_x(s):
        rcopy(xn.at[s, ri, pl.ds(0, 64)], relay.at[0, s], RZ + s * 2, up).start()
        rcopy(xn.at[s, ri, pl.ds(64, 64)], relay.at[1, s], RZ + s * 2 + 1, down).start()
        rcopy(xn.at[s, ri], xn.at[s, ri], XM + s, {"ri": mate}).start()

    def relay_x(s):
        arrived(relay.at[0, s], RZ + s * 2)
        rcopy(relay.at[0, s], xn.at[s, ri_down, pl.ds(0, 64)], XZ + s * 2, up).start()
        arrived(relay.at[1, s], RZ + s * 2 + 1)
        rcopy(relay.at[1, s], xn.at[s, ri_up, pl.ds(64, 64)], XZ + s * 2 + 1, down).start()

    for s in range(4):
        send_x(s)
    for k in range(5, 10):
        local(k).wait()
    w_lower, w_upper = first(160), second(160)
    ring_start(wbuf.at[rj], WT, plus_y, minus_y)

    for k in range(2, 5):
        local(k).wait()
    pn[...] = norm(pair[...].astype(F32), pgain[...]).astype(BF).astype(F32)
    for j in range(8):
        tile = pn[pl.ds(j, 128, stride=8), :].astype(BF)
        bt[pl.ds(j, 8, stride=8), :] = nt(bw[...], tile)
    for half in range(2):
        bg[half, zl, x, rj] = bt[pl.ds(half * 32, 32), :].astype(BF)
    for d in (1, 2, 3):
        rcopy(bg.at[:, zl, x, rj], bg.at[:, zl, x, rj], BZ + d - 1, zpeer[d - 1]).start()
    relay_x(0)
    relay_x(1)

    for k in range(10, len(inward)):
        local(k).wait()
    ring_pass(
        wbuf.at[behind(rj, 1)], wbuf.at[ahead(rj, 1)], w_lower, w_upper, WT, plus_y, minus_y
    )
    for d in (1, 2, 3):
        arrived(bg.at[:, behind(zl, d), x, rj], BZ + d - 1)
    b_lower, b_upper = first(2), second(2)
    ring_start(bg.at[0, :, x, rj], AY, plus_y, minus_y)
    ring_start(bg.at[1, :, x, rj], BX, plus_x, minus_x)
    relay_x(2)

    row128 = lax.broadcasted_iota(jnp.int32, (128, 128), 0)
    col128 = lax.broadcasted_iota(jnp.int32, (128, 128), 1)
    ones = jnp.ones((128, 128), BF)
    for b in range(4):
        res = resm[pl.ds(b, 1), :].astype(F32)
        spread = jnp.where(row128 == col128, jnp.broadcast_to(res, (128, 128)), 0.0).astype(BF)
        cm[b] = mm(spread, ones)
    for b in range(2):
        gbt[pl.ds(b * 128, 128), :] = jnp.transpose(
            jnp.broadcast_to(gb[:, pl.ds(b * 128, 128)], (128, 128))
        )
    e128 = eye(128)
    for k in range(4):
        wst[pl.ds(k * 128, 128), :] = nt(e128, ow[pl.ds(k * 256, 256), :]).astype(BF)
    pick = (
        lax.broadcasted_iota(jnp.int32, (32, 128), 0)
        == lax.rem(lax.broadcasted_iota(jnp.int32, (32, 128), 1), 32)
    ).astype(F32).astype(BF)
    p1t = p1[...]
    p2r = jnp.concatenate([p2[...]] * 4, 0)
    total = jnp.maximum(jnp.sum(rowv[...].astype(F32)), 1.0)

    ring_pass(
        bg.at[0, :, x, behind(rj, 1)], bg.at[0, :, x, ahead(rj, 1)], b_lower, b_upper,
        AY, plus_y, minus_y,
    )
    ring_pass(
        bg.at[1, :, behind(x, 1), rj], bg.at[1, :, ahead(x, 1), rj], b_lower, b_upper,
        BX, plus_x, minus_x,
    )
    ring_end(bg.at[0, :, x, ahead(rj, 2)], b_lower, b_upper, AY)
    ring_start(bg.at[0, :, x], AX, plus_x, minus_x)
    ring_end(bg.at[1, :, ahead(x, 2), rj], b_lower, b_upper, BX)
    ring_start(bg.at[1, :, :, rj], BY, plus_y, minus_y)
    relay_x(3)

    def forward(s):
        arrived(xn.at[s, opp, pl.ds(0, 64)], XZ + s * 2)
        arrived(xn.at[s, opp, pl.ds(64, 64)], XZ + s * 2 + 1)
        rcopy(xn.at[s, opp], xn.at[s, opp], XF + s, {"ri": mate}).start()

    ring_pass(
        bg.at[0, :, behind(x, 1)], bg.at[0, :, ahead(x, 1)], b_lower, b_upper, AX, plus_x, minus_x
    )
    ring_pass(
        bg.at[1, :, :, behind(rj, 1)], bg.at[1, :, :, ahead(rj, 1)], b_lower, b_upper,
        BY, plus_y, minus_y,
    )
    forward(0)
    ring_end(wbuf.at[ahead(rj, 2)], w_lower, w_upper, WT)
    ring_end(bg.at[0, :, ahead(x, 2)], b_lower, b_upper, AX)
    ring_end(bg.at[1, :, :, ahead(rj, 2)], b_lower, b_upper, BY)

    keymask = (jnp.concatenate([cm[b] for b in range(4)], 0) - 1.0) * 1e9
    for hp in range(4):
        two = bg[hp // 2, :, :, :, pl.ds(hp % 2 * 16, 16), :].astype(F32).reshape(64, 2, 8, 128)
        for h in range(2):
            biasf[hp * 2 + h] = two[:, h].reshape(512, 128) + keymask

    def weight(k):
        return wbuf[:, pl.ds(k * 64, 64), :].reshape(256, 256)

    lane8 = lax.div(lax.broadcasted_iota(jnp.int32, (8, 128), 1), 32)

    def attend(s, carry):
        @pl.when(s < 3)
        def _():
            forward(s + 1)

        arrived(xn.at[s, mate], XM + s)
        arrived(xn.at[s, oppmate], XF + s)
        every = xn[s].reshape(512, 256)
        own = xn[s, ri]
        key = nt(every, weight(1)).astype(BF)
        value = nt(weight(2), every).astype(BF)
        query = (nt(weight(0), own) * 32 ** -0.5).astype(BF)
        gate = jax.nn.sigmoid(nt(weight(3), own) + gbt[...])
        parts = []
        for h in range(8):
            g, r = h // 4, h % 4
            pieces = [jnp.zeros((32, 128), BF)] * 4
            pieces[r] = query[h * 32 : h * 32 + 32]
            logits = mm(key[:, g * 128 : g * 128 + 128], jnp.concatenate(pieces, 0)) + biasf[h]
            top = jnp.max(logits, 0, keepdims=True)
            probs = jnp.exp(logits - top)
            denom = jnp.sum(probs, 0, keepdims=True)
            head = mm(value[h * 32 : h * 32 + 32], probs.astype(BF))
            parts.append(head * (1.0 / denom))
        attended = (jnp.concatenate(parts, 0) * gate).astype(BF)
        attended = nt(e128, attended).astype(BF)
        result = (xin[s].astype(F32) + mm(attended, weight(4))).astype(BF)
        al[s] = result
        pltpu.make_async_copy(al.at[s], out_al.at[rj * 4 + s], osem.at[s]).start()
        rcopy(al.at[s], out_al.at[rj * 4 + s], AL + s * 4, plus_y).start()
        rcopy(al.at[s], out_al.at[rj * 4 + s], AL + s * 4 + 1, minus_y).start()
        on = norm(result.astype(F32), cscale[...])
        keep = cm[ri] * rows[seq * 16 + rj * 4 + s].astype(F32)
        on = (on * jnp.concatenate([keep, keep], 1)).astype(BF)
        left = nt(p1t, on)
        right[...] = nt(on, p2r)
        for y in range(4):
            ltile = jnp.zeros((8, 128), F32)
            rtile = jnp.zeros((8, 128), F32)
            for k in range(4):
                piece = left[k * 8 : k * 8 + 8]
                if k != y:
                    piece = pltpu.roll(piece, (32 * (k - y)) % 128, 1)
                ltile = jnp.where(lane8 == k, piece, ltile)
                rtile = jnp.where(lane8 == k, right[pl.ds(y * 32 + k, 8, stride=4), :], rtile)
            sndf[y, pl.ds(pl.multiple_of(s * 8, 8), 8), :] = ltile
            sndf[y, pl.ds(pl.multiple_of(32 + s * 8, 8), 8), :] = rtile

        @pl.when(s > 0)
        def _():
            pass_out(s - 1)

        return carry

    a_lower, a_upper = first(64), second(64)

    def pass_out(s):
        ring_pass(
            out_al.at[behind(rj, 1) * 4 + s],
            out_al.at[ahead(rj, 1) * 4 + s],
            a_lower,
            a_upper,
            AL + s * 4,
            plus_y,
            minus_y,
        )

    lax.fori_loop(0, 4, attend, 0)

    snd[...] = sndf[...].astype(BF)
    for d in (1, 2, 3):
        rcopy(snd.at[ahead(rj, d)], rcv.at[rj], A2 + d - 1, ypeer[d - 1]).start()
    rcv[rj] = snd[rj]
    for d in (1, 2, 3):
        arrived(rcv.at[behind(rj, d)], A2 + d - 1)
    for y in range(4):
        block = rcv[y].astype(F32)
        for side in range(2):
            for s in range(4):
                r = side * 32 + s * 8
                scr[side, pl.ds(y * 4 + s, 8, stride=16), :] = block[r : r + 8]
    lb[:, pl.ds(seq, 1)] = scr[0].astype(BF).reshape(8, 1, 16, 128)
    rblock = scr[1].astype(BF).reshape(8, 16, 128)
    rst[...] = rblock

    @pl.when(diagonal)
    def _():
        rb[:, pl.ds(seq, 1)] = rblock.reshape(8, 1, 16, 128)

    for d in (1, 2, 3):
        rcopy(lb.at[:, seq], lb.at[:, seq], LZ + d - 1, zpeer[d - 1]).start()

    def rfirst(t):
        return rcopy(rst, rb.at[:, seq], R2 + zl, rdest[t], R2 + t)

    for t in range(4):

        @pl.when(jnp.logical_not(jnp.logical_and(diagonal, ri == t)))
        def _():
            rfirst(t).start()

    q_lower, q_upper = first(4), second(4)
    for b in range(4):
        src = behind(zl, b) * 4 + x
        if b > 0:
            arrived(lb.at[:, src], LZ + b - 1)
        ring_start(lb.at[:, src], LX + b * 4, plus_x, minus_x)
        came = b * 4 + rj

        @pl.when(jnp.logical_not(jnp.logical_and(diagonal, zl == b)))
        def _():
            arrived(rb.at[:, came], R2 + b)

        ring_start(rb.at[:, came], R4 + b * 4, plus_y, minus_y)
    for b in range(4):
        z4 = behind(zl, b) * 4
        ring_pass(
            lb.at[:, z4 + behind(x, 1)], lb.at[:, z4 + ahead(x, 1)], q_lower, q_upper,
            LX + b * 4, plus_x, minus_x,
        )
        ring_pass(
            rb.at[:, b * 4 + behind(rj, 1)], rb.at[:, b * 4 + ahead(rj, 1)], q_lower, q_upper,
            R4 + b * 4, plus_y, minus_y,
        )
    for b in range(4):
        ring_end(lb.at[:, behind(zl, b) * 4 + ahead(x, 2)], q_lower, q_upper, LX + b * 4)
        ring_end(rb.at[:, b * 4 + ahead(rj, 2)], q_lower, q_upper, R4 + b * 4)
    pass_out(3)

    lane128 = lax.div(lax.broadcasted_iota(jnp.int32, (128, 128), 1), 32)

    def product(peer, u):
        turned = nt(e128, rb[peer * 2 + u].reshape(256, 128)).astype(BF)
        for k in range(8):
            outer = mm(turned, lb[k].reshape(256, 128)).astype(BF)
            for j in range(4):
                bscr[j // 2, pl.ds(k * 32, 32), pl.ds((j % 2) * 128, 128)] = outer[
                    j * 32 : j * 32 + 32
                ]
        for jp in range(2):
            wide = mm(wst[...], bscr[jp])
            for half in range(2):
                c = half * 128
                mixed = wide[0:128, c : c + 128]
                for k in range(1, 4):
                    mixed = jnp.where(
                        lane128 == k, wide[k * 128 : k * 128 + 128, c : c + 128], mixed
                    )
                ub[peer, pl.ds(u * 4 + jp * 2 + half, 32, stride=8), :] = nt(
                    pick, mixed.astype(BF)
                )

    for d in (1, 2, 3, 4):
        peer = ahead(rj, d)
        for u in range(2):
            product(peer, u)
        ubf[peer] = ub[peer].astype(BF)
        if d < 4:
            rcopy(ubf.at[peer], urecv.at[rj], UP + d - 1, ypeer[d - 1]).start()
    urecv[rj] = ubf[rj]
    scale = 1.0 / total
    for d in (1, 2, 3):
        arrived(urecv.at[behind(rj, d)], UP + d - 1)
    out_pair[...] = (
        pair[...].astype(F32) + urecv[...].reshape(1024, 128).astype(F32) * scale
    ).astype(BF)

    for s in range(4):
        pltpu.make_async_copy(al.at[s], out_al.at[rj * 4 + s], osem.at[s]).wait()
        for half in range(2):
            left_here(relay.at[half, s], RZ + s * 2 + half)
            left_here(relay.at[half, s], XZ + s * 2 + half)
        left_here(xn.at[s, ri], XM + s)
        left_here(xn.at[s, opp], XF + s)
        ring_end(out_al.at[ahead(rj, 2) * 4 + s], a_lower, a_upper, AL + s * 4)
        ring_sent(al.at[s], a_lower, a_upper, AL + s * 4)
    ring_sent(wbuf.at[rj], w_lower, w_upper, WT)
    ring_sent(bg.at[0, :, x, rj], b_lower, b_upper, AY)
    ring_sent(bg.at[0, :, x], b_lower, b_upper, AX)
    ring_sent(bg.at[1, :, x, rj], b_lower, b_upper, BX)
    ring_sent(bg.at[1, :, :, rj], b_lower, b_upper, BY)
    for d in (1, 2, 3):
        left_here(bg.at[:, zl, x, rj], BZ + d - 1)
        left_here(snd.at[ahead(rj, d)], A2 + d - 1)
        left_here(lb.at[:, seq], LZ + d - 1)
        left_here(ubf.at[ahead(rj, d)], UP + d - 1)
    for b in range(4):
        ring_sent(lb.at[:, behind(zl, b) * 4 + x], q_lower, q_upper, LX + b * 4)
        ring_sent(rb.at[:, b * 4 + rj], q_lower, q_upper, R4 + b * 4)
    for t in range(4):

        @pl.when(jnp.logical_not(jnp.logical_and(diagonal, ri == t)))
        def _():
            left_here(rst, R2 + t)


def on_device(
    homolog_embedding,
    pairwise_state,
    residue_mask,
    alignment_row_mask,
    focus_layer_scale,
    asking_projector,
    lookup_projector,
    content_projector,
    sigmoid_projector,
    gate_offset_bias,
    final_projector,
    pairwise_norm_gain,
    bias_weight,
    cross_layer_scale,
    first_cross_projector,
    second_cross_projector,
    outer_weight,
):
    vmem = pl.BlockSpec(memory_space=pltpu.VMEM)
    hbm = pl.BlockSpec(memory_space=pl.ANY)
    alignment_output, pair_rows = pl.pallas_call(
        kernel,
        out_shape=(
            jax.ShapeDtypeStruct((16, 128, 256), BF),
            jax.ShapeDtypeStruct((1024, 128), BF),
        ),
        in_specs=[hbm] * 18,
        out_specs=(hbm, vmem),
        scratch_shapes=[
            pltpu.VMEM((4, 128, 256), BF),
            pltpu.VMEM((1024, 128), BF),
            pltpu.VMEM((4, 128), jnp.int32),
            pltpu.SMEM((256,), jnp.int32),
            pltpu.VMEM((2, 128), jnp.int32),
            pltpu.VMEM((1, 256), F32),
            pltpu.VMEM((1, 256), F32),
            pltpu.VMEM((1, 128), F32),
            pltpu.VMEM((8, 128), BF),
            pltpu.VMEM((1, 256), F32),
            pltpu.VMEM((32, 256), BF),
            pltpu.VMEM((32, 256), BF),
            pltpu.VMEM((1024, 128), BF),
            pltpu.VMEM((4, 4, 128, 256), BF),
            pltpu.VMEM((2, 4, 64, 256), BF),
            pltpu.VMEM((4, 320, 256), BF),
            pltpu.VMEM((1024, 128), F32),
            pltpu.VMEM((64, 128), F32),
            pltpu.VMEM((2, 4, 4, 4, 32, 128), BF),
            pltpu.VMEM((8, 512, 128), F32),
            pltpu.VMEM((256, 128), F32),
            pltpu.VMEM((4, 128, 128), F32),
            pltpu.VMEM((512, 256), BF),
            pltpu.VMEM((4, 128, 256), BF),
            pltpu.VMEM((128, 128), F32),
            pltpu.VMEM((4, 64, 128), F32),
            pltpu.VMEM((4, 64, 128), BF),
            pltpu.VMEM((4, 64, 128), BF),
            pltpu.VMEM((2, 128, 128), F32),
            pltpu.VMEM((8, 16, 16, 128), BF),
            pltpu.VMEM((8, 16, 128), BF),
            pltpu.VMEM((8, 16, 16, 128), BF),
            pltpu.VMEM((2, 256, 256), BF),
            pltpu.VMEM((4, 256, 128), F32),
            pltpu.VMEM((4, 256, 128), BF),
            pltpu.VMEM((4, 256, 128), BF),
            pltpu.SemaphoreType.DMA((COUNT,)),
            pltpu.SemaphoreType.DMA((COUNT,)),
            pltpu.SemaphoreType.DMA((18,)),
            pltpu.SemaphoreType.DMA((4,)),
        ],
        compiler_params=pltpu.CompilerParams(
            collective_id=0, has_side_effects=True, vmem_limit_bytes=60 * 1024 * 1024
        ),
        cost_estimate=pl.CostEstimate(
            flops=4_000_000_000, bytes_accessed=4_000_000, transcendentals=2_000_000
        ),
    )(
        homolog_embedding,
        pairwise_state.reshape(1024, 128),
        residue_mask.reshape(4, 128),
        alignment_row_mask,
        alignment_row_mask.reshape(2, 128),
        focus_layer_scale.reshape(1, 256),
        asking_projector.T,
        lookup_projector.T,
        content_projector.T,
        sigmoid_projector.T,
        gate_offset_bias.reshape(1, 256),
        final_projector,
        pairwise_norm_gain.reshape(1, 128),
        bias_weight.T,
        cross_layer_scale.reshape(1, 256),
        first_cross_projector.T,
        second_cross_projector.T,
        outer_weight,
    )
    return alignment_output, pair_rows.reshape(128, 8, 128)


def solution(mesh):
    placed = (
        P("seq", "ri", None),
        P("ri", ("seq", "rj"), None),
        P(),
        P(),
        P(),
        P(None, "rj"),
        P(None, "rj"),
        P(None, "rj"),
        P(None, "rj"),
        P(),
        P("rj", None),
        P(),
        P(),
        P(),
        P(),
        P(),
        P(),
    )
    return jax.shard_map(
        on_device,
        mesh=mesh,
        in_specs=placed,
        out_specs=(P("seq", "ri", None), P("ri", ("seq", "rj"), None)),
        check_vma=False,
    )
```

```python
import jax
import jax.numpy as jnp
from jax import lax
from jax.experimental import pallas as pl
from jax.experimental.pallas import tpu as pltpu
from jax.sharding import PartitionSpec as P

F32 = jnp.float32
BF = jnp.bfloat16
NT = (((1,), (1,)), ((), ()))

RZ, XZ, XM, XF = 0, 8, 16, 20
WT, BZ = 24, 28
AY, AX, BX, BY = 31, 35, 39, 43
AL, A2 = 47, 63
LZ, LX = 66, 69
R2, R4 = 85, 89
UP = 105
COUNT = 108


def nt(a, b):
    return lax.dot_general(a, b, NT, preferred_element_type=F32)


def mm(a, b):
    return jnp.dot(a, b, preferred_element_type=F32)


def norm(values, gain):
    centre = values - jnp.mean(values, -1, keepdims=True)
    spread = jnp.mean(centre * centre, -1, keepdims=True)
    return centre * lax.rsqrt(spread + 1e-5) * gain


def eye(n):
    row = lax.broadcasted_iota(jnp.int32, (n, n), 0)
    col = lax.broadcasted_iota(jnp.int32, (n, n), 1)
    return (row == col).astype(F32).astype(BF)


def kernel(
    hom, pair_in, resm_in, rows_in, rowv_in, fscale_in, wq, wk, wv, wg, gb_in, wo, pgain_in, bw_in,
    cscale_in, p1_in, p2_in, ow_in,
    out_al, out_pair,
    xin, pair, resm, rows, rowv, fscale, gb, pgain, bw, cscale, p1, p2, ow,
    xn, relay, wbuf, pn, bt, bg, wkn, wqvg, kb, qt, vt, gate, biasb, gbt, cm, wst, al, right, sndf, snd, rcv, scr, lb, rst, rb,
    bscr, ub, ubf, urecv,
    ssem, rsem, lsem, osem,
):
    seq = lax.axis_index("seq")
    ri = lax.axis_index("ri")
    rj = lax.axis_index("rj")
    zl, x = lax.div(seq, 4), lax.rem(seq, 4)
    mate = ri + 1 - 2 * lax.rem(ri, 2)
    opp = lax.rem(ri + 2, 4)
    oppmate = lax.rem(mate + 2, 4)

    def ahead(v, d):
        return lax.rem(v + d, 4)

    def behind(v, d):
        return lax.rem(v + 4 - d, 4)

    plus_y, minus_y = {"rj": ahead(rj, 1)}, {"rj": behind(rj, 1)}
    plus_x, minus_x = {"seq": zl * 4 + ahead(x, 1)}, {"seq": zl * 4 + behind(x, 1)}
    core, z = lax.rem(ri, 2), lax.div(ri, 2) * 4 + zl

    def along_z(step):
        to = lax.rem(z + step, 8)
        return lax.div(to, 4) * 2 + core, {
            "seq": lax.rem(to, 4) * 4 + x,
            "ri": lax.div(to, 4) * 2 + core,
        }

    ri_up, up = along_z(2)
    ri_down, down = along_z(6)
    ypeer = [{"rj": ahead(rj, d)} for d in (1, 2, 3)]
    zpeer = [{"seq": ahead(zl, d) * 4 + x} for d in (1, 2, 3)]
    rdest = [{"seq": ri * 4 + rj, "ri": t, "rj": x} for t in range(4)]
    rsrc = [{"seq": t * 4 + rj, "ri": zl, "rj": x} for t in range(4)]
    diagonal = jnp.logical_and(zl == ri, x == rj)

    def rcopy(src, dst, k, dev, send=None):
        return pltpu.make_async_remote_copy(
            src_ref=src,
            dst_ref=dst,
            send_sem=ssem.at[k if send is None else send],
            recv_sem=rsem.at[k],
            device_id=dev,
            device_id_type=pl.DeviceIdType.MESH,
        )

    def arrived(ref, k):
        pltpu.make_async_copy(ref, ref, rsem.at[k]).wait()

    def left_here(ref, k):
        pltpu.make_async_copy(ref, ref, ssem.at[k]).wait()

    def ring_start(own, k, plus, minus):
        rcopy(own, own, k, plus).start()
        rcopy(own, own, k + 1, minus).start()

    def ring_pass(before, after, lower, upper, k, plus, minus):
        arrived(before, k)
        rcopy(lower(before), lower(before), k + 2, plus).start()
        arrived(after, k + 1)
        rcopy(upper(after), upper(after), k + 3, minus).start()

    def ring_end(far, lower, upper, k):
        arrived(lower(far), k + 2)
        arrived(upper(far), k + 3)

    def ring_sent(own, lower, upper, k):
        left_here(own, k)
        left_here(own, k + 1)
        left_here(lower(own), k + 2)
        left_here(upper(own), k + 3)

    def first(n):
        return lambda ref: ref.at[pl.ds(0, n)]

    def second(n):
        return lambda ref: ref.at[pl.ds(n, n)]

    inward = [
        (hom.at[pl.ds(rj * 4, 4)], xin),
        (fscale_in, fscale),
        (pair_in, pair),
        (pgain_in, pgain),
        (bw_in, bw),
        (wq, wbuf.at[rj, pl.ds(0, 64)]),
        (wk, wbuf.at[rj, pl.ds(64, 64)]),
        (wv, wbuf.at[rj, pl.ds(128, 64)]),
        (wg, wbuf.at[rj, pl.ds(192, 64)]),
        (wo, wbuf.at[rj, pl.ds(256, 64)]),
        (resm_in, resm),
        (rows_in, rows),
        (rowv_in, rowv),
        (gb_in, gb),
        (cscale_in, cscale),
        (p1_in, p1),
        (p2_in, p2),
        (ow_in, ow),
    ]

    def local(k):
        return pltpu.make_async_copy(inward[k][0], inward[k][1], lsem.at[k])

    for k in range(len(inward)):
        local(k).start()

    barrier = pltpu.get_barrier_semaphore()

    def greet(dev):
        pl.semaphore_signal(barrier, inc=1, device_id=dev, device_id_type=pl.DeviceIdType.MESH)

    for dev in ypeer + [plus_x, minus_x] + zpeer + [{"ri": mate}, up, down]:
        greet(dev)
    for t in range(4):

        @pl.when(jnp.logical_not(jnp.logical_and(diagonal, ri == t)))
        def _():
            greet(rdest[t])

        @pl.when(jnp.logical_not(jnp.logical_and(diagonal, zl == t)))
        def _():
            greet(rsrc[t])

    local(0).wait()
    local(1).wait()

    def norm_x(s, carry):
        xn[s, ri] = norm(xin[s].astype(F32), fscale[...]).astype(BF)
        return carry

    lax.fori_loop(0, 4, norm_x, 0)

    pl.semaphore_wait(barrier, 19 - 2 * diagonal.astype(jnp.int32))

    def send_x(s):
        rcopy(xn.at[s, ri, pl.ds(0, 64)], relay.at[0, s], RZ + s * 2, up).start()
        rcopy(xn.at[s, ri, pl.ds(64, 64)], relay.at[1, s], RZ + s * 2 + 1, down).start()
        rcopy(xn.at[s, ri], xn.at[s, ri], XM + s, {"ri": mate}).start()

    def relay_x(s):
        arrived(relay.at[0, s], RZ + s * 2)
        rcopy(relay.at[0, s], xn.at[s, ri_down, pl.ds(0, 64)], XZ + s * 2, up).start()
        arrived(relay.at[1, s], RZ + s * 2 + 1)
        rcopy(relay.at[1, s], xn.at[s, ri_up, pl.ds(64, 64)], XZ + s * 2 + 1, down).start()

    for s in range(4):
        send_x(s)
    for k in range(5, 10):
        local(k).wait()
    w_lower, w_upper = first(160), second(160)
    ring_start(wbuf.at[rj], WT, plus_y, minus_y)

    for k in range(2, 5):
        local(k).wait()
    pn[...] = norm(pair[...].astype(F32), pgain[...]).astype(BF).astype(F32)
    for j in range(8):
        tile = pn[pl.ds(j, 128, stride=8), :].astype(BF)
        bt[pl.ds(j, 8, stride=8), :] = nt(bw[...], tile)
    for half in range(2):
        bg[half, zl, x, rj] = bt[pl.ds(half * 32, 32), :].astype(BF)
    for d in (1, 2, 3):
        rcopy(bg.at[:, zl, x, rj], bg.at[:, zl, x, rj], BZ + d - 1, zpeer[d - 1]).start()
    relay_x(0)
    relay_x(1)

    for k in range(10, len(inward)):
        local(k).wait()
    ring_pass(
        wbuf.at[behind(rj, 1)], wbuf.at[ahead(rj, 1)], w_lower, w_upper, WT, plus_y, minus_y
    )
    for d in (1, 2, 3):
        arrived(bg.at[:, behind(zl, d), x, rj], BZ + d - 1)
    b_lower, b_upper = first(2), second(2)
    ring_start(bg.at[0, :, x, rj], AY, plus_y, minus_y)
    ring_start(bg.at[1, :, x, rj], BX, plus_x, minus_x)
    relay_x(2)

    row128 = lax.broadcasted_iota(jnp.int32, (128, 128), 0)
    col128 = lax.broadcasted_iota(jnp.int32, (128, 128), 1)
    ones = jnp.ones((128, 128), BF)
    for b in range(4):
        res = resm[pl.ds(b, 1), :].astype(F32)
        spread = jnp.where(row128 == col128, jnp.broadcast_to(res, (128, 128)), 0.0).astype(BF)
        cm[b] = mm(spread, ones)
    for b in range(2):
        gbt[pl.ds(b * 128, 128), :] = jnp.transpose(
            jnp.broadcast_to(gb[:, pl.ds(b * 128, 128)], (128, 128))
        )
    e128 = eye(128)
    for k in range(4):
        wst[pl.ds(k * 128, 128), :] = nt(e128, ow[pl.ds(k * 256, 256), :]).astype(BF)
    pick = (
        lax.broadcasted_iota(jnp.int32, (32, 128), 0)
        == lax.rem(lax.broadcasted_iota(jnp.int32, (32, 128), 1), 32)
    ).astype(F32).astype(BF)
    p1t = p1[...]
    p2r = jnp.concatenate([p2[...]] * 4, 0)
    total = jnp.maximum(jnp.sum(rowv[...].astype(F32)), 1.0)

    ring_pass(
        bg.at[0, :, x, behind(rj, 1)], bg.at[0, :, x, ahead(rj, 1)], b_lower, b_upper,
        AY, plus_y, minus_y,
    )
    ring_pass(
        bg.at[1, :, behind(x, 1), rj], bg.at[1, :, ahead(x, 1), rj], b_lower, b_upper,
        BX, plus_x, minus_x,
    )
    ring_end(bg.at[0, :, x, ahead(rj, 2)], b_lower, b_upper, AY)
    ring_start(bg.at[0, :, x], AX, plus_x, minus_x)
    ring_end(bg.at[1, :, ahead(x, 2), rj], b_lower, b_upper, BX)
    ring_start(bg.at[1, :, :, rj], BY, plus_y, minus_y)
    relay_x(3)

    ring_end(wbuf.at[ahead(rj, 2)], w_lower, w_upper, WT)

    def weight(k):
        return wbuf[:, pl.ds(k * 64, 64), :].reshape(256, 256)

    wkn[...] = nt(eye(256), weight(1)).astype(BF)
    wqvg[0:256] = weight(0)
    wqvg[256:512] = weight(2)
    wqvg[512:768] = weight(3)

    def own_rows(s, carry):
        block = xn[s, ri]
        kb[s, ri] = mm(block, wkn[...]).astype(BF)
        three = nt(wqvg[...], block)
        qt[s] = (three[0:256] * 32 ** -0.5).astype(BF)
        vt[s, ri] = three[256:512].astype(BF)
        gate[s] = jax.nn.sigmoid(three[512:768] + gbt[...])
        return carry

    def other_rows(s, b):
        block = xn[s, b]
        kb[s, b] = mm(block, wkn[...]).astype(BF)
        vt[s, b] = nt(wqvg[256:512], block).astype(BF)

    lax.fori_loop(0, 4, own_rows, 0)
    ring_pass(
        bg.at[0, :, behind(x, 1)], bg.at[0, :, ahead(x, 1)], b_lower, b_upper, AX, plus_x, minus_x
    )
    ring_pass(
        bg.at[1, :, :, behind(rj, 1)], bg.at[1, :, :, ahead(rj, 1)], b_lower, b_upper,
        BY, plus_y, minus_y,
    )

    def near_rows(s, carry):
        arrived(xn.at[s, mate], XM + s)
        other_rows(s, mate)
        return carry

    def far_rows(s, carry):
        arrived(xn.at[s, opp, pl.ds(0, 64)], XZ + s * 2)
        arrived(xn.at[s, opp, pl.ds(64, 64)], XZ + s * 2 + 1)
        rcopy(xn.at[s, opp], xn.at[s, opp], XF + s, {"ri": mate}).start()
        other_rows(s, opp)
        return carry

    def last_rows(s, carry):
        arrived(xn.at[s, oppmate], XF + s)
        other_rows(s, oppmate)
        return carry

    lax.fori_loop(0, 4, near_rows, 0)
    lax.fori_loop(0, 4, far_rows, 0)
    lax.fori_loop(0, 4, last_rows, 0)
    ring_end(bg.at[0, :, ahead(x, 2)], b_lower, b_upper, AX)
    ring_end(bg.at[1, :, :, ahead(rj, 2)], b_lower, b_upper, BY)

    keymask = (jnp.concatenate([cm[b] for b in range(4)], 0) - 1.0) * 1e9
    for hp in range(4):
        two = bg[hp // 2, :, :, :, pl.ds(hp % 2 * 16, 16), :].astype(F32).reshape(64, 2, 8, 128)
        for h in range(2):
            biasb[hp * 2 + h] = (two[:, h].reshape(512, 128) + keymask).astype(BF)

    lane8 = lax.div(lax.broadcasted_iota(jnp.int32, (8, 128), 1), 32)

    def attend(s, carry):
        key = kb[s].reshape(512, 256)
        value = jnp.concatenate([vt[s, b] for b in range(4)], 1)
        query = qt[s]
        parts = []
        for h in range(8):
            g, r = h // 4, h % 4
            pieces = [jnp.zeros((32, 128), BF)] * 4 + [e128]
            pieces[r] = query[h * 32 : h * 32 + 32]
            logits = mm(
                jnp.concatenate([key[:, g * 128 : g * 128 + 128], biasb[h]], 1),
                jnp.concatenate(pieces, 0),
            )
            probs = jnp.exp(logits - jnp.max(logits, 0, keepdims=True)).astype(BF)
            summed = mm(
                jnp.concatenate([value[h * 32 : h * 32 + 32], jnp.ones((16, 512), BF)], 0), probs
            )
            parts.append(summed[0:32] * (1.0 / summed[32:33]))
        attended = (jnp.concatenate(parts, 0) * gate[s]).astype(BF)
        attended = nt(e128, attended).astype(BF)
        result = (xin[s].astype(F32) + mm(attended, weight(4))).astype(BF)
        al[s] = result
        pltpu.make_async_copy(al.at[s], out_al.at[rj * 4 + s], osem.at[s]).start()

        @pl.when(s < 2)
        def _():
            start_out(s)

        on = norm(result.astype(F32), cscale[...])
        keep = cm[ri] * rows[seq * 16 + rj * 4 + s].astype(F32)
        on = (on * jnp.concatenate([keep, keep], 1)).astype(BF)
        left = nt(p1t, on)
        right[...] = nt(on, p2r)
        for y in range(4):
            ltile = jnp.zeros((8, 128), F32)
            rtile = jnp.zeros((8, 128), F32)
            for k in range(4):
                piece = left[k * 8 : k * 8 + 8]
                if k != y:
                    piece = pltpu.roll(piece, (32 * (k - y)) % 128, 1)
                ltile = jnp.where(lane8 == k, piece, ltile)
                rtile = jnp.where(lane8 == k, right[pl.ds(y * 32 + k, 8, stride=4), :], rtile)
            sndf[y, pl.ds(pl.multiple_of(s * 8, 8), 8), :] = ltile
            sndf[y, pl.ds(pl.multiple_of(32 + s * 8, 8), 8), :] = rtile
        return carry

    a_lower, a_upper = first(64), second(64)

    def start_out(s):
        rcopy(al.at[s], out_al.at[rj * 4 + s], AL + s * 4, plus_y).start()
        rcopy(al.at[s], out_al.at[rj * 4 + s], AL + s * 4 + 1, minus_y).start()

    def pass_out(s):
        ring_pass(
            out_al.at[behind(rj, 1) * 4 + s],
            out_al.at[ahead(rj, 1) * 4 + s],
            a_lower,
            a_upper,
            AL + s * 4,
            plus_y,
            minus_y,
        )

    lax.fori_loop(0, 4, attend, 0)

    snd[...] = sndf[...].astype(BF)
    for d in (1, 2, 3):
        rcopy(snd.at[ahead(rj, d)], rcv.at[rj], A2 + d - 1, ypeer[d - 1]).start()
    rcv[rj] = snd[rj]
    for d in (1, 2, 3):
        arrived(rcv.at[behind(rj, d)], A2 + d - 1)
    for y in range(4):
        block = rcv[y].astype(F32)
        for side in range(2):
            for s in range(4):
                r = side * 32 + s * 8
                scr[side, pl.ds(y * 4 + s, 8, stride=16), :] = block[r : r + 8]
    lb[:, pl.ds(seq, 1)] = scr[0].astype(BF).reshape(8, 1, 16, 128)
    rblock = scr[1].astype(BF).reshape(8, 16, 128)
    rst[...] = rblock

    @pl.when(diagonal)
    def _():
        rb[:, pl.ds(seq, 1)] = rblock.reshape(8, 1, 16, 128)

    for d in (1, 2, 3):
        rcopy(lb.at[:, seq], lb.at[:, seq], LZ + d - 1, zpeer[d - 1]).start()

    def rfirst(t):
        return rcopy(rst, rb.at[:, seq], R2 + zl, rdest[t], R2 + t)

    for t in range(4):

        @pl.when(jnp.logical_not(jnp.logical_and(diagonal, ri == t)))
        def _():
            rfirst(t).start()

    start_out(2)
    q_lower, q_upper = first(4), second(4)
    for b in range(4):
        src = behind(zl, b) * 4 + x
        if b > 0:
            arrived(lb.at[:, src], LZ + b - 1)
        ring_start(lb.at[:, src], LX + b * 4, plus_x, minus_x)
        came = b * 4 + rj

        @pl.when(jnp.logical_not(jnp.logical_and(diagonal, zl == b)))
        def _():
            arrived(rb.at[:, came], R2 + b)

        ring_start(rb.at[:, came], R4 + b * 4, plus_y, minus_y)
    for b in range(4):
        z4 = behind(zl, b) * 4
        ring_pass(
            lb.at[:, z4 + behind(x, 1)], lb.at[:, z4 + ahead(x, 1)], q_lower, q_upper,
            LX + b * 4, plus_x, minus_x,
        )
        ring_pass(
            rb.at[:, b * 4 + behind(rj, 1)], rb.at[:, b * 4 + ahead(rj, 1)], q_lower, q_upper,
            R4 + b * 4, plus_y, minus_y,
        )
    for b in range(4):
        ring_end(lb.at[:, behind(zl, b) * 4 + ahead(x, 2)], q_lower, q_upper, LX + b * 4)
        ring_end(rb.at[:, b * 4 + ahead(rj, 2)], q_lower, q_upper, R4 + b * 4)
    start_out(3)

    lane128 = lax.div(lax.broadcasted_iota(jnp.int32, (128, 128), 1), 32)

    def product(peer, u):
        turned = nt(e128, rb[peer * 2 + u].reshape(256, 128)).astype(BF)
        for k in range(8):
            outer = mm(turned, lb[k].reshape(256, 128)).astype(BF)
            for j in range(4):
                bscr[j // 2, pl.ds(k * 32, 32), pl.ds((j % 2) * 128, 128)] = outer[
                    j * 32 : j * 32 + 32
                ]
        for jp in range(2):
            wide = mm(wst[...], bscr[jp])
            for half in range(2):
                c = half * 128
                mixed = wide[0:128, c : c + 128]
                for k in range(1, 4):
                    mixed = jnp.where(
                        lane128 == k, wide[k * 128 : k * 128 + 128, c : c + 128], mixed
                    )
                ub[peer, pl.ds(u * 4 + jp * 2 + half, 32, stride=8), :] = nt(
                    pick, mixed.astype(BF)
                )

    for d in (1, 2, 3, 4):
        pass_out(d - 1)
        peer = ahead(rj, d)
        for u in range(2):
            product(peer, u)
        ubf[peer] = ub[peer].astype(BF)
        if d < 4:
            rcopy(ubf.at[peer], urecv.at[rj], UP + d - 1, ypeer[d - 1]).start()
    urecv[rj] = ubf[rj]
    scale = 1.0 / total
    for d in (1, 2, 3):
        arrived(urecv.at[behind(rj, d)], UP + d - 1)
    out_pair[...] = (
        pair[...].astype(F32) + urecv[...].reshape(1024, 128).astype(F32) * scale
    ).astype(BF)

    for s in range(4):
        pltpu.make_async_copy(al.at[s], out_al.at[rj * 4 + s], osem.at[s]).wait()
        for half in range(2):
            left_here(relay.at[half, s], RZ + s * 2 + half)
            left_here(relay.at[half, s], XZ + s * 2 + half)
        left_here(xn.at[s, ri], XM + s)
        left_here(xn.at[s, opp], XF + s)
        ring_end(out_al.at[ahead(rj, 2) * 4 + s], a_lower, a_upper, AL + s * 4)
        ring_sent(al.at[s], a_lower, a_upper, AL + s * 4)
    ring_sent(wbuf.at[rj], w_lower, w_upper, WT)
    ring_sent(bg.at[0, :, x, rj], b_lower, b_upper, AY)
    ring_sent(bg.at[0, :, x], b_lower, b_upper, AX)
    ring_sent(bg.at[1, :, x, rj], b_lower, b_upper, BX)
    ring_sent(bg.at[1, :, :, rj], b_lower, b_upper, BY)
    for d in (1, 2, 3):
        left_here(bg.at[:, zl, x, rj], BZ + d - 1)
        left_here(snd.at[ahead(rj, d)], A2 + d - 1)
        left_here(lb.at[:, seq], LZ + d - 1)
        left_here(ubf.at[ahead(rj, d)], UP + d - 1)
    for b in range(4):
        ring_sent(lb.at[:, behind(zl, b) * 4 + x], q_lower, q_upper, LX + b * 4)
        ring_sent(rb.at[:, b * 4 + rj], q_lower, q_upper, R4 + b * 4)
    for t in range(4):

        @pl.when(jnp.logical_not(jnp.logical_and(diagonal, ri == t)))
        def _():
            left_here(rst, R2 + t)


def on_device(
    homolog_embedding,
    pairwise_state,
    residue_mask,
    alignment_row_mask,
    focus_layer_scale,
    asking_projector,
    lookup_projector,
    content_projector,
    sigmoid_projector,
    gate_offset_bias,
    final_projector,
    pairwise_norm_gain,
    bias_weight,
    cross_layer_scale,
    first_cross_projector,
    second_cross_projector,
    outer_weight,
):
    vmem = pl.BlockSpec(memory_space=pltpu.VMEM)
    hbm = pl.BlockSpec(memory_space=pl.ANY)
    alignment_output, pair_rows = pl.pallas_call(
        kernel,
        out_shape=(
            jax.ShapeDtypeStruct((16, 128, 256), BF),
            jax.ShapeDtypeStruct((1024, 128), BF),
        ),
        in_specs=[hbm] * 18,
        out_specs=(hbm, vmem),
        scratch_shapes=[
            pltpu.VMEM((4, 128, 256), BF),
            pltpu.VMEM((1024, 128), BF),
            pltpu.VMEM((4, 128), jnp.int32),
            pltpu.SMEM((256,), jnp.int32),
            pltpu.VMEM((2, 128), jnp.int32),
            pltpu.VMEM((1, 256), F32),
            pltpu.VMEM((1, 256), F32),
            pltpu.VMEM((1, 128), F32),
            pltpu.VMEM((8, 128), BF),
            pltpu.VMEM((1, 256), F32),
            pltpu.VMEM((32, 256), BF),
            pltpu.VMEM((32, 256), BF),
            pltpu.VMEM((1024, 128), BF),
            pltpu.VMEM((4, 4, 128, 256), BF),
            pltpu.VMEM((2, 4, 64, 256), BF),
            pltpu.VMEM((4, 320, 256), BF),
            pltpu.VMEM((1024, 128), F32),
            pltpu.VMEM((64, 128), F32),
            pltpu.VMEM((2, 4, 4, 4, 32, 128), BF),
            pltpu.VMEM((256, 256), BF),
            pltpu.VMEM((768, 256), BF),
            pltpu.VMEM((4, 4, 128, 256), BF),
            pltpu.VMEM((4, 256, 128), BF),
            pltpu.VMEM((4, 4, 256, 128), BF),
            pltpu.VMEM((4, 256, 128), F32),
            pltpu.VMEM((8, 512, 128), BF),
            pltpu.VMEM((256, 128), F32),
            pltpu.VMEM((4, 128, 128), F32),
            pltpu.VMEM((512, 256), BF),
            pltpu.VMEM((4, 128, 256), BF),
            pltpu.VMEM((128, 128), F32),
            pltpu.VMEM((4, 64, 128), F32),
            pltpu.VMEM((4, 64, 128), BF),
            pltpu.VMEM((4, 64, 128), BF),
            pltpu.VMEM((2, 128, 128), F32),
            pltpu.VMEM((8, 16, 16, 128), BF),
            pltpu.VMEM((8, 16, 128), BF),
            pltpu.VMEM((8, 16, 16, 128), BF),
            pltpu.VMEM((2, 256, 256), BF),
            pltpu.VMEM((4, 256, 128), F32),
            pltpu.VMEM((4, 256, 128), BF),
            pltpu.VMEM((4, 256, 128), BF),
            pltpu.SemaphoreType.DMA((COUNT,)),
            pltpu.SemaphoreType.DMA((COUNT,)),
            pltpu.SemaphoreType.DMA((18,)),
            pltpu.SemaphoreType.DMA((4,)),
        ],
        compiler_params=pltpu.CompilerParams(
            collective_id=0, has_side_effects=True, vmem_limit_bytes=60 * 1024 * 1024
        ),
        cost_estimate=pl.CostEstimate(
            flops=4_000_000_000, bytes_accessed=4_000_000, transcendentals=2_000_000
        ),
    )(
        homolog_embedding,
        pairwise_state.reshape(1024, 128),
        residue_mask.reshape(4, 128),
        alignment_row_mask,
        alignment_row_mask.reshape(2, 128),
        focus_layer_scale.reshape(1, 256),
        asking_projector.T,
        lookup_projector.T,
        content_projector.T,
        sigmoid_projector.T,
        gate_offset_bias.reshape(1, 256),
        final_projector,
        pairwise_norm_gain.reshape(1, 128),
        bias_weight.T,
        cross_layer_scale.reshape(1, 256),
        first_cross_projector.T,
        second_cross_projector.T,
        outer_weight,
    )
    return alignment_output, pair_rows.reshape(128, 8, 128)


def solution(mesh):
    placed = (
        P("seq", "ri", None),
        P("ri", ("seq", "rj"), None),
        P(),
        P(),
        P(),
        P(None, "rj"),
        P(None, "rj"),
        P(None, "rj"),
        P(None, "rj"),
        P(),
        P("rj", None),
        P(),
        P(),
        P(),
        P(),
        P(),
        P(),
    )
    return jax.shard_map(
        on_device,
        mesh=mesh,
        in_specs=placed,
        out_specs=(P("seq", "ri", None), P("ri", ("seq", "rj"), None)),
        check_vma=False,
    )
```

```python
import jax
import jax.numpy as jnp
from jax import lax
from jax.experimental import pallas as pl
from jax.experimental.pallas import tpu as pltpu
from jax.sharding import PartitionSpec as P

F32 = jnp.float32
BF = jnp.bfloat16
NT = (((1,), (1,)), ((), ()))

SIZES = (8, 8, 4, 4, 6, 16, 16, 6, 6, 24, 16, 16, 6, 6, 3)
RZ, XZ, XM, XF, WT, BA, BB, AX, BY, AL, LL, RR, LX, R4, UP = (
    sum(SIZES[:i]) for i in range(len(SIZES))
)
COUNT = sum(SIZES)


def nt(a, b):
    return lax.dot_general(a, b, NT, preferred_element_type=F32)


def mm(a, b):
    return jnp.dot(a, b, preferred_element_type=F32)


def norm(values, gain):
    centre = values - jnp.mean(values, -1, keepdims=True)
    spread = jnp.mean(centre * centre, -1, keepdims=True)
    return centre * lax.rsqrt(spread + 1e-5) * gain


def eye(n):
    row = lax.broadcasted_iota(jnp.int32, (n, n), 0)
    col = lax.broadcasted_iota(jnp.int32, (n, n), 1)
    return (row == col).astype(F32).astype(BF)


def kernel(
    hom, pair_in, resm_in, rows_in, rowv_in, fscale_in, wq, wk, wv, wg, gb_in, wo, pgain_in, bw_in,
    cscale_in, p1_in, p2_in, ow_in,
    out_al, out_pair,
    xin, pair, resm, rows, rowv, fscale, gb, pgain, bw, cscale, p1, p2, ow,
    xn, relay, wbuf, pn, bt, bg, wkn, wqvg, kb, qt, vt, gate, biasb, gbt, cm, wst, al, right, sndf, snd, lraw, rraw, scr, lb, rb,
    bscr, ub, ubf, urecv,
    ssem, rsem, lsem, osem,
):
    seq = lax.axis_index("seq")
    ri = lax.axis_index("ri")
    rj = lax.axis_index("rj")
    zl, x = lax.div(seq, 4), lax.rem(seq, 4)
    mate = ri + 1 - 2 * lax.rem(ri, 2)
    opp = lax.rem(ri + 2, 4)
    oppmate = lax.rem(mate + 2, 4)

    def ahead(v, d):
        return lax.rem(v + d, 4)

    def behind(v, d):
        return lax.rem(v + 4 - d, 4)

    plus_y, minus_y = {"rj": ahead(rj, 1)}, {"rj": behind(rj, 1)}
    plus_x, minus_x = {"seq": zl * 4 + ahead(x, 1)}, {"seq": zl * 4 + behind(x, 1)}
    core, z = lax.rem(ri, 2), lax.div(ri, 2) * 4 + zl

    def along_z(step):
        to = lax.rem(z + step, 8)
        return lax.div(to, 4) * 2 + core, {
            "seq": lax.rem(to, 4) * 4 + x,
            "ri": lax.div(to, 4) * 2 + core,
        }

    ri_up, up = along_z(2)
    ri_down, down = along_z(6)

    def seq_of(zz, xx):
        return zz * 4 + xx

    def in_zy(n):
        return {"seq": seq_of(ahead(zl, lax.div(n, 4)), x), "rj": ahead(rj, lax.rem(n, 4))}

    def in_zx(n):
        return {"seq": seq_of(ahead(zl, lax.div(n, 4)), ahead(x, lax.rem(n, 4)))}

    def right_to(n):
        return {"seq": seq_of(ri, lax.div(n, 4)), "ri": lax.rem(n, 4), "rj": x}

    def right_from(n):
        return {"seq": seq_of(lax.div(n, 4), rj), "ri": zl, "rj": lax.rem(n, 4)}

    def each(low, high, body):
        def step(n, carry):
            body(n)
            return carry

        lax.fori_loop(low, high, step, 0)

    diagonal = jnp.logical_and(zl == ri, x == rj)

    def to_self(n):
        return jnp.logical_and(diagonal, n == seq_of(x, ri))

    def from_self(n):
        return jnp.logical_and(diagonal, n == seq_of(zl, rj))


    def rcopy(src, dst, k, dev, send=None):
        return pltpu.make_async_remote_copy(
            src_ref=src,
            dst_ref=dst,
            send_sem=ssem.at[k if send is None else send],
            recv_sem=rsem.at[k],
            device_id=dev,
            device_id_type=pl.DeviceIdType.MESH,
        )

    def arrived(ref, k):
        pltpu.make_async_copy(ref, ref, rsem.at[k]).wait()

    def left_here(ref, k):
        pltpu.make_async_copy(ref, ref, ssem.at[k]).wait()

    def ring_start(own, lower, upper, k, plus, minus):
        for i, (part, dev) in enumerate(
            ((lower, plus), (upper, minus), (upper, plus), (lower, minus))
        ):
            rcopy(part(own), part(own), k + i, dev).start()

    def ring_pass(before, after, lower, upper, k, plus, minus):
        arrived(lower(before), k)
        rcopy(lower(before), lower(before), k + 4, plus).start()
        arrived(upper(after), k + 1)
        rcopy(upper(after), upper(after), k + 5, minus).start()

    def ring_end(before, after, far, lower, upper, k):
        arrived(upper(before), k + 2)
        arrived(lower(after), k + 3)
        arrived(lower(far), k + 4)
        arrived(upper(far), k + 5)

    def ring_sent(own, lower, upper, k):
        for i, part in enumerate((lower, upper, upper, lower, lower, upper)):
            left_here(part(own), k + i)

    def first(n):
        return lambda ref: ref.at[pl.ds(0, n)]

    def second(n):
        return lambda ref: ref.at[pl.ds(n, n)]

    inward = [
        (hom.at[pl.ds(rj * 4, 4)], xin),
        (fscale_in, fscale),
        (pair_in, pair),
        (pgain_in, pgain),
        (bw_in, bw),
        (wq, wbuf.at[rj, pl.ds(0, 64)]),
        (wk, wbuf.at[rj, pl.ds(64, 64)]),
        (wv, wbuf.at[rj, pl.ds(128, 64)]),
        (wg, wbuf.at[rj, pl.ds(192, 64)]),
        (wo, wbuf.at[rj, pl.ds(256, 64)]),
        (resm_in, resm),
        (rows_in, rows),
        (rowv_in, rowv),
        (gb_in, gb),
        (cscale_in, cscale),
        (p1_in, p1),
        (p2_in, p2),
        (ow_in, ow),
    ]

    def local(k):
        return pltpu.make_async_copy(inward[k][0], inward[k][1], lsem.at[k])

    for k in range(len(inward)):
        local(k).start()

    barrier = pltpu.get_barrier_semaphore()

    def greet(dev):
        pl.semaphore_signal(barrier, inc=1, device_id=dev, device_id_type=pl.DeviceIdType.MESH)

    def greet_all(n):
        greet(in_zy(n))
        greet(in_zx(n))

    each(1, 16, greet_all)
    for dev in ({"ri": mate}, up, down):
        greet(dev)

    def greet_right(n):
        @pl.when(jnp.logical_not(to_self(n)))
        def _():
            greet(right_to(n))

        @pl.when(jnp.logical_not(from_self(n)))
        def _():
            greet(right_from(n))

    each(0, 16, greet_right)

    local(0).wait()
    local(1).wait()

    def norm_x(s, carry):
        xn[s, ri] = norm(xin[s].astype(F32), fscale[...]).astype(BF)
        return carry

    lax.fori_loop(0, 4, norm_x, 0)

    pl.semaphore_wait(barrier, 65 - 2 * diagonal.astype(jnp.int32))

    def send_x(s):
        rcopy(xn.at[s, ri, pl.ds(0, 64)], relay.at[0, s], RZ + s * 2, up).start()
        rcopy(xn.at[s, ri, pl.ds(64, 64)], relay.at[1, s], RZ + s * 2 + 1, down).start()
        rcopy(xn.at[s, ri], xn.at[s, ri], XM + s, {"ri": mate}).start()

    def relay_x(s):
        arrived(relay.at[0, s], RZ + s * 2)
        rcopy(relay.at[0, s], xn.at[s, ri_down, pl.ds(0, 64)], XZ + s * 2, up).start()
        arrived(relay.at[1, s], RZ + s * 2 + 1)
        rcopy(relay.at[1, s], xn.at[s, ri_up, pl.ds(64, 64)], XZ + s * 2 + 1, down).start()

    for s in range(4):
        send_x(s)
    for k in range(5, 10):
        local(k).wait()
    w_lower, w_upper = first(160), second(160)
    ring_start(wbuf.at[rj], w_lower, w_upper, WT, plus_y, minus_y)

    for k in range(2, 5):
        local(k).wait()
    pn[...] = norm(pair[...].astype(F32), pgain[...]).astype(BF).astype(F32)
    for j in range(8):
        tile = pn[pl.ds(j, 128, stride=8), :].astype(BF)
        bt[pl.ds(j, 8, stride=8), :] = nt(bw[...], tile)
    for half in range(2):
        bg[half, zl, x, rj] = bt[pl.ds(half * 32, 32), :].astype(BF)
    def send_bias(n):
        rcopy(bg.at[0, zl, x, rj], bg.at[0, zl, x, rj], BA + n, in_zy(n)).start()
        rcopy(bg.at[1, zl, x, rj], bg.at[1, zl, x, rj], BB + n, in_zx(n)).start()

    each(1, 16, send_bias)
    relay_x(0)
    relay_x(1)

    for k in range(10, len(inward)):
        local(k).wait()
    ring_pass(
        wbuf.at[behind(rj, 1)], wbuf.at[ahead(rj, 1)], w_lower, w_upper, WT, plus_y, minus_y
    )
    def came_bias(n):
        dz, d = lax.div(n, 4), lax.rem(n, 4)
        arrived(bg.at[0, behind(zl, dz), x, behind(rj, d)], BA + n)
        arrived(bg.at[1, behind(zl, dz), behind(x, d), rj], BB + n)

    each(1, 16, came_bias)
    b_lower, b_upper = first(2), second(2)
    ring_start(bg.at[0, :, x], b_lower, b_upper, AX, plus_x, minus_x)
    ring_start(bg.at[1, :, :, rj], b_lower, b_upper, BY, plus_y, minus_y)
    relay_x(2)

    row128 = lax.broadcasted_iota(jnp.int32, (128, 128), 0)
    col128 = lax.broadcasted_iota(jnp.int32, (128, 128), 1)
    ones = jnp.ones((128, 128), BF)
    for b in range(4):
        res = resm[pl.ds(b, 1), :].astype(F32)
        spread = jnp.where(row128 == col128, jnp.broadcast_to(res, (128, 128)), 0.0).astype(BF)
        cm[b] = mm(spread, ones)
    for b in range(2):
        gbt[pl.ds(b * 128, 128), :] = jnp.transpose(
            jnp.broadcast_to(gb[:, pl.ds(b * 128, 128)], (128, 128))
        )
    e128 = eye(128)
    for k in range(4):
        wst[pl.ds(k * 128, 128), :] = nt(e128, ow[pl.ds(k * 256, 256), :]).astype(BF)
    pick = (
        lax.broadcasted_iota(jnp.int32, (32, 128), 0)
        == lax.rem(lax.broadcasted_iota(jnp.int32, (32, 128), 1), 32)
    ).astype(F32).astype(BF)
    p1t = p1[...]
    p2r = jnp.concatenate([p2[...]] * 4, 0)
    total = jnp.maximum(jnp.sum(rowv[...].astype(F32)), 1.0)

    relay_x(3)

    ring_end(
        wbuf.at[behind(rj, 1)], wbuf.at[ahead(rj, 1)], wbuf.at[ahead(rj, 2)], w_lower, w_upper, WT
    )

    def weight(k):
        return wbuf[:, pl.ds(k * 64, 64), :].reshape(256, 256)

    wkn[...] = nt(eye(256), weight(1)).astype(BF)
    wqvg[0:256] = weight(0)
    wqvg[256:512] = weight(2)
    wqvg[512:768] = weight(3)

    def own_rows(s, carry):
        block = xn[s, ri]
        kb[s, ri] = mm(block, wkn[...]).astype(BF)
        three = nt(wqvg[...], block)
        qt[s] = (three[0:256] * 32 ** -0.5).astype(BF)
        vt[s, ri] = three[256:512].astype(BF)
        gate[s] = jax.nn.sigmoid(three[512:768] + gbt[...])
        return carry

    def other_rows(s, b):
        block = xn[s, b]
        kb[s, b] = mm(block, wkn[...]).astype(BF)
        vt[s, b] = nt(wqvg[256:512], block).astype(BF)

    lax.fori_loop(0, 4, own_rows, 0)
    ring_pass(
        bg.at[0, :, behind(x, 1)], bg.at[0, :, ahead(x, 1)], b_lower, b_upper, AX, plus_x, minus_x
    )
    ring_pass(
        bg.at[1, :, :, behind(rj, 1)], bg.at[1, :, :, ahead(rj, 1)], b_lower, b_upper,
        BY, plus_y, minus_y,
    )

    def near_rows(s, carry):
        arrived(xn.at[s, mate], XM + s)
        other_rows(s, mate)
        return carry

    def far_rows(s, carry):
        arrived(xn.at[s, opp, pl.ds(0, 64)], XZ + s * 2)
        arrived(xn.at[s, opp, pl.ds(64, 64)], XZ + s * 2 + 1)
        rcopy(xn.at[s, opp], xn.at[s, opp], XF + s, {"ri": mate}).start()
        other_rows(s, opp)
        return carry

    def last_rows(s, carry):
        arrived(xn.at[s, oppmate], XF + s)
        other_rows(s, oppmate)
        return carry

    lax.fori_loop(0, 4, near_rows, 0)
    lax.fori_loop(0, 4, far_rows, 0)
    lax.fori_loop(0, 4, last_rows, 0)
    ring_end(
        bg.at[0, :, behind(x, 1)], bg.at[0, :, ahead(x, 1)], bg.at[0, :, ahead(x, 2)],
        b_lower, b_upper, AX,
    )
    ring_end(
        bg.at[1, :, :, behind(rj, 1)], bg.at[1, :, :, ahead(rj, 1)], bg.at[1, :, :, ahead(rj, 2)],
        b_lower, b_upper, BY,
    )

    keymask = (jnp.concatenate([cm[b] for b in range(4)], 0) - 1.0) * 1e9
    for hp in range(4):
        two = bg[hp // 2, :, :, :, pl.ds(hp % 2 * 16, 16), :].astype(F32).reshape(64, 2, 8, 128)
        for h in range(2):
            biasb[hp, :, pl.ds(h * 128, 128)] = (two[:, h].reshape(512, 128) + keymask).astype(F32)

    lane8 = lax.div(lax.broadcasted_iota(jnp.int32, (8, 128), 1), 32)

    def attend(s, carry):
        key = kb[s].reshape(512, 256)
        value = jnp.concatenate([vt[s, b] for b in range(4)], 1)
        query = qt[s]
        parts = []
        for hp in range(4):
            g, r = hp // 2, hp % 2 * 2
            zero = jnp.zeros((32, 128), BF)
            pair_q = []
            for h in range(2):
                pieces = [zero] * 4
                pieces[r + h] = query[hp * 64 + h * 32 : hp * 64 + h * 32 + 32]
                pair_q.append(jnp.concatenate(pieces, 0))
            logits = mm(key[:, g * 128 : g * 128 + 128], jnp.concatenate(pair_q, 1)) + biasb[hp]
            low = logits - jnp.max(logits, 0, keepdims=True)
            probs = jnp.exp(low).astype(BF)
            summed = mm(
                jnp.concatenate([value[hp * 64 : hp * 64 + 64], jnp.ones((16, 512), BF)], 0), probs
            )
            scale = 1.0 / summed[64:65]
            parts.append(summed[0:32, 0:128] * scale[:, 0:128])
            parts.append(summed[32:64, 128:256] * scale[:, 128:256])
        attended = (jnp.concatenate(parts, 0) * gate[s]).astype(BF)
        attended = nt(e128, attended).astype(BF)
        result = (xin[s].astype(F32) + mm(attended, weight(4))).astype(BF)
        al[s] = result
        pltpu.make_async_copy(al.at[s], out_al.at[rj * 4 + s], osem.at[s]).start()

        @pl.when(s < 2)
        def _():
            start_out(s)

        on = norm(result.astype(F32), cscale[...])
        keep = cm[ri] * rows[seq * 16 + rj * 4 + s].astype(F32)
        on = (on * jnp.concatenate([keep, keep], 1)).astype(BF)
        left = nt(p1t, on)
        right[...] = nt(on, p2r)
        for y in range(4):
            ltile = jnp.zeros((8, 128), F32)
            rtile = jnp.zeros((8, 128), F32)
            for k in range(4):
                piece = left[k * 8 : k * 8 + 8]
                if k != y:
                    piece = pltpu.roll(piece, (32 * (k - y)) % 128, 1)
                ltile = jnp.where(lane8 == k, piece, ltile)
                rtile = jnp.where(lane8 == k, right[pl.ds(y * 32 + k, 8, stride=4), :], rtile)
            sndf[y, pl.ds(pl.multiple_of(s * 8, 8), 8), :] = ltile
            sndf[y, pl.ds(pl.multiple_of(32 + s * 8, 8), 8), :] = rtile
        return carry

    a_lower, a_upper = first(64), second(64)

    def out(s, source):
        return out_al.at[source * 4 + s]

    def start_out(s):
        for i, (part, dev) in enumerate(
            ((a_lower, plus_y), (a_upper, minus_y), (a_upper, plus_y), (a_lower, minus_y))
        ):
            rcopy(part(al.at[s]), part(out(s, rj)), AL + s * 6 + i, dev).start()

    def pass_out(s):
        ring_pass(
            out(s, behind(rj, 1)), out(s, ahead(rj, 1)), a_lower, a_upper, AL + s * 6,
            plus_y, minus_y,
        )

    lax.fori_loop(0, 4, attend, 0)

    snd[...] = sndf[...].astype(BF)

    def send_sides(n):
        rcopy(
            snd.at[ahead(rj, lax.rem(n, 4)), pl.ds(0, 32)], lraw.at[zl, rj], LL + n, in_zy(n)
        ).start()

    each(1, 16, send_sides)

    def right_copy(n):
        return rcopy(
            snd.at[lax.div(n, 4), pl.ds(32, 32)], rraw.at[zl, rj], RR + zl * 4 + rj, right_to(n),
            RR + n,
        )

    def send_right(n):
        @pl.when(jnp.logical_not(to_self(n)))
        def _():
            right_copy(n).start()

    each(0, 16, send_right)
    start_out(2)
    start_out(3)
    lraw[zl, rj] = snd[rj, 0:32]

    @pl.when(diagonal)
    def _():
        rraw[zl, rj] = snd[x, 32:64]

    def came_left(n):
        arrived(lraw.at[behind(zl, lax.div(n, 4)), behind(rj, lax.rem(n, 4))], LL + n)

    def came_right(n):
        @pl.when(jnp.logical_not(from_self(n)))
        def _():
            arrived(rraw.at[lax.div(n, 4), lax.rem(n, 4)], RR + n)

    def regroup(raw, buf, place):
        def step(t):
            block = raw[t].astype(F32)
            for y in range(4):
                for s in range(4):
                    scr[pl.ds(y * 4 + s, 8, stride=16), :] = block[y, s * 8 : s * 8 + 8]
            buf[:, place, t] = scr[...].astype(BF).reshape(8, 16, 128)

        each(0, 4, step)

    q_lower, q_upper = first(4), second(4)
    each(1, 16, came_left)
    regroup(lraw, lb, x)
    ring_start(lb.at[:, x], q_lower, q_upper, LX, plus_x, minus_x)
    each(0, 16, came_right)
    regroup(rraw, rb, rj)
    ring_start(rb.at[:, rj], q_lower, q_upper, R4, plus_y, minus_y)
    ring_pass(
        lb.at[:, behind(x, 1)], lb.at[:, ahead(x, 1)], q_lower, q_upper, LX, plus_x, minus_x
    )
    ring_pass(
        rb.at[:, behind(rj, 1)], rb.at[:, ahead(rj, 1)], q_lower, q_upper, R4, plus_y, minus_y
    )
    each(0, 4, pass_out)
    ring_end(
        lb.at[:, behind(x, 1)], lb.at[:, ahead(x, 1)], lb.at[:, ahead(x, 2)], q_lower, q_upper, LX
    )
    ring_end(
        rb.at[:, behind(rj, 1)], rb.at[:, ahead(rj, 1)], rb.at[:, ahead(rj, 2)],
        q_lower, q_upper, R4,
    )

    lane128 = lax.div(lax.broadcasted_iota(jnp.int32, (128, 128), 1), 32)

    def product(peer, u, carry):
        turned = nt(e128, rb[peer * 2 + u].reshape(256, 128)).astype(BF)
        for k in range(8):
            outer = mm(turned, lb[k].reshape(256, 128)).astype(BF)
            for j in range(4):
                bscr[j // 2, pl.ds(k * 32, 32), pl.ds((j % 2) * 128, 128)] = outer[
                    j * 32 : j * 32 + 32
                ]
        for jp in range(2):
            wide = mm(wst[...], bscr[jp])
            for half in range(2):
                c = half * 128
                mixed = wide[0:128, c : c + 128]
                for k in range(1, 4):
                    mixed = jnp.where(
                        lane128 == k, wide[k * 128 : k * 128 + 128, c : c + 128], mixed
                    )
                ub[peer, pl.ds(u * 4 + jp * 2 + half, 32, stride=8), :] = nt(
                    pick, mixed.astype(BF)
                )
        return carry

    def for_peer(d):
        peer = ahead(rj, d)
        lax.fori_loop(0, 2, lambda u, carry: product(peer, u, carry), 0)
        ubf[peer] = ub[peer].astype(BF)

        @pl.when(d < 4)
        def _():
            update_copy(d).start()

    def update_copy(d):
        peer = ahead(rj, d)
        return rcopy(ubf.at[peer], urecv.at[rj], UP + d - 1, {"rj": peer})

    each(1, 5, for_peer)
    urecv[rj] = ubf[rj]
    scale = 1.0 / total
    for d in (1, 2, 3):
        arrived(urecv.at[behind(rj, d)], UP + d - 1)
    out_pair[...] = (
        pair[...].astype(F32) + urecv[...].reshape(1024, 128).astype(F32) * scale
    ).astype(BF)

    def drain(s):
        pltpu.make_async_copy(al.at[s], out_al.at[rj * 4 + s], osem.at[s]).wait()
        for half in range(2):
            left_here(relay.at[half, s], RZ + s * 2 + half)
            left_here(relay.at[half, s], XZ + s * 2 + half)
        left_here(xn.at[s, ri], XM + s)
        left_here(xn.at[s, opp], XF + s)
        ring_end(
            out(s, behind(rj, 1)), out(s, ahead(rj, 1)), out(s, ahead(rj, 2)), a_lower, a_upper,
            AL + s * 6,
        )
        ring_sent(al.at[s], a_lower, a_upper, AL + s * 6)

    each(0, 4, drain)
    ring_sent(wbuf.at[rj], w_lower, w_upper, WT)
    ring_sent(bg.at[0, :, x], b_lower, b_upper, AX)
    ring_sent(bg.at[1, :, :, rj], b_lower, b_upper, BY)
    ring_sent(lb.at[:, x], q_lower, q_upper, LX)
    ring_sent(rb.at[:, rj], q_lower, q_upper, R4)

    def drain_small(n):
        left_here(bg.at[0, zl, x, rj], BA + n)
        left_here(bg.at[1, zl, x, rj], BB + n)
        left_here(lraw.at[zl, rj], LL + n)

    each(1, 16, drain_small)

    def drain_right(n):
        @pl.when(jnp.logical_not(to_self(n)))
        def _():
            left_here(rraw.at[zl, rj], RR + n)

    each(0, 16, drain_right)
    each(1, 4, lambda d: left_here(ubf.at[ahead(rj, d)], UP + d - 1))


def on_device(
    homolog_embedding,
    pairwise_state,
    residue_mask,
    alignment_row_mask,
    focus_layer_scale,
    asking_projector,
    lookup_projector,
    content_projector,
    sigmoid_projector,
    gate_offset_bias,
    final_projector,
    pairwise_norm_gain,
    bias_weight,
    cross_layer_scale,
    first_cross_projector,
    second_cross_projector,
    outer_weight,
):
    vmem = pl.BlockSpec(memory_space=pltpu.VMEM)
    hbm = pl.BlockSpec(memory_space=pl.ANY)
    alignment_output, pair_rows = pl.pallas_call(
        kernel,
        out_shape=(
            jax.ShapeDtypeStruct((16, 128, 256), BF),
            jax.ShapeDtypeStruct((1024, 128), BF),
        ),
        in_specs=[hbm] * 18,
        out_specs=(hbm, vmem),
        scratch_shapes=[
            pltpu.VMEM((4, 128, 256), BF),
            pltpu.VMEM((1024, 128), BF),
            pltpu.VMEM((4, 128), jnp.int32),
            pltpu.SMEM((256,), jnp.int32),
            pltpu.VMEM((2, 128), jnp.int32),
            pltpu.VMEM((1, 256), F32),
            pltpu.VMEM((1, 256), F32),
            pltpu.VMEM((1, 128), F32),
            pltpu.VMEM((8, 128), BF),
            pltpu.VMEM((1, 256), F32),
            pltpu.VMEM((32, 256), BF),
            pltpu.VMEM((32, 256), BF),
            pltpu.VMEM((1024, 128), BF),
            pltpu.VMEM((4, 4, 128, 256), BF),
            pltpu.VMEM((2, 4, 64, 256), BF),
            pltpu.VMEM((4, 320, 256), BF),
            pltpu.VMEM((1024, 128), F32),
            pltpu.VMEM((64, 128), F32),
            pltpu.VMEM((2, 4, 4, 4, 32, 128), BF),
            pltpu.VMEM((256, 256), BF),
            pltpu.VMEM((768, 256), BF),
            pltpu.VMEM((4, 4, 128, 256), BF),
            pltpu.VMEM((4, 256, 128), BF),
            pltpu.VMEM((4, 4, 256, 128), BF),
            pltpu.VMEM((4, 256, 128), F32),
            pltpu.VMEM((4, 512, 256), F32),
            pltpu.VMEM((256, 128), F32),
            pltpu.VMEM((4, 128, 128), F32),
            pltpu.VMEM((512, 256), BF),
            pltpu.VMEM((4, 128, 256), BF),
            pltpu.VMEM((128, 128), F32),
            pltpu.VMEM((4, 64, 128), F32),
            pltpu.VMEM((4, 64, 128), BF),
            pltpu.VMEM((4, 4, 32, 128), BF),
            pltpu.VMEM((4, 4, 32, 128), BF),
            pltpu.VMEM((128, 128), F32),
            pltpu.VMEM((8, 4, 4, 16, 128), BF),
            pltpu.VMEM((8, 4, 4, 16, 128), BF),
            pltpu.VMEM((2, 256, 256), BF),
            pltpu.VMEM((4, 256, 128), F32),
            pltpu.VMEM((4, 256, 128), BF),
            pltpu.VMEM((4, 256, 128), BF),
            pltpu.SemaphoreType.DMA((COUNT,)),
            pltpu.SemaphoreType.DMA((COUNT,)),
            pltpu.SemaphoreType.DMA((18,)),
            pltpu.SemaphoreType.DMA((4,)),
        ],
        compiler_params=pltpu.CompilerParams(
            collective_id=0, has_side_effects=True, vmem_limit_bytes=60 * 1024 * 1024
        ),
        cost_estimate=pl.CostEstimate(
            flops=4_000_000_000, bytes_accessed=4_000_000, transcendentals=2_000_000
        ),
    )(
        homolog_embedding,
        pairwise_state.reshape(1024, 128),
        residue_mask.reshape(4, 128),
        alignment_row_mask,
        alignment_row_mask.reshape(2, 128),
        focus_layer_scale.reshape(1, 256),
        asking_projector.T,
        lookup_projector.T,
        content_projector.T,
        sigmoid_projector.T,
        gate_offset_bias.reshape(1, 256),
        final_projector,
        pairwise_norm_gain.reshape(1, 128),
        bias_weight.T,
        cross_layer_scale.reshape(1, 256),
        first_cross_projector.T,
        second_cross_projector.T,
        outer_weight,
    )
    return alignment_output, pair_rows.reshape(128, 8, 128)


def solution(mesh):
    placed = (
        P("seq", "ri", None),
        P("ri", ("seq", "rj"), None),
        P(),
        P(),
        P(),
        P(None, "rj"),
        P(None, "rj"),
        P(None, "rj"),
        P(None, "rj"),
        P(),
        P("rj", None),
        P(),
        P(),
        P(),
        P(),
        P(),
        P(),
    )
    return jax.shard_map(
        on_device,
        mesh=mesh,
        in_specs=placed,
        out_specs=(P("seq", "ri", None), P("ri", ("seq", "rj"), None)),
        check_vma=False,
    )
```

```python
import jax
import jax.numpy as jnp
from jax import lax
from jax.experimental import pallas as pl
from jax.experimental.pallas import tpu as pltpu
from jax.sharding import PartitionSpec as P

F32 = jnp.float32
BF = jnp.bfloat16
NT = (((1,), (1,)), ((), ()))

SIZES = (8, 8, 4, 4, 6, 1, 1, 6, 6, 24, 1, 1, 6, 6, 3)
RZ, XZ, XM, XF, WT, BA, BB, AX, BY, AL, LL, RR, LX, R4, UP = (
    sum(SIZES[:i]) for i in range(len(SIZES))
)
COUNT = sum(SIZES)


def nt(a, b):
    return lax.dot_general(a, b, NT, preferred_element_type=F32)


def mm(a, b):
    return jnp.dot(a, b, preferred_element_type=F32)


def norm(values, gain):
    centre = values - jnp.mean(values, -1, keepdims=True)
    spread = jnp.mean(centre * centre, -1, keepdims=True)
    return centre * lax.rsqrt(spread + 1e-5) * gain


def eye(n):
    row = lax.broadcasted_iota(jnp.int32, (n, n), 0)
    col = lax.broadcasted_iota(jnp.int32, (n, n), 1)
    return (row == col).astype(F32).astype(BF)


def kernel(
    hom, pair_in, resm_in, rows_in, fscale_in, wq, wk, wv, wg, gb_in, wo, pgain_in, bw_in,
    cscale_in, p1_in, p2_in, ow_in,
    out_al, out_update,
    xin, pair, resm, rows, fscale, gb, pgain, bw, cscale, p1, p2, ow,
    xn, relay, wbuf, pn, bt, bg, wkn, wqvg, kb, qt, vt, gate, biasb, gbt, cm, wst, al, right, sndf, snd, lraw, rraw, scr, lb, rb,
    bscr, ub, ubf,
    ssem, rsem, lsem, osem, usem,
):
    seq = lax.axis_index("seq")
    ri = lax.axis_index("ri")
    rj = lax.axis_index("rj")
    zl, x = lax.div(seq, 4), lax.rem(seq, 4)
    mate = ri + 1 - 2 * lax.rem(ri, 2)
    opp = lax.rem(ri + 2, 4)
    oppmate = lax.rem(mate + 2, 4)

    def ahead(v, d):
        return lax.rem(v + d, 4)

    def behind(v, d):
        return lax.rem(v + 4 - d, 4)

    plus_y, minus_y = {"rj": ahead(rj, 1)}, {"rj": behind(rj, 1)}
    plus_x, minus_x = {"seq": zl * 4 + ahead(x, 1)}, {"seq": zl * 4 + behind(x, 1)}
    core, z = lax.rem(ri, 2), lax.div(ri, 2) * 4 + zl

    def along_z(step):
        to = lax.rem(z + step, 8)
        return lax.div(to, 4) * 2 + core, {
            "seq": lax.rem(to, 4) * 4 + x,
            "ri": lax.div(to, 4) * 2 + core,
        }

    ri_up, up = along_z(2)
    ri_down, down = along_z(6)

    def seq_of(zz, xx):
        return zz * 4 + xx

    def in_zy(n):
        return {"seq": seq_of(ahead(zl, lax.div(n, 4)), x), "rj": ahead(rj, lax.rem(n, 4))}

    def in_zx(n):
        return {"seq": seq_of(ahead(zl, lax.div(n, 4)), ahead(x, lax.rem(n, 4)))}

    def right_to(n):
        return {"seq": seq_of(ri, lax.div(n, 4)), "ri": lax.rem(n, 4), "rj": x}

    def right_from(n):
        return {"seq": seq_of(lax.div(n, 4), rj), "ri": zl, "rj": lax.rem(n, 4)}

    def each(low, high, body):
        def step(n, carry):
            body(n)
            return carry

        lax.fori_loop(low, high, step, 0)

    diagonal = jnp.logical_and(zl == ri, x == rj)

    def to_self(n):
        return jnp.logical_and(diagonal, n == seq_of(x, ri))

    def from_self(n):
        return jnp.logical_and(diagonal, n == seq_of(zl, rj))


    def rcopy(src, dst, k, dev, send=None):
        return pltpu.make_async_remote_copy(
            src_ref=src,
            dst_ref=dst,
            send_sem=ssem.at[k if send is None else send],
            recv_sem=rsem.at[k],
            device_id=dev,
            device_id_type=pl.DeviceIdType.MESH,
        )

    def arrived(ref, k):
        pltpu.make_async_copy(ref, ref, rsem.at[k]).wait()

    def left_here(ref, k):
        pltpu.make_async_copy(ref, ref, ssem.at[k]).wait()

    def ring_start(own, lower, upper, k, plus, minus):
        for i, (part, dev) in enumerate(
            ((lower, plus), (upper, minus), (upper, plus), (lower, minus))
        ):
            rcopy(part(own), part(own), k + i, dev).start()

    def ring_pass(before, after, lower, upper, k, plus, minus):
        arrived(lower(before), k)
        rcopy(lower(before), lower(before), k + 4, plus).start()
        arrived(upper(after), k + 1)
        rcopy(upper(after), upper(after), k + 5, minus).start()

    def ring_end(before, after, far, lower, upper, k):
        arrived(upper(before), k + 2)
        arrived(lower(after), k + 3)
        arrived(lower(far), k + 4)
        arrived(upper(far), k + 5)

    def ring_sent(own, lower, upper, k):
        for i, part in enumerate((lower, upper, upper, lower, lower, upper)):
            left_here(part(own), k + i)

    def first(n):
        return lambda ref: ref.at[pl.ds(0, n)]

    def second(n):
        return lambda ref: ref.at[pl.ds(n, n)]

    inward = [
        (hom.at[pl.ds(rj * 4, 4)], xin),
        (fscale_in, fscale),
        (pair_in, pair),
        (pgain_in, pgain),
        (bw_in, bw),
        (wq, wbuf.at[rj, pl.ds(0, 64)]),
        (wk, wbuf.at[rj, pl.ds(64, 64)]),
        (wv, wbuf.at[rj, pl.ds(128, 64)]),
        (wg, wbuf.at[rj, pl.ds(192, 64)]),
        (wo, wbuf.at[rj, pl.ds(256, 64)]),
        (resm_in, resm),
        (rows_in, rows),
        (gb_in, gb),
        (cscale_in, cscale),
        (p1_in, p1),
        (p2_in, p2),
        (ow_in, ow),
    ]

    def local(k):
        return pltpu.make_async_copy(inward[k][0], inward[k][1], lsem.at[k])

    for k in range(len(inward)):
        local(k).start()

    barrier = pltpu.get_barrier_semaphore()

    def greet(dev):
        pl.semaphore_signal(barrier, inc=1, device_id=dev, device_id_type=pl.DeviceIdType.MESH)

    def greet_all(n):
        greet(in_zy(n))
        greet(in_zx(n))

    each(1, 16, greet_all)
    for dev in ({"ri": mate}, up, down):
        greet(dev)

    def greet_right(n):
        @pl.when(jnp.logical_not(from_self(n)))
        def _():
            greet(right_from(n))

    each(0, 16, greet_right)

    local(0).wait()
    local(1).wait()

    def norm_x(s, carry):
        xn[s, ri] = norm(xin[s].astype(F32), fscale[...]).astype(BF)
        return carry

    lax.fori_loop(0, 4, norm_x, 0)

    pl.semaphore_wait(barrier, 49 - diagonal.astype(jnp.int32))

    def send_x(s):
        rcopy(xn.at[s, ri, pl.ds(0, 64)], relay.at[0, s], RZ + s * 2, up).start()
        rcopy(xn.at[s, ri, pl.ds(64, 64)], relay.at[1, s], RZ + s * 2 + 1, down).start()
        rcopy(xn.at[s, ri], xn.at[s, ri], XM + s, {"ri": mate}).start()

    def relay_x(s):
        arrived(relay.at[0, s], RZ + s * 2)
        rcopy(relay.at[0, s], xn.at[s, ri_down, pl.ds(0, 64)], XZ + s * 2, up).start()
        arrived(relay.at[1, s], RZ + s * 2 + 1)
        rcopy(relay.at[1, s], xn.at[s, ri_up, pl.ds(64, 64)], XZ + s * 2 + 1, down).start()

    for s in range(4):
        send_x(s)
    for k in range(5, 10):
        local(k).wait()
    w_lower, w_upper = first(160), second(160)
    ring_start(wbuf.at[rj], w_lower, w_upper, WT, plus_y, minus_y)

    for k in range(2, 5):
        local(k).wait()
    pn[...] = norm(pair[...].astype(F32), pgain[...]).astype(BF).astype(F32)
    for j in range(8):
        tile = pn[pl.ds(j, 128, stride=8), :].astype(BF)
        bt[pl.ds(j, 8, stride=8), :] = nt(bw[...], tile)
    for half in range(2):
        bg[half, zl, x, rj] = bt[pl.ds(half * 32, 32), :].astype(BF)
    def send_bias(n):
        rcopy(bg.at[0, zl, x, rj], bg.at[0, zl, x, rj], BA, in_zy(n)).start()
        rcopy(bg.at[1, zl, x, rj], bg.at[1, zl, x, rj], BB, in_zx(n)).start()

    each(1, 16, send_bias)
    relay_x(0)
    relay_x(1)

    for k in range(10, len(inward)):
        local(k).wait()
    ring_pass(
        wbuf.at[behind(rj, 1)], wbuf.at[ahead(rj, 1)], w_lower, w_upper, WT, plus_y, minus_y
    )
    fifteen, sixteen = bscr.at[0, pl.ds(0, 240)], bscr.at[0]
    arrived(fifteen, BA)
    arrived(fifteen, BB)
    b_lower, b_upper = first(2), second(2)
    ring_start(bg.at[0, :, x], b_lower, b_upper, AX, plus_x, minus_x)
    ring_start(bg.at[1, :, :, rj], b_lower, b_upper, BY, plus_y, minus_y)
    relay_x(2)

    row128 = lax.broadcasted_iota(jnp.int32, (128, 128), 0)
    col128 = lax.broadcasted_iota(jnp.int32, (128, 128), 1)
    ones = jnp.ones((128, 128), BF)
    for b in range(4):
        res = resm[pl.ds(b, 1), :].astype(F32)
        spread = jnp.where(row128 == col128, jnp.broadcast_to(res, (128, 128)), 0.0).astype(BF)
        cm[b] = mm(spread, ones)
    for b in range(2):
        gbt[pl.ds(b * 128, 128), :] = jnp.transpose(
            jnp.broadcast_to(gb[:, pl.ds(b * 128, 128)], (128, 128))
        )
    e128 = eye(128)
    for k in range(4):
        wst[pl.ds(k * 128, 128), :] = nt(e128, ow[pl.ds(k * 256, 256), :]).astype(BF)
    pick = (
        lax.broadcasted_iota(jnp.int32, (32, 128), 0)
        == lax.rem(lax.broadcasted_iota(jnp.int32, (32, 128), 1), 32)
    ).astype(F32).astype(BF)
    p1t = p1[...]
    p2r = jnp.concatenate([p2[...]] * 4, 0)

    relay_x(3)

    ring_end(
        wbuf.at[behind(rj, 1)], wbuf.at[ahead(rj, 1)], wbuf.at[ahead(rj, 2)], w_lower, w_upper, WT
    )

    def weight(k):
        return wbuf[:, pl.ds(k * 64, 64), :].reshape(256, 256)

    wkn[...] = nt(eye(256), weight(1)).astype(BF)
    wqvg[0:256] = weight(0)
    wqvg[256:512] = weight(2)
    wqvg[512:768] = weight(3)

    def own_rows(s, carry):
        block = xn[s, ri]
        kb[s, ri] = mm(block, wkn[...]).astype(BF)
        three = nt(wqvg[...], block)
        qt[s] = (three[0:256] * 32 ** -0.5).astype(BF)
        vt[s, ri] = three[256:512].astype(BF)
        gate[s] = jax.nn.sigmoid(three[512:768] + gbt[...])
        return carry

    def other_rows(s, b):
        block = xn[s, b]
        kb[s, b] = mm(block, wkn[...]).astype(BF)
        vt[s, b] = nt(wqvg[256:512], block).astype(BF)

    lax.fori_loop(0, 4, own_rows, 0)
    ring_pass(
        bg.at[0, :, behind(x, 1)], bg.at[0, :, ahead(x, 1)], b_lower, b_upper, AX, plus_x, minus_x
    )
    ring_pass(
        bg.at[1, :, :, behind(rj, 1)], bg.at[1, :, :, ahead(rj, 1)], b_lower, b_upper,
        BY, plus_y, minus_y,
    )

    def near_rows(s, carry):
        arrived(xn.at[s, mate], XM + s)
        other_rows(s, mate)
        return carry

    def far_rows(s, carry):
        arrived(xn.at[s, opp, pl.ds(0, 64)], XZ + s * 2)
        arrived(xn.at[s, opp, pl.ds(64, 64)], XZ + s * 2 + 1)
        rcopy(xn.at[s, opp], xn.at[s, opp], XF + s, {"ri": mate}).start()
        other_rows(s, opp)
        return carry

    def last_rows(s, carry):
        arrived(xn.at[s, oppmate], XF + s)
        other_rows(s, oppmate)
        return carry

    lax.fori_loop(0, 4, near_rows, 0)
    lax.fori_loop(0, 2, far_rows, 0)
    ring_end(
        bg.at[0, :, behind(x, 1)], bg.at[0, :, ahead(x, 1)], bg.at[0, :, ahead(x, 2)],
        b_lower, b_upper, AX,
    )
    ring_end(
        bg.at[1, :, :, behind(rj, 1)], bg.at[1, :, :, ahead(rj, 1)], bg.at[1, :, :, ahead(rj, 2)],
        b_lower, b_upper, BY,
    )

    keymask = (jnp.concatenate([cm[b] for b in range(4)], 0) - 1.0) * 1e9
    for hp in range(4):
        two = bg[hp // 2, :, :, :, pl.ds(hp % 2 * 16, 16), :].astype(F32).reshape(64, 2, 8, 128)
        for h in range(2):
            biasb[hp, :, pl.ds(h * 128, 128)] = (two[:, h].reshape(512, 128) + keymask).astype(F32)

    lane8 = lax.div(lax.broadcasted_iota(jnp.int32, (8, 128), 1), 32)

    def attend(s, carry):
        last_rows(s, carry)
        key = kb[s].reshape(512, 256)
        value = jnp.concatenate([vt[s, b] for b in range(4)], 1)
        query = qt[s]
        parts = []
        for hp in range(4):
            g, r = hp // 2, hp % 2 * 2
            zero = jnp.zeros((32, 128), BF)
            pair_q = []
            for h in range(2):
                pieces = [zero] * 4
                pieces[r + h] = query[hp * 64 + h * 32 : hp * 64 + h * 32 + 32]
                pair_q.append(jnp.concatenate(pieces, 0))
            logits = mm(key[:, g * 128 : g * 128 + 128], jnp.concatenate(pair_q, 1)) + biasb[hp]
            low = logits - jnp.max(logits, 0, keepdims=True)
            probs = jnp.exp(low).astype(BF)
            summed = mm(
                jnp.concatenate([value[hp * 64 : hp * 64 + 64], jnp.ones((16, 512), BF)], 0), probs
            )
            scale = 1.0 / summed[64:65]
            parts.append(summed[0:32, 0:128] * scale[:, 0:128])
            parts.append(summed[32:64, 128:256] * scale[:, 128:256])
        attended = (jnp.concatenate(parts, 0) * gate[s]).astype(BF)
        attended = nt(e128, attended).astype(BF)
        result = (xin[s].astype(F32) + mm(attended, weight(4))).astype(BF)
        al[s] = result
        pltpu.make_async_copy(al.at[s], out_al.at[rj * 4 + s], osem.at[s]).start()

        @pl.when(s < 3)
        def _():
            start_out(s)

        on = norm(result.astype(F32), cscale[...])
        keep = cm[ri] * rows[seq * 16 + rj * 4 + s].astype(F32)
        on = (on * jnp.concatenate([keep, keep], 1)).astype(BF)
        left = nt(p1t, on)
        right[...] = nt(on, p2r)
        for y in range(4):
            ltile = jnp.zeros((8, 128), F32)
            rtile = jnp.zeros((8, 128), F32)
            for k in range(4):
                piece = left[k * 8 : k * 8 + 8]
                if k != y:
                    piece = pltpu.roll(piece, (32 * (k - y)) % 128, 1)
                ltile = jnp.where(lane8 == k, piece, ltile)
                rtile = jnp.where(lane8 == k, right[pl.ds(y * 32 + k, 8, stride=4), :], rtile)
            sndf[y, pl.ds(pl.multiple_of(s * 8, 8), 8), :] = ltile
            sndf[y, pl.ds(pl.multiple_of(32 + s * 8, 8), 8), :] = rtile

        @pl.when(s < 2)
        def _():
            far_rows(s + 2, carry)

        return carry

    a_lower, a_upper = first(64), second(64)

    def out(s, source):
        return out_al.at[source * 4 + s]

    def start_out(s):
        for i, (part, dev) in enumerate(
            ((a_lower, plus_y), (a_upper, minus_y), (a_upper, plus_y), (a_lower, minus_y))
        ):
            rcopy(part(al.at[s]), part(out(s, rj)), AL + s * 6 + i, dev).start()

    def pass_out(s):
        ring_pass(
            out(s, behind(rj, 1)), out(s, ahead(rj, 1)), a_lower, a_upper, AL + s * 6,
            plus_y, minus_y,
        )

    lax.fori_loop(0, 4, attend, 0)

    snd[...] = sndf[...].astype(BF)

    def send_sides(n):
        rcopy(
            snd.at[ahead(rj, lax.rem(n, 4)), pl.ds(0, 32)], lraw.at[zl, rj], LL, in_zy(n)
        ).start()

    each(1, 16, send_sides)

    def send_right(n):
        @pl.when(jnp.logical_not(to_self(n)))
        def _():
            rcopy(
                snd.at[lax.div(n, 4), pl.ds(32, 32)], rraw.at[zl, rj], RR, right_to(n)
            ).start()

    each(0, 16, send_right)
    each(0, 2, pass_out)
    start_out(3)
    lraw[zl, rj] = snd[rj, 0:32]

    @pl.when(diagonal)
    def _():
        rraw[zl, rj] = snd[x, 32:64]

    def drain_head(s):
        for half in range(2):
            left_here(relay.at[half, s], RZ + s * 2 + half)
            left_here(relay.at[half, s], XZ + s * 2 + half)
        left_here(xn.at[s, ri], XM + s)
        left_here(xn.at[s, opp], XF + s)

    each(0, 4, drain_head)
    left_here(fifteen, BA)
    left_here(fifteen, BB)
    ring_sent(wbuf.at[rj], w_lower, w_upper, WT)
    ring_sent(bg.at[0, :, x], b_lower, b_upper, AX)
    ring_sent(bg.at[1, :, :, rj], b_lower, b_upper, BY)

    def regroup(raw, buf, place):
        def step(t):
            block = raw[t].astype(F32)
            for y in range(4):
                for s in range(4):
                    scr[pl.ds(y * 4 + s, 8, stride=16), :] = block[y, s * 8 : s * 8 + 8]
            buf[:, place, t] = scr[...].astype(BF).reshape(8, 16, 128)

        each(0, 4, step)

    q_lower, q_upper = first(4), second(4)
    arrived(fifteen, LL)
    regroup(lraw, lb, x)
    ring_start(lb.at[:, x], q_lower, q_upper, LX, plus_x, minus_x)

    @pl.when(diagonal)
    def _():
        arrived(fifteen, RR)

    @pl.when(jnp.logical_not(diagonal))
    def _():
        arrived(sixteen, RR)

    regroup(rraw, rb, rj)
    ring_start(rb.at[:, rj], q_lower, q_upper, R4, plus_y, minus_y)
    ring_pass(
        lb.at[:, behind(x, 1)], lb.at[:, ahead(x, 1)], q_lower, q_upper, LX, plus_x, minus_x
    )
    ring_pass(
        rb.at[:, behind(rj, 1)], rb.at[:, ahead(rj, 1)], q_lower, q_upper, R4, plus_y, minus_y
    )
    each(2, 4, pass_out)
    ring_end(
        lb.at[:, behind(x, 1)], lb.at[:, ahead(x, 1)], lb.at[:, ahead(x, 2)], q_lower, q_upper, LX
    )
    ring_end(
        rb.at[:, behind(rj, 1)], rb.at[:, ahead(rj, 1)], rb.at[:, ahead(rj, 2)],
        q_lower, q_upper, R4,
    )

    lane128 = lax.div(lax.broadcasted_iota(jnp.int32, (128, 128), 1), 32)

    def product(peer, u, carry):
        turned = nt(e128, rb[peer * 2 + u].reshape(256, 128)).astype(BF)
        for k in range(8):
            outer = mm(turned, lb[k].reshape(256, 128)).astype(BF)
            for j in range(4):
                bscr[j // 2, pl.ds(k * 32, 32), pl.ds((j % 2) * 128, 128)] = outer[
                    j * 32 : j * 32 + 32
                ]
        for jp in range(2):
            wide = mm(wst[...], bscr[jp])
            for half in range(2):
                c = half * 128
                mixed = wide[0:128, c : c + 128]
                for k in range(1, 4):
                    mixed = jnp.where(
                        lane128 == k, wide[k * 128 : k * 128 + 128, c : c + 128], mixed
                    )
                ub[peer, pl.ds(u * 4 + jp * 2 + half, 32, stride=8), :] = nt(
                    pick, mixed.astype(BF)
                )
        return carry

    def in_order(t):
        return jnp.where(t == 0, 2, jnp.where(t == 1, 1, t + 1))

    def for_peer(t):
        d = in_order(t)
        peer = ahead(rj, d)
        lax.fori_loop(0, 2, lambda u, carry: product(peer, u, carry), 0)
        ubf[peer] = ub[peer].astype(BF)

        @pl.when(t < 3)
        def _():
            update_copy(d).start()

    def update_copy(d):
        peer = ahead(rj, d)
        return rcopy(ubf.at[peer], out_update.at[rj], UP + d - 1, {"rj": peer})

    each(0, 4, for_peer)
    keep_own = pltpu.make_async_copy(ubf.at[rj], out_update.at[rj], usem)
    keep_own.start()
    each(1, 4, lambda d: arrived(out_update.at[behind(rj, d)], UP + d - 1))

    def drain(s):
        pltpu.make_async_copy(al.at[s], out_al.at[rj * 4 + s], osem.at[s]).wait()
        ring_end(
            out(s, behind(rj, 1)), out(s, ahead(rj, 1)), out(s, ahead(rj, 2)), a_lower, a_upper,
            AL + s * 6,
        )
        ring_sent(al.at[s], a_lower, a_upper, AL + s * 6)

    each(0, 4, drain)
    ring_sent(lb.at[:, x], q_lower, q_upper, LX)
    ring_sent(rb.at[:, rj], q_lower, q_upper, R4)
    left_here(fifteen, LL)

    @pl.when(diagonal)
    def _():
        left_here(fifteen, RR)

    @pl.when(jnp.logical_not(diagonal))
    def _():
        left_here(sixteen, RR)

    each(1, 4, lambda d: left_here(ubf.at[ahead(rj, d)], UP + d - 1))
    keep_own.wait()


def finish(al_in, update_in, pair_in, rowv_in, al_out, pair_out, update, pair, rowv, result, sem):
    whole = pltpu.make_async_copy(al_in, al_out, sem.at[0])
    whole.start()
    parts = [
        pltpu.make_async_copy(update_in, update, sem.at[1]),
        pltpu.make_async_copy(pair_in, pair, sem.at[2]),
        pltpu.make_async_copy(rowv_in, rowv, sem.at[3]),
    ]
    for part in parts:
        part.start()
    for part in parts:
        part.wait()
    scale = 1.0 / jnp.maximum(jnp.sum(rowv[...].astype(F32)), 1.0)
    result[...] = (
        pair[...].astype(F32) + update[...].reshape(1024, 128).astype(F32) * scale
    ).astype(BF)
    back = pltpu.make_async_copy(result, pair_out, sem.at[4])
    back.start()
    back.wait()
    whole.wait()


def on_device(
    homolog_embedding,
    pairwise_state,
    residue_mask,
    alignment_row_mask,
    focus_layer_scale,
    asking_projector,
    lookup_projector,
    content_projector,
    sigmoid_projector,
    gate_offset_bias,
    final_projector,
    pairwise_norm_gain,
    bias_weight,
    cross_layer_scale,
    first_cross_projector,
    second_cross_projector,
    outer_weight,
):
    hbm = pl.BlockSpec(memory_space=pl.ANY)
    gathered, update = pl.pallas_call(
        kernel,
        out_shape=(
            jax.ShapeDtypeStruct((16, 128, 256), BF),
            jax.ShapeDtypeStruct((4, 256, 128), BF),
        ),
        in_specs=[hbm] * 17,
        out_specs=(hbm, hbm),
        scratch_shapes=[
            pltpu.VMEM((4, 128, 256), BF),
            pltpu.VMEM((1024, 128), BF),
            pltpu.VMEM((4, 128), jnp.int32),
            pltpu.SMEM((256,), jnp.int32),
            pltpu.VMEM((1, 256), F32),
            pltpu.VMEM((1, 256), F32),
            pltpu.VMEM((1, 128), F32),
            pltpu.VMEM((8, 128), BF),
            pltpu.VMEM((1, 256), F32),
            pltpu.VMEM((32, 256), BF),
            pltpu.VMEM((32, 256), BF),
            pltpu.VMEM((1024, 128), BF),
            pltpu.VMEM((4, 4, 128, 256), BF),
            pltpu.VMEM((2, 4, 64, 256), BF),
            pltpu.VMEM((4, 320, 256), BF),
            pltpu.VMEM((1024, 128), F32),
            pltpu.VMEM((64, 128), F32),
            pltpu.VMEM((2, 4, 4, 4, 32, 128), BF),
            pltpu.VMEM((256, 256), BF),
            pltpu.VMEM((768, 256), BF),
            pltpu.VMEM((4, 4, 128, 256), BF),
            pltpu.VMEM((4, 256, 128), BF),
            pltpu.VMEM((4, 4, 256, 128), BF),
            pltpu.VMEM((4, 256, 128), F32),
            pltpu.VMEM((4, 512, 256), F32),
            pltpu.VMEM((256, 128), F32),
            pltpu.VMEM((4, 128, 128), F32),
            pltpu.VMEM((512, 256), BF),
            pltpu.VMEM((4, 128, 256), BF),
            pltpu.VMEM((128, 128), F32),
            pltpu.VMEM((4, 64, 128), F32),
            pltpu.VMEM((4, 64, 128), BF),
            pltpu.VMEM((4, 4, 32, 128), BF),
            pltpu.VMEM((4, 4, 32, 128), BF),
            pltpu.VMEM((128, 128), F32),
            pltpu.VMEM((8, 4, 4, 16, 128), BF),
            pltpu.VMEM((8, 4, 4, 16, 128), BF),
            pltpu.VMEM((2, 256, 256), BF),
            pltpu.VMEM((4, 256, 128), F32),
            pltpu.VMEM((4, 256, 128), BF),
            pltpu.SemaphoreType.DMA((COUNT,)),
            pltpu.SemaphoreType.DMA((COUNT,)),
            pltpu.SemaphoreType.DMA((17,)),
            pltpu.SemaphoreType.DMA((4,)),
            pltpu.SemaphoreType.DMA,
        ],
        compiler_params=pltpu.CompilerParams(
            collective_id=0, has_side_effects=True, vmem_limit_bytes=60 * 1024 * 1024
        ),
        cost_estimate=pl.CostEstimate(
            flops=4_000_000_000, bytes_accessed=4_000_000, transcendentals=2_000_000
        ),
    )(
        homolog_embedding,
        pairwise_state.reshape(1024, 128),
        residue_mask.reshape(4, 128),
        alignment_row_mask,
        focus_layer_scale.reshape(1, 256),
        asking_projector.T,
        lookup_projector.T,
        content_projector.T,
        sigmoid_projector.T,
        gate_offset_bias.reshape(1, 256),
        final_projector,
        pairwise_norm_gain.reshape(1, 128),
        bias_weight.T,
        cross_layer_scale.reshape(1, 256),
        first_cross_projector.T,
        second_cross_projector.T,
        outer_weight,
    )
    alignment_output, pair_rows = pl.pallas_call(
        finish,
        out_shape=(
            jax.ShapeDtypeStruct((16, 128, 256), BF),
            jax.ShapeDtypeStruct((1024, 128), BF),
        ),
        in_specs=[hbm] * 4,
        out_specs=(hbm, hbm),
        scratch_shapes=[
            pltpu.VMEM((4, 256, 128), BF),
            pltpu.VMEM((1024, 128), BF),
            pltpu.VMEM((2, 128), jnp.int32),
            pltpu.VMEM((1024, 128), BF),
            pltpu.SemaphoreType.DMA((5,)),
        ],
        compiler_params=pltpu.CompilerParams(vmem_limit_bytes=60 * 1024 * 1024),
    )(gathered, update, pairwise_state.reshape(1024, 128), alignment_row_mask.reshape(2, 128))
    return alignment_output, pair_rows.reshape(128, 8, 128)


def solution(mesh):
    placed = (
        P("seq", "ri", None),
        P("ri", ("seq", "rj"), None),
        P(),
        P(),
        P(),
        P(None, "rj"),
        P(None, "rj"),
        P(None, "rj"),
        P(None, "rj"),
        P(),
        P("rj", None),
        P(),
        P(),
        P(),
        P(),
        P(),
        P(),
    )
    return jax.shard_map(
        on_device,
        mesh=mesh,
        in_specs=placed,
        out_specs=(P("seq", "ri", None), P("ri", ("seq", "rj"), None)),
        check_vma=False,
    )
```

```python
import jax
import jax.numpy as jnp
from jax import lax
from jax.experimental import pallas as pl
from jax.experimental.pallas import tpu as pltpu
from jax.sharding import PartitionSpec as P

F32 = jnp.float32
BF = jnp.bfloat16
NT = (((1,), (1,)), ((), ()))

SIZES = (8, 8, 4, 4, 6, 1, 1, 6, 6, 24, 1, 1, 6, 6, 3)
RZ, XZ, XM, XF, WT, BA, BB, AX, BY, AL, LL, RR, LX, R4, UP = (
    sum(SIZES[:i]) for i in range(len(SIZES))
)
COUNT = sum(SIZES)


def nt(a, b):
    return lax.dot_general(a, b, NT, preferred_element_type=F32)


def mm(a, b):
    return jnp.dot(a, b, preferred_element_type=F32)


def norm(values, gain):
    centre = values - jnp.mean(values, -1, keepdims=True)
    spread = jnp.mean(centre * centre, -1, keepdims=True)
    return centre * lax.rsqrt(spread + 1e-5) * gain


def eye(n):
    row = lax.broadcasted_iota(jnp.int32, (n, n), 0)
    col = lax.broadcasted_iota(jnp.int32, (n, n), 1)
    return (row == col).astype(F32).astype(BF)


def kernel(
    hom, pair_in, resm_in, rows_in, fscale_in, wq, wk, wv, wg, gb_in, wo, pgain_in, bw_in,
    cscale_in, p1_in, p2_in, ow_in,
    out_al, out_update,
    xin, pair, resm, rows, fscale, gb, pgain, bw, cscale, p1, p2, ow,
    xn, relay, wbuf, pn, bt, bg, wkn, wqvg, kb, qt, vt, gate, biasb, gbt, cm, wst, al, right, sndf, snd, lraw, rraw, scr, lb, rb,
    bscr, ub, ubf, ugot,
    ssem, rsem, lsem, osem, usem,
):
    seq = lax.axis_index("seq")
    ri = lax.axis_index("ri")
    rj = lax.axis_index("rj")
    zl, x = lax.div(seq, 4), lax.rem(seq, 4)
    mate = ri + 1 - 2 * lax.rem(ri, 2)
    opp = lax.rem(ri + 2, 4)
    oppmate = lax.rem(mate + 2, 4)

    def ahead(v, d):
        return lax.rem(v + d, 4)

    def behind(v, d):
        return lax.rem(v + 4 - d, 4)

    plus_y, minus_y = {"rj": ahead(rj, 1)}, {"rj": behind(rj, 1)}
    plus_x, minus_x = {"seq": zl * 4 + ahead(x, 1)}, {"seq": zl * 4 + behind(x, 1)}
    core, z = lax.rem(ri, 2), lax.div(ri, 2) * 4 + zl

    def along_z(step):
        to = lax.rem(z + step, 8)
        return lax.div(to, 4) * 2 + core, {
            "seq": lax.rem(to, 4) * 4 + x,
            "ri": lax.div(to, 4) * 2 + core,
        }

    ri_up, up = along_z(2)
    ri_down, down = along_z(6)

    def seq_of(zz, xx):
        return zz * 4 + xx

    def in_zy(n):
        return {"seq": seq_of(ahead(zl, lax.div(n, 4)), x), "rj": ahead(rj, lax.rem(n, 4))}

    def in_zx(n):
        return {"seq": seq_of(ahead(zl, lax.div(n, 4)), ahead(x, lax.rem(n, 4)))}

    def right_to(n):
        return {"seq": seq_of(ri, lax.div(n, 4)), "ri": lax.rem(n, 4), "rj": x}

    def right_from(n):
        return {"seq": seq_of(lax.div(n, 4), rj), "ri": zl, "rj": lax.rem(n, 4)}

    def each(low, high, body):
        def step(n, carry):
            body(n)
            return carry

        lax.fori_loop(low, high, step, 0)

    diagonal = jnp.logical_and(zl == ri, x == rj)

    def to_self(n):
        return jnp.logical_and(diagonal, n == seq_of(x, ri))

    def from_self(n):
        return jnp.logical_and(diagonal, n == seq_of(zl, rj))


    def rcopy(src, dst, k, dev, send=None):
        return pltpu.make_async_remote_copy(
            src_ref=src,
            dst_ref=dst,
            send_sem=ssem.at[k if send is None else send],
            recv_sem=rsem.at[k],
            device_id=dev,
            device_id_type=pl.DeviceIdType.MESH,
        )

    def arrived(ref, k):
        pltpu.make_async_copy(ref, ref, rsem.at[k]).wait()

    def left_here(ref, k):
        pltpu.make_async_copy(ref, ref, ssem.at[k]).wait()

    def ring_start(own, lower, upper, k, plus, minus):
        for i, (part, dev) in enumerate(
            ((lower, plus), (upper, minus), (upper, plus), (lower, minus))
        ):
            rcopy(part(own), part(own), k + i, dev).start()

    def ring_pass(before, after, lower, upper, k, plus, minus):
        arrived(lower(before), k)
        rcopy(lower(before), lower(before), k + 4, plus).start()
        arrived(upper(after), k + 1)
        rcopy(upper(after), upper(after), k + 5, minus).start()

    def ring_end(before, after, far, lower, upper, k):
        arrived(upper(before), k + 2)
        arrived(lower(after), k + 3)
        arrived(lower(far), k + 4)
        arrived(upper(far), k + 5)

    def ring_sent(own, lower, upper, k):
        for i, part in enumerate((lower, upper, upper, lower, lower, upper)):
            left_here(part(own), k + i)

    def first(n):
        return lambda ref: ref.at[pl.ds(0, n)]

    def second(n):
        return lambda ref: ref.at[pl.ds(n, n)]

    inward = [
        (hom.at[pl.ds(rj * 4, 4)], xin),
        (fscale_in, fscale),
        (pair_in, pair),
        (pgain_in, pgain),
        (bw_in, bw),
        (wq, wbuf.at[rj, pl.ds(0, 64)]),
        (wk, wbuf.at[rj, pl.ds(64, 64)]),
        (wv, wbuf.at[rj, pl.ds(128, 64)]),
        (wg, wbuf.at[rj, pl.ds(192, 64)]),
        (wo, wbuf.at[rj, pl.ds(256, 64)]),
        (resm_in, resm),
        (rows_in, rows),
        (gb_in, gb),
        (cscale_in, cscale),
        (p1_in, p1),
        (p2_in, p2),
        (ow_in, ow),
    ]

    def local(k):
        return pltpu.make_async_copy(inward[k][0], inward[k][1], lsem.at[k])

    for k in range(len(inward)):
        local(k).start()

    barrier = pltpu.get_barrier_semaphore()

    def greet(dev):
        pl.semaphore_signal(barrier, inc=1, device_id=dev, device_id_type=pl.DeviceIdType.MESH)

    def greet_all(n):
        greet(in_zy(n))
        greet(in_zx(n))

    each(1, 16, greet_all)
    for dev in ({"ri": mate}, up, down):
        greet(dev)

    def greet_right(n):
        @pl.when(jnp.logical_not(from_self(n)))
        def _():
            greet(right_from(n))

    each(0, 16, greet_right)

    local(0).wait()
    local(1).wait()

    def norm_x(s, carry):
        xn[s, ri] = norm(xin[s].astype(F32), fscale[...]).astype(BF)
        return carry

    lax.fori_loop(0, 4, norm_x, 0)

    pl.semaphore_wait(barrier, 49 - diagonal.astype(jnp.int32))

    def send_x(s):
        rcopy(xn.at[s, ri, pl.ds(0, 64)], relay.at[0, s], RZ + s * 2, up).start()
        rcopy(xn.at[s, ri, pl.ds(64, 64)], relay.at[1, s], RZ + s * 2 + 1, down).start()
        rcopy(xn.at[s, ri], xn.at[s, ri], XM + s, {"ri": mate}).start()

    def relay_x(s):
        arrived(relay.at[0, s], RZ + s * 2)
        rcopy(relay.at[0, s], xn.at[s, ri_down, pl.ds(0, 64)], XZ + s * 2, up).start()
        arrived(relay.at[1, s], RZ + s * 2 + 1)
        rcopy(relay.at[1, s], xn.at[s, ri_up, pl.ds(64, 64)], XZ + s * 2 + 1, down).start()

    for s in range(4):
        send_x(s)
    for k in range(5, 10):
        local(k).wait()
    w_lower, w_upper = first(160), second(160)
    ring_start(wbuf.at[rj], w_lower, w_upper, WT, plus_y, minus_y)

    for k in range(2, 5):
        local(k).wait()
    pn[...] = norm(pair[...].astype(F32), pgain[...]).astype(BF).astype(F32)
    for j in range(8):
        tile = pn[pl.ds(j, 128, stride=8), :].astype(BF)
        bt[pl.ds(j, 8, stride=8), :] = nt(bw[...], tile)
    for half in range(2):
        bg[half, zl, x, rj] = bt[pl.ds(half * 32, 32), :].astype(BF)
    def send_bias(n):
        rcopy(bg.at[0, zl, x, rj], bg.at[0, zl, x, rj], BA, in_zy(n)).start()
        rcopy(bg.at[1, zl, x, rj], bg.at[1, zl, x, rj], BB, in_zx(n)).start()

    each(1, 16, send_bias)
    relay_x(0)
    relay_x(1)

    for k in range(10, len(inward)):
        local(k).wait()
    ring_pass(
        wbuf.at[behind(rj, 1)], wbuf.at[ahead(rj, 1)], w_lower, w_upper, WT, plus_y, minus_y
    )
    fifteen, sixteen = bscr.at[0, pl.ds(0, 240)], bscr.at[0]
    arrived(fifteen, BA)
    arrived(fifteen, BB)
    b_lower, b_upper = first(2), second(2)
    ring_start(bg.at[0, :, x], b_lower, b_upper, AX, plus_x, minus_x)
    ring_start(bg.at[1, :, :, rj], b_lower, b_upper, BY, plus_y, minus_y)
    relay_x(2)

    row128 = lax.broadcasted_iota(jnp.int32, (128, 128), 0)
    col128 = lax.broadcasted_iota(jnp.int32, (128, 128), 1)
    ones = jnp.ones((128, 128), BF)
    for b in range(4):
        res = resm[pl.ds(b, 1), :].astype(F32)
        spread = jnp.where(row128 == col128, jnp.broadcast_to(res, (128, 128)), 0.0).astype(BF)
        cm[b] = mm(spread, ones)
    for b in range(2):
        gbt[pl.ds(b * 128, 128), :] = jnp.transpose(
            jnp.broadcast_to(gb[:, pl.ds(b * 128, 128)], (128, 128))
        )
    e128 = eye(128)
    for k in range(4):
        wst[pl.ds(k * 128, 128), :] = nt(e128, ow[pl.ds(k * 256, 256), :]).astype(BF)
    pick = (
        lax.broadcasted_iota(jnp.int32, (32, 128), 0)
        == lax.rem(lax.broadcasted_iota(jnp.int32, (32, 128), 1), 32)
    ).astype(F32).astype(BF)
    p1t = p1[...]
    p2r = jnp.concatenate([p2[...]] * 4, 0)

    relay_x(3)

    ring_end(
        wbuf.at[behind(rj, 1)], wbuf.at[ahead(rj, 1)], wbuf.at[ahead(rj, 2)], w_lower, w_upper, WT
    )

    def weight(k):
        return wbuf[:, pl.ds(k * 64, 64), :].reshape(256, 256)

    wkn[...] = nt(eye(256), weight(1)).astype(BF)
    wqvg[0:256] = weight(0)
    wqvg[256:512] = weight(2)
    wqvg[512:768] = weight(3)

    def own_rows(s, carry):
        block = xn[s, ri]
        kb[s, ri] = mm(block, wkn[...]).astype(BF)
        three = nt(wqvg[...], block)
        qt[s] = (three[0:256] * 32 ** -0.5).astype(BF)
        vt[s, ri] = three[256:512].astype(BF)
        gate[s] = jax.nn.sigmoid(three[512:768] + gbt[...])
        return carry

    def other_rows(s, b):
        block = xn[s, b]
        kb[s, b] = mm(block, wkn[...]).astype(BF)
        vt[s, b] = nt(wqvg[256:512], block).astype(BF)

    lax.fori_loop(0, 4, own_rows, 0)
    ring_pass(
        bg.at[0, :, behind(x, 1)], bg.at[0, :, ahead(x, 1)], b_lower, b_upper, AX, plus_x, minus_x
    )
    ring_pass(
        bg.at[1, :, :, behind(rj, 1)], bg.at[1, :, :, ahead(rj, 1)], b_lower, b_upper,
        BY, plus_y, minus_y,
    )

    def near_rows(s, carry):
        arrived(xn.at[s, mate], XM + s)
        other_rows(s, mate)
        return carry

    def far_rows(s, carry):
        arrived(xn.at[s, opp, pl.ds(0, 64)], XZ + s * 2)
        arrived(xn.at[s, opp, pl.ds(64, 64)], XZ + s * 2 + 1)
        rcopy(xn.at[s, opp], xn.at[s, opp], XF + s, {"ri": mate}).start()
        other_rows(s, opp)
        return carry

    def last_rows(s, carry):
        arrived(xn.at[s, oppmate], XF + s)
        other_rows(s, oppmate)
        return carry

    lax.fori_loop(0, 4, near_rows, 0)
    lax.fori_loop(0, 2, far_rows, 0)
    ring_end(
        bg.at[0, :, behind(x, 1)], bg.at[0, :, ahead(x, 1)], bg.at[0, :, ahead(x, 2)],
        b_lower, b_upper, AX,
    )
    ring_end(
        bg.at[1, :, :, behind(rj, 1)], bg.at[1, :, :, ahead(rj, 1)], bg.at[1, :, :, ahead(rj, 2)],
        b_lower, b_upper, BY,
    )

    keymask = (jnp.concatenate([cm[b] for b in range(4)], 0) - 1.0) * 1e9
    for hp in range(4):
        two = bg[hp // 2, :, :, :, pl.ds(hp % 2 * 16, 16), :].astype(F32).reshape(64, 2, 8, 128)
        for h in range(2):
            biasb[hp, :, pl.ds(h * 128, 128)] = (two[:, h].reshape(512, 128) + keymask).astype(F32)

    lane8 = lax.div(lax.broadcasted_iota(jnp.int32, (8, 128), 1), 32)

    def attend(s, carry):
        last_rows(s, carry)
        key = kb[s].reshape(512, 256)
        value = jnp.concatenate([vt[s, b] for b in range(4)], 1)
        query = qt[s]
        parts = []
        for hp in range(4):
            g, r = hp // 2, hp % 2 * 2
            zero = jnp.zeros((32, 128), BF)
            pair_q = []
            for h in range(2):
                pieces = [zero] * 4
                pieces[r + h] = query[hp * 64 + h * 32 : hp * 64 + h * 32 + 32]
                pair_q.append(jnp.concatenate(pieces, 0))
            logits = mm(key[:, g * 128 : g * 128 + 128], jnp.concatenate(pair_q, 1)) + biasb[hp]
            low = logits - jnp.max(logits, 0, keepdims=True)
            probs = jnp.exp(low).astype(BF)
            summed = mm(
                jnp.concatenate([value[hp * 64 : hp * 64 + 64], jnp.ones((16, 512), BF)], 0), probs
            )
            scale = 1.0 / summed[64:65]
            parts.append(summed[0:32, 0:128] * scale[:, 0:128])
            parts.append(summed[32:64, 128:256] * scale[:, 128:256])
        attended = (jnp.concatenate(parts, 0) * gate[s]).astype(BF)
        attended = nt(e128, attended).astype(BF)
        result = (xin[s].astype(F32) + mm(attended, weight(4))).astype(BF)
        al[rj, s] = result

        @pl.when(s < 3)
        def _():
            start_out(s)

        on = norm(result.astype(F32), cscale[...])
        keep = cm[ri] * rows[seq * 16 + rj * 4 + s].astype(F32)
        on = (on * jnp.concatenate([keep, keep], 1)).astype(BF)
        left = nt(p1t, on)
        right[...] = nt(on, p2r)
        for y in range(4):
            ltile = jnp.zeros((8, 128), F32)
            rtile = jnp.zeros((8, 128), F32)
            for k in range(4):
                piece = left[k * 8 : k * 8 + 8]
                if k != y:
                    piece = pltpu.roll(piece, (32 * (k - y)) % 128, 1)
                ltile = jnp.where(lane8 == k, piece, ltile)
                rtile = jnp.where(lane8 == k, right[pl.ds(y * 32 + k, 8, stride=4), :], rtile)
            sndf[y, pl.ds(pl.multiple_of(s * 8, 8), 8), :] = ltile
            sndf[y, pl.ds(pl.multiple_of(32 + s * 8, 8), 8), :] = rtile

        @pl.when(s < 2)
        def _():
            far_rows(s + 2, carry)

        return carry

    a_lower, a_upper = first(64), second(64)

    def out(s, source):
        return al.at[source, s]

    def start_out(s):
        for i, (part, dev) in enumerate(
            ((a_lower, plus_y), (a_upper, minus_y), (a_upper, plus_y), (a_lower, minus_y))
        ):
            rcopy(part(out(s, rj)), part(out(s, rj)), AL + s * 6 + i, dev).start()

    def pass_out(s):
        ring_pass(
            out(s, behind(rj, 1)), out(s, ahead(rj, 1)), a_lower, a_upper, AL + s * 6,
            plus_y, minus_y,
        )

    lax.fori_loop(0, 4, attend, 0)

    snd[...] = sndf[...].astype(BF)

    def send_sides(n):
        rcopy(
            snd.at[ahead(rj, lax.rem(n, 4)), pl.ds(0, 32)], lraw.at[zl, rj], LL, in_zy(n)
        ).start()

    each(1, 16, send_sides)

    def send_right(n):
        @pl.when(jnp.logical_not(to_self(n)))
        def _():
            rcopy(
                snd.at[lax.div(n, 4), pl.ds(32, 32)], rraw.at[zl, rj], RR, right_to(n)
            ).start()

    each(0, 16, send_right)
    each(0, 2, pass_out)
    start_out(3)
    lraw[zl, rj] = snd[rj, 0:32]

    @pl.when(diagonal)
    def _():
        rraw[zl, rj] = snd[x, 32:64]

    def drain_head(s):
        for half in range(2):
            left_here(relay.at[half, s], RZ + s * 2 + half)
            left_here(relay.at[half, s], XZ + s * 2 + half)
        left_here(xn.at[s, ri], XM + s)
        left_here(xn.at[s, opp], XF + s)

    each(0, 4, drain_head)
    left_here(fifteen, BA)
    left_here(fifteen, BB)
    ring_sent(wbuf.at[rj], w_lower, w_upper, WT)
    ring_sent(bg.at[0, :, x], b_lower, b_upper, AX)
    ring_sent(bg.at[1, :, :, rj], b_lower, b_upper, BY)

    def regroup(raw, buf, place):
        def step(t):
            block = raw[t].astype(F32)
            for y in range(4):
                for s in range(4):
                    scr[pl.ds(y * 4 + s, 8, stride=16), :] = block[y, s * 8 : s * 8 + 8]
            buf[:, place, t] = scr[...].astype(BF).reshape(8, 16, 128)

        each(0, 4, step)

    q_lower, q_upper = first(4), second(4)
    arrived(fifteen, LL)
    regroup(lraw, lb, x)
    ring_start(lb.at[:, x], q_lower, q_upper, LX, plus_x, minus_x)

    @pl.when(diagonal)
    def _():
        arrived(fifteen, RR)

    @pl.when(jnp.logical_not(diagonal))
    def _():
        arrived(sixteen, RR)

    regroup(rraw, rb, rj)
    ring_start(rb.at[:, rj], q_lower, q_upper, R4, plus_y, minus_y)
    ring_pass(
        lb.at[:, behind(x, 1)], lb.at[:, ahead(x, 1)], q_lower, q_upper, LX, plus_x, minus_x
    )
    ring_pass(
        rb.at[:, behind(rj, 1)], rb.at[:, ahead(rj, 1)], q_lower, q_upper, R4, plus_y, minus_y
    )
    each(2, 4, pass_out)
    ring_end(
        lb.at[:, behind(x, 1)], lb.at[:, ahead(x, 1)], lb.at[:, ahead(x, 2)], q_lower, q_upper, LX
    )
    ring_end(
        rb.at[:, behind(rj, 1)], rb.at[:, ahead(rj, 1)], rb.at[:, ahead(rj, 2)],
        q_lower, q_upper, R4,
    )

    lane128 = lax.div(lax.broadcasted_iota(jnp.int32, (128, 128), 1), 32)

    def product(peer, u, carry):
        turned = nt(e128, rb[peer * 2 + u].reshape(256, 128)).astype(BF)
        for k in range(8):
            outer = mm(turned, lb[k].reshape(256, 128)).astype(BF)
            for j in range(4):
                bscr[j // 2, pl.ds(k * 32, 32), pl.ds((j % 2) * 128, 128)] = outer[
                    j * 32 : j * 32 + 32
                ]
        for jp in range(2):
            wide = mm(wst[...], bscr[jp])
            for half in range(2):
                c = half * 128
                mixed = wide[0:128, c : c + 128]
                for k in range(1, 4):
                    mixed = jnp.where(
                        lane128 == k, wide[k * 128 : k * 128 + 128, c : c + 128], mixed
                    )
                ub[peer, pl.ds(u * 4 + jp * 2 + half, 32, stride=8), :] = nt(
                    pick, mixed.astype(BF)
                )
        return carry

    def in_order(t):
        return jnp.where(t == 0, 2, jnp.where(t == 1, 1, t + 1))

    def for_peer(t):
        d = in_order(t)
        peer = ahead(rj, d)
        lax.fori_loop(0, 2, lambda u, carry: product(peer, u, carry), 0)
        ubf[peer] = ub[peer].astype(BF)

        @pl.when(t < 3)
        def _():
            update_copy(d).start()

    def update_copy(d):
        peer = ahead(rj, d)
        return rcopy(ubf.at[peer], ugot.at[rj], UP + d - 1, {"rj": peer})

    each(0, 4, for_peer)
    ugot[rj] = ubf[rj]
    each(1, 4, lambda d: arrived(ugot.at[behind(rj, d)], UP + d - 1))
    keep = pltpu.make_async_copy(ugot, out_update, usem)
    keep.start()

    def write_out(s):
        return pltpu.make_async_copy(al.at[:, s], out_al.at[:, s], osem.at[s])

    def drain(s):
        ring_end(
            out(s, behind(rj, 1)), out(s, ahead(rj, 1)), out(s, ahead(rj, 2)), a_lower, a_upper,
            AL + s * 6,
        )
        write_out(s).start()

    each(0, 4, drain)
    each(0, 4, lambda s: ring_sent(out(s, rj), a_lower, a_upper, AL + s * 6))
    ring_sent(lb.at[:, x], q_lower, q_upper, LX)
    ring_sent(rb.at[:, rj], q_lower, q_upper, R4)
    left_here(fifteen, LL)

    @pl.when(diagonal)
    def _():
        left_here(fifteen, RR)

    @pl.when(jnp.logical_not(diagonal))
    def _():
        left_here(sixteen, RR)

    each(1, 4, lambda d: left_here(ubf.at[ahead(rj, d)], UP + d - 1))
    keep.wait()
    each(0, 4, lambda s: write_out(s).wait())


def finish(
    al_in, update_in, pair_in, rowv_in, al_out, pair_out, al, update, pair, rowv, result, sem, back
):
    inward = [
        pltpu.make_async_copy(update_in, update, sem.at[0]),
        pltpu.make_async_copy(pair_in, pair, sem.at[1]),
        pltpu.make_async_copy(rowv_in, rowv, sem.at[2]),
    ] + [pltpu.make_async_copy(al_in.at[k], al.at[k], sem.at[3 + k]) for k in range(4)]
    outward = [pltpu.make_async_copy(al.at[k], al_out.at[k], back.at[k]) for k in range(4)]
    outward.append(pltpu.make_async_copy(result, pair_out, back.at[4]))
    for copy in inward:
        copy.start()
    for k in range(3):
        inward[k].wait()
    scale = 1.0 / jnp.maximum(jnp.sum(rowv[...].astype(F32)), 1.0)
    result[...] = (
        pair[...].astype(F32) + update[...].reshape(1024, 128).astype(F32) * scale
    ).astype(BF)
    outward[4].start()
    for k in range(4):
        inward[3 + k].wait()
        outward[k].start()
    for copy in outward:
        copy.wait()


def on_device(
    homolog_embedding,
    pairwise_state,
    residue_mask,
    alignment_row_mask,
    focus_layer_scale,
    asking_projector,
    lookup_projector,
    content_projector,
    sigmoid_projector,
    gate_offset_bias,
    final_projector,
    pairwise_norm_gain,
    bias_weight,
    cross_layer_scale,
    first_cross_projector,
    second_cross_projector,
    outer_weight,
):
    hbm = pl.BlockSpec(memory_space=pl.ANY)
    gathered, update = pl.pallas_call(
        kernel,
        out_shape=(
            jax.ShapeDtypeStruct((4, 4, 128, 256), BF),
            jax.ShapeDtypeStruct((4, 256, 128), BF),
        ),
        in_specs=[hbm] * 17,
        out_specs=(hbm, hbm),
        scratch_shapes=[
            pltpu.VMEM((4, 128, 256), BF),
            pltpu.VMEM((1024, 128), BF),
            pltpu.VMEM((4, 128), jnp.int32),
            pltpu.SMEM((256,), jnp.int32),
            pltpu.VMEM((1, 256), F32),
            pltpu.VMEM((1, 256), F32),
            pltpu.VMEM((1, 128), F32),
            pltpu.VMEM((8, 128), BF),
            pltpu.VMEM((1, 256), F32),
            pltpu.VMEM((32, 256), BF),
            pltpu.VMEM((32, 256), BF),
            pltpu.VMEM((1024, 128), BF),
            pltpu.VMEM((4, 4, 128, 256), BF),
            pltpu.VMEM((2, 4, 64, 256), BF),
            pltpu.VMEM((4, 320, 256), BF),
            pltpu.VMEM((1024, 128), F32),
            pltpu.VMEM((64, 128), F32),
            pltpu.VMEM((2, 4, 4, 4, 32, 128), BF),
            pltpu.VMEM((256, 256), BF),
            pltpu.VMEM((768, 256), BF),
            pltpu.VMEM((4, 4, 128, 256), BF),
            pltpu.VMEM((4, 256, 128), BF),
            pltpu.VMEM((4, 4, 256, 128), BF),
            pltpu.VMEM((4, 256, 128), F32),
            pltpu.VMEM((4, 512, 256), F32),
            pltpu.VMEM((256, 128), F32),
            pltpu.VMEM((4, 128, 128), F32),
            pltpu.VMEM((512, 256), BF),
            pltpu.VMEM((4, 4, 128, 256), BF),
            pltpu.VMEM((128, 128), F32),
            pltpu.VMEM((4, 64, 128), F32),
            pltpu.VMEM((4, 64, 128), BF),
            pltpu.VMEM((4, 4, 32, 128), BF),
            pltpu.VMEM((4, 4, 32, 128), BF),
            pltpu.VMEM((128, 128), F32),
            pltpu.VMEM((8, 4, 4, 16, 128), BF),
            pltpu.VMEM((8, 4, 4, 16, 128), BF),
            pltpu.VMEM((2, 256, 256), BF),
            pltpu.VMEM((4, 256, 128), F32),
            pltpu.VMEM((4, 256, 128), BF),
            pltpu.VMEM((4, 256, 128), BF),
            pltpu.SemaphoreType.DMA((COUNT,)),
            pltpu.SemaphoreType.DMA((COUNT,)),
            pltpu.SemaphoreType.DMA((17,)),
            pltpu.SemaphoreType.DMA((4,)),
            pltpu.SemaphoreType.DMA,
        ],
        compiler_params=pltpu.CompilerParams(
            collective_id=0, has_side_effects=True, vmem_limit_bytes=60 * 1024 * 1024
        ),
        cost_estimate=pl.CostEstimate(
            flops=4_000_000_000, bytes_accessed=4_000_000, transcendentals=2_000_000
        ),
    )(
        homolog_embedding,
        pairwise_state.reshape(1024, 128),
        residue_mask.reshape(4, 128),
        alignment_row_mask,
        focus_layer_scale.reshape(1, 256),
        asking_projector.T,
        lookup_projector.T,
        content_projector.T,
        sigmoid_projector.T,
        gate_offset_bias.reshape(1, 256),
        final_projector,
        pairwise_norm_gain.reshape(1, 128),
        bias_weight.T,
        cross_layer_scale.reshape(1, 256),
        first_cross_projector.T,
        second_cross_projector.T,
        outer_weight,
    )
    alignment_output, pair_rows = pl.pallas_call(
        finish,
        out_shape=(
            jax.ShapeDtypeStruct((4, 4, 128, 256), BF),
            jax.ShapeDtypeStruct((1024, 128), BF),
        ),
        in_specs=[hbm] * 4,
        out_specs=(hbm, hbm),
        scratch_shapes=[
            pltpu.VMEM((4, 4, 128, 256), BF),
            pltpu.VMEM((4, 256, 128), BF),
            pltpu.VMEM((1024, 128), BF),
            pltpu.VMEM((2, 128), jnp.int32),
            pltpu.VMEM((1024, 128), BF),
            pltpu.SemaphoreType.DMA((7,)),
            pltpu.SemaphoreType.DMA((5,)),
        ],
        compiler_params=pltpu.CompilerParams(vmem_limit_bytes=60 * 1024 * 1024),
    )(gathered, update, pairwise_state.reshape(1024, 128), alignment_row_mask.reshape(2, 128))
    return alignment_output.reshape(16, 128, 256), pair_rows.reshape(128, 8, 128)


def solution(mesh):
    placed = (
        P("seq", "ri", None),
        P("ri", ("seq", "rj"), None),
        P(),
        P(),
        P(),
        P(None, "rj"),
        P(None, "rj"),
        P(None, "rj"),
        P(None, "rj"),
        P(),
        P("rj", None),
        P(),
        P(),
        P(),
        P(),
        P(),
        P(),
    )
    return jax.shard_map(
        on_device,
        mesh=mesh,
        in_specs=placed,
        out_specs=(P("seq", "ri", None), P("ri", ("seq", "rj"), None)),
        check_vma=False,
    )
```

```python
import jax
import jax.numpy as jnp
from jax import lax
from jax.experimental import pallas as pl
from jax.experimental.pallas import tpu as pltpu
from jax.sharding import PartitionSpec as P

F32 = jnp.float32
BF = jnp.bfloat16
NT = (((1,), (1,)), ((), ()))

SIZES = (8, 8, 4, 4, 6, 1, 1, 6, 6, 24, 1, 1, 6, 6, 3)
RZ, XZ, XM, XF, WT, BA, BB, AX, BY, AL, LL, RR, LX, R4, UP = (
    sum(SIZES[:i]) for i in range(len(SIZES))
)
COUNT = sum(SIZES)


def nt(a, b):
    return lax.dot_general(a, b, NT, preferred_element_type=F32)


def mm(a, b):
    return jnp.dot(a, b, preferred_element_type=F32)


def norm(values, gain):
    centre = values - jnp.mean(values, -1, keepdims=True)
    spread = jnp.mean(centre * centre, -1, keepdims=True)
    return centre * lax.rsqrt(spread + 1e-5) * gain


def eye(n):
    row = lax.broadcasted_iota(jnp.int32, (n, n), 0)
    col = lax.broadcasted_iota(jnp.int32, (n, n), 1)
    return (row == col).astype(F32).astype(BF)


def kernel(
    hom, pair_in, resm_in, rows_in, fscale_in, wq, wk, wv, wg, gb_in, wo, pgain_in, bw_in,
    cscale_in, p1_in, p2_in, ow_in,
    out_al, out_update,
    xin, pair, resm, rows, fscale, gb, pgain, bw, cscale, p1, p2, ow,
    xn, relay, wbuf, pn, bt, bg, wkn, wqvg, kb, qt, vt, gate, biasb, gbt, cm, wst, al, right, sndf, snd, lraw, rraw, scr, lb, rb,
    bscr, ub, ubf, ugot,
    ssem, rsem, lsem, osem, usem,
):
    seq = lax.axis_index("seq")
    ri = lax.axis_index("ri")
    rj = lax.axis_index("rj")
    zl, x = lax.div(seq, 4), lax.rem(seq, 4)
    mate = ri + 1 - 2 * lax.rem(ri, 2)
    opp = lax.rem(ri + 2, 4)
    oppmate = lax.rem(mate + 2, 4)

    def ahead(v, d):
        return lax.rem(v + d, 4)

    def behind(v, d):
        return lax.rem(v + 4 - d, 4)

    plus_y, minus_y = {"rj": ahead(rj, 1)}, {"rj": behind(rj, 1)}
    plus_x, minus_x = {"seq": zl * 4 + ahead(x, 1)}, {"seq": zl * 4 + behind(x, 1)}
    core, z = lax.rem(ri, 2), lax.div(ri, 2) * 4 + zl

    def along_z(step):
        to = lax.rem(z + step, 8)
        return lax.div(to, 4) * 2 + core, {
            "seq": lax.rem(to, 4) * 4 + x,
            "ri": lax.div(to, 4) * 2 + core,
        }

    ri_up, up = along_z(2)
    ri_down, down = along_z(6)

    def seq_of(zz, xx):
        return zz * 4 + xx

    def in_zy(n):
        return {"seq": seq_of(ahead(zl, lax.div(n, 4)), x), "rj": ahead(rj, lax.rem(n, 4))}

    def in_zx(n):
        return {"seq": seq_of(ahead(zl, lax.div(n, 4)), ahead(x, lax.rem(n, 4)))}

    def right_to(n):
        return {"seq": seq_of(ri, lax.div(n, 4)), "ri": lax.rem(n, 4), "rj": x}

    def right_from(n):
        return {"seq": seq_of(lax.div(n, 4), rj), "ri": zl, "rj": lax.rem(n, 4)}

    def each(low, high, body):
        def step(n, carry):
            body(n)
            return carry

        lax.fori_loop(low, high, step, 0)

    diagonal = jnp.logical_and(zl == ri, x == rj)

    def to_self(n):
        return jnp.logical_and(diagonal, n == seq_of(x, ri))

    def from_self(n):
        return jnp.logical_and(diagonal, n == seq_of(zl, rj))


    def rcopy(src, dst, k, dev, send=None):
        return pltpu.make_async_remote_copy(
            src_ref=src,
            dst_ref=dst,
            send_sem=ssem.at[k if send is None else send],
            recv_sem=rsem.at[k],
            device_id=dev,
            device_id_type=pl.DeviceIdType.MESH,
        )

    def arrived(ref, k):
        pltpu.make_async_copy(ref, ref, rsem.at[k]).wait()

    def left_here(ref, k):
        pltpu.make_async_copy(ref, ref, ssem.at[k]).wait()

    def ring_start(own, lower, upper, k, plus, minus):
        for i, (part, dev) in enumerate(
            ((lower, plus), (upper, minus), (upper, plus), (lower, minus))
        ):
            rcopy(part(own), part(own), k + i, dev).start()

    def ring_pass(before, after, lower, upper, k, plus, minus):
        arrived(lower(before), k)
        rcopy(lower(before), lower(before), k + 4, plus).start()
        arrived(upper(after), k + 1)
        rcopy(upper(after), upper(after), k + 5, minus).start()

    def ring_end(before, after, far, lower, upper, k):
        arrived(upper(before), k + 2)
        arrived(lower(after), k + 3)
        arrived(lower(far), k + 4)
        arrived(upper(far), k + 5)

    def ring_sent(own, lower, upper, k):
        for i, part in enumerate((lower, upper, upper, lower, lower, upper)):
            left_here(part(own), k + i)

    def first(n):
        return lambda ref: ref.at[pl.ds(0, n)]

    def second(n):
        return lambda ref: ref.at[pl.ds(n, n)]

    inward = [
        (hom.at[pl.ds(rj * 4, 4)], xin),
        (fscale_in, fscale),
        (pair_in, pair),
        (pgain_in, pgain),
        (bw_in, bw),
        (wq, wbuf.at[rj, pl.ds(0, 64)]),
        (wk, wbuf.at[rj, pl.ds(64, 64)]),
        (wv, wbuf.at[rj, pl.ds(128, 64)]),
        (wg, wbuf.at[rj, pl.ds(192, 64)]),
        (wo, wbuf.at[rj, pl.ds(256, 64)]),
        (resm_in, resm),
        (rows_in, rows),
        (gb_in, gb),
        (cscale_in, cscale),
        (p1_in, p1),
        (p2_in, p2),
        (ow_in, ow),
    ]

    def local(k):
        return pltpu.make_async_copy(inward[k][0], inward[k][1], lsem.at[k])

    for k in range(len(inward)):
        local(k).start()

    barrier = pltpu.get_barrier_semaphore()

    def greet(dev):
        pl.semaphore_signal(barrier, inc=1, device_id=dev, device_id_type=pl.DeviceIdType.MESH)

    def greet_all(n):
        greet(in_zy(n))
        greet(in_zx(n))

    each(1, 16, greet_all)
    for dev in ({"ri": mate}, up, down):
        greet(dev)

    def greet_right(n):
        @pl.when(jnp.logical_not(from_self(n)))
        def _():
            greet(right_from(n))

    each(0, 16, greet_right)

    local(0).wait()
    local(1).wait()

    def norm_x(s, carry):
        xn[s, ri] = norm(xin[s].astype(F32), fscale[...]).astype(BF)
        return carry

    lax.fori_loop(0, 4, norm_x, 0)

    pl.semaphore_wait(barrier, 49 - diagonal.astype(jnp.int32))

    def send_x(s):
        rcopy(xn.at[s, ri, pl.ds(0, 64)], relay.at[0, s], RZ + s * 2, up).start()
        rcopy(xn.at[s, ri, pl.ds(64, 64)], relay.at[1, s], RZ + s * 2 + 1, down).start()
        rcopy(xn.at[s, ri], xn.at[s, ri], XM + s, {"ri": mate}).start()

    def relay_x(s):
        arrived(relay.at[0, s], RZ + s * 2)
        rcopy(relay.at[0, s], xn.at[s, ri_down, pl.ds(0, 64)], XZ + s * 2, up).start()
        arrived(relay.at[1, s], RZ + s * 2 + 1)
        rcopy(relay.at[1, s], xn.at[s, ri_up, pl.ds(64, 64)], XZ + s * 2 + 1, down).start()

    for s in range(4):
        send_x(s)
    for k in range(5, 10):
        local(k).wait()
    w_lower, w_upper = first(160), second(160)
    ring_start(wbuf.at[rj], w_lower, w_upper, WT, plus_y, minus_y)

    for k in range(2, 5):
        local(k).wait()
    pn[...] = norm(pair[...].astype(F32), pgain[...]).astype(BF).astype(F32)
    for j in range(8):
        tile = pn[pl.ds(j, 128, stride=8), :].astype(BF)
        bt[pl.ds(j, 8, stride=8), :] = nt(bw[...], tile)
    for half in range(2):
        bg[half, zl, x, rj] = bt[pl.ds(half * 32, 32), :].astype(BF)
    def send_bias(n):
        rcopy(bg.at[0, zl, x, rj], bg.at[0, zl, x, rj], BA, in_zy(n)).start()
        rcopy(bg.at[1, zl, x, rj], bg.at[1, zl, x, rj], BB, in_zx(n)).start()

    each(1, 16, send_bias)
    relay_x(0)
    relay_x(1)

    for k in range(10, len(inward)):
        local(k).wait()
    ring_pass(
        wbuf.at[behind(rj, 1)], wbuf.at[ahead(rj, 1)], w_lower, w_upper, WT, plus_y, minus_y
    )
    fifteen, sixteen = bscr.at[0, 0, pl.ds(0, 240)], bscr.at[0, 0]
    arrived(fifteen, BA)
    arrived(fifteen, BB)
    b_lower, b_upper = first(2), second(2)
    ring_start(bg.at[0, :, x], b_lower, b_upper, AX, plus_x, minus_x)
    ring_start(bg.at[1, :, :, rj], b_lower, b_upper, BY, plus_y, minus_y)
    relay_x(2)

    row128 = lax.broadcasted_iota(jnp.int32, (128, 128), 0)
    col128 = lax.broadcasted_iota(jnp.int32, (128, 128), 1)
    ones = jnp.ones((128, 128), BF)
    for b in range(4):
        res = resm[pl.ds(b, 1), :].astype(F32)
        spread = jnp.where(row128 == col128, jnp.broadcast_to(res, (128, 128)), 0.0).astype(BF)
        cm[b] = mm(spread, ones)
    for b in range(2):
        gbt[pl.ds(b * 128, 128), :] = jnp.transpose(
            jnp.broadcast_to(gb[:, pl.ds(b * 128, 128)], (128, 128))
        )
    e128 = eye(128)
    for k in range(4):
        wst[pl.ds(k * 128, 128), :] = nt(e128, ow[pl.ds(k * 256, 256), :]).astype(BF)
    pick = (
        lax.broadcasted_iota(jnp.int32, (32, 128), 0)
        == lax.rem(lax.broadcasted_iota(jnp.int32, (32, 128), 1), 32)
    ).astype(F32).astype(BF)
    p1t = p1[...]
    p2r = jnp.concatenate([p2[...]] * 4, 0)

    relay_x(3)

    ring_end(
        wbuf.at[behind(rj, 1)], wbuf.at[ahead(rj, 1)], wbuf.at[ahead(rj, 2)], w_lower, w_upper, WT
    )

    def weight(k):
        return wbuf[:, pl.ds(k * 64, 64), :].reshape(256, 256)

    wkn[...] = nt(eye(256), weight(1)).astype(BF)
    wqvg[0:256] = weight(0)
    wqvg[256:512] = weight(2)
    wqvg[512:768] = weight(3)

    def own_rows(s, carry):
        block = xn[s, ri]
        kb[s, ri] = mm(block, wkn[...]).astype(BF)
        three = nt(wqvg[...], block)
        qt[s] = (three[0:256] * 32 ** -0.5).astype(BF)
        vt[s, ri] = three[256:512].astype(BF)
        gate[s] = jax.nn.sigmoid(three[512:768] + gbt[...])
        return carry

    def other_rows(s, b):
        block = xn[s, b]
        kb[s, b] = mm(block, wkn[...]).astype(BF)
        vt[s, b] = nt(wqvg[256:512], block).astype(BF)

    lax.fori_loop(0, 4, own_rows, 0)
    ring_pass(
        bg.at[0, :, behind(x, 1)], bg.at[0, :, ahead(x, 1)], b_lower, b_upper, AX, plus_x, minus_x
    )
    ring_pass(
        bg.at[1, :, :, behind(rj, 1)], bg.at[1, :, :, ahead(rj, 1)], b_lower, b_upper,
        BY, plus_y, minus_y,
    )

    def near_rows(s, carry):
        arrived(xn.at[s, mate], XM + s)
        other_rows(s, mate)
        return carry

    def far_rows(s, carry):
        arrived(xn.at[s, opp, pl.ds(0, 64)], XZ + s * 2)
        arrived(xn.at[s, opp, pl.ds(64, 64)], XZ + s * 2 + 1)
        rcopy(xn.at[s, opp], xn.at[s, opp], XF + s, {"ri": mate}).start()
        other_rows(s, opp)
        return carry

    def last_rows(s, carry):
        arrived(xn.at[s, oppmate], XF + s)
        other_rows(s, oppmate)
        return carry

    lax.fori_loop(0, 4, near_rows, 0)
    lax.fori_loop(0, 2, far_rows, 0)
    ring_end(
        bg.at[0, :, behind(x, 1)], bg.at[0, :, ahead(x, 1)], bg.at[0, :, ahead(x, 2)],
        b_lower, b_upper, AX,
    )
    ring_end(
        bg.at[1, :, :, behind(rj, 1)], bg.at[1, :, :, ahead(rj, 1)], bg.at[1, :, :, ahead(rj, 2)],
        b_lower, b_upper, BY,
    )

    keymask = (jnp.concatenate([cm[b] for b in range(4)], 0) - 1.0) * 1e9
    for hp in range(4):
        two = bg[hp // 2, :, :, :, pl.ds(hp % 2 * 16, 16), :].astype(F32).reshape(64, 2, 8, 128)
        for h in range(2):
            biasb[hp, :, pl.ds(h * 128, 128)] = (two[:, h].reshape(512, 128) + keymask).astype(F32)

    lane8 = lax.div(lax.broadcasted_iota(jnp.int32, (8, 128), 1), 32)

    def heads(s):
        key = kb[s].reshape(512, 256)
        value = jnp.concatenate([vt[s, b] for b in range(4)], 1)
        query = qt[s]
        parts = []
        for hp in range(4):
            g, r = hp // 2, hp % 2 * 2
            zero = jnp.zeros((32, 128), BF)
            pair_q = []
            for h in range(2):
                pieces = [zero] * 4
                pieces[r + h] = query[hp * 64 + h * 32 : hp * 64 + h * 32 + 32]
                pair_q.append(jnp.concatenate(pieces, 0))
            logits = mm(key[:, g * 128 : g * 128 + 128], jnp.concatenate(pair_q, 1)) + biasb[hp]
            low = logits - jnp.max(logits, 0, keepdims=True)
            probs = jnp.exp(low).astype(BF)
            summed = mm(
                jnp.concatenate([value[hp * 64 : hp * 64 + 64], jnp.ones((16, 512), BF)], 0), probs
            )
            scale = 1.0 / summed[64:65]
            parts.append(summed[0:32, 0:128] * scale[:, 0:128])
            parts.append(summed[32:64, 128:256] * scale[:, 128:256])
        return (jnp.concatenate(parts, 0) * gate[s]).astype(BF)

    def project(s, attended):
        attended = nt(e128, attended).astype(BF)
        result = (xin[s].astype(F32) + mm(attended, weight(4))).astype(BF)
        al[rj, s] = result
        on = norm(result.astype(F32), cscale[...])
        keep = cm[ri] * rows[seq * 16 + rj * 4 + s].astype(F32)
        on = (on * jnp.concatenate([keep, keep], 1)).astype(BF)
        left = nt(p1t, on)
        right[...] = nt(on, p2r)
        for y in range(4):
            ltile = jnp.zeros((8, 128), F32)
            rtile = jnp.zeros((8, 128), F32)
            for k in range(4):
                piece = left[k * 8 : k * 8 + 8]
                if k != y:
                    piece = pltpu.roll(piece, (32 * (k - y)) % 128, 1)
                ltile = jnp.where(lane8 == k, piece, ltile)
                rtile = jnp.where(lane8 == k, right[pl.ds(y * 32 + k, 8, stride=4), :], rtile)
            sndf[y, pl.ds(pl.multiple_of(s * 8, 8), 8), :] = ltile
            sndf[y, pl.ds(pl.multiple_of(32 + s * 8, 8), 8), :] = rtile

    def attend(s, before):
        last_rows(s, 0)
        attended = heads(s)
        project(lax.rem(s + 3, 4), before)

        @pl.when(s > 0)
        def _():
            start_out(s - 1)

        @pl.when(s < 2)
        def _():
            far_rows(s + 2, 0)

        return attended

    a_lower, a_upper = first(64), second(64)

    def out(s, source):
        return al.at[source, s]

    def start_out(s):
        for i, (part, dev) in enumerate(
            ((a_lower, plus_y), (a_upper, minus_y), (a_upper, plus_y), (a_lower, minus_y))
        ):
            rcopy(part(out(s, rj)), part(out(s, rj)), AL + s * 6 + i, dev).start()

    def pass_out(s):
        ring_pass(
            out(s, behind(rj, 1)), out(s, ahead(rj, 1)), a_lower, a_upper, AL + s * 6,
            plus_y, minus_y,
        )

    project(3, lax.fori_loop(0, 4, attend, jnp.zeros((256, 128), BF)))

    snd[...] = sndf[...].astype(BF)

    def send_sides(n):
        rcopy(
            snd.at[ahead(rj, lax.rem(n, 4)), pl.ds(0, 32)], lraw.at[zl, rj], LL, in_zy(n)
        ).start()

    each(1, 16, send_sides)

    def send_right(n):
        @pl.when(jnp.logical_not(to_self(n)))
        def _():
            rcopy(
                snd.at[lax.div(n, 4), pl.ds(32, 32)], rraw.at[zl, rj], RR, right_to(n)
            ).start()

    each(0, 16, send_right)
    each(0, 2, pass_out)
    start_out(3)
    lraw[zl, rj] = snd[rj, 0:32]

    @pl.when(diagonal)
    def _():
        rraw[zl, rj] = snd[x, 32:64]

    def drain_head(s):
        for half in range(2):
            left_here(relay.at[half, s], RZ + s * 2 + half)
            left_here(relay.at[half, s], XZ + s * 2 + half)
        left_here(xn.at[s, ri], XM + s)
        left_here(xn.at[s, opp], XF + s)

    each(0, 4, drain_head)
    left_here(fifteen, BA)
    left_here(fifteen, BB)
    ring_sent(wbuf.at[rj], w_lower, w_upper, WT)
    ring_sent(bg.at[0, :, x], b_lower, b_upper, AX)
    ring_sent(bg.at[1, :, :, rj], b_lower, b_upper, BY)

    def regroup(raw, buf, place):
        def step(t):
            block = raw[t].astype(F32)
            for y in range(4):
                for s in range(4):
                    scr[pl.ds(y * 4 + s, 8, stride=16), :] = block[y, s * 8 : s * 8 + 8]
            buf[:, place, t] = scr[...].astype(BF).reshape(8, 16, 128)

        each(0, 4, step)

    q_lower, q_upper = first(4), second(4)
    arrived(fifteen, LL)
    regroup(lraw, lb, x)
    ring_start(lb.at[:, x], q_lower, q_upper, LX, plus_x, minus_x)

    @pl.when(diagonal)
    def _():
        arrived(fifteen, RR)

    @pl.when(jnp.logical_not(diagonal))
    def _():
        arrived(sixteen, RR)

    regroup(rraw, rb, rj)
    ring_start(rb.at[:, rj], q_lower, q_upper, R4, plus_y, minus_y)
    ring_pass(
        lb.at[:, behind(x, 1)], lb.at[:, ahead(x, 1)], q_lower, q_upper, LX, plus_x, minus_x
    )
    ring_pass(
        rb.at[:, behind(rj, 1)], rb.at[:, ahead(rj, 1)], q_lower, q_upper, R4, plus_y, minus_y
    )
    each(2, 4, pass_out)
    ring_end(
        lb.at[:, behind(x, 1)], lb.at[:, ahead(x, 1)], lb.at[:, ahead(x, 2)], q_lower, q_upper, LX
    )
    ring_end(
        rb.at[:, behind(rj, 1)], rb.at[:, ahead(rj, 1)], rb.at[:, ahead(rj, 2)],
        q_lower, q_upper, R4,
    )

    lane128 = lax.div(lax.broadcasted_iota(jnp.int32, (128, 128), 1), 32)

    def product(peer, u):
        turned = nt(e128, rb[peer * 2 + u].reshape(256, 128)).astype(BF)
        for k in range(8):
            outer = mm(turned, lb[k].reshape(256, 128)).astype(BF)
            for j in range(4):
                bscr[u, j // 2, pl.ds(k * 32, 32), pl.ds((j % 2) * 128, 128)] = outer[
                    j * 32 : j * 32 + 32
                ]
        for jp in range(2):
            wide = mm(wst[...], bscr[u, jp])
            for half in range(2):
                c = half * 128
                mixed = wide[0:128, c : c + 128]
                for k in range(1, 4):
                    mixed = jnp.where(
                        lane128 == k, wide[k * 128 : k * 128 + 128, c : c + 128], mixed
                    )
                ub[peer, pl.ds(u * 4 + jp * 2 + half, 32, stride=8), :] = nt(
                    pick, mixed.astype(BF)
                )

    def in_order(t):
        return jnp.where(t == 0, 2, jnp.where(t == 1, 1, t + 1))

    def for_peer(t):
        d = in_order(t)
        peer = ahead(rj, d)
        for u in range(2):
            product(peer, u)
        ubf[peer] = ub[peer].astype(BF)

        @pl.when(t < 3)
        def _():
            update_copy(d).start()

    def update_copy(d):
        peer = ahead(rj, d)
        return rcopy(ubf.at[peer], ugot.at[rj], UP + d - 1, {"rj": peer})

    each(0, 4, for_peer)
    ugot[rj] = ubf[rj]
    each(1, 4, lambda d: arrived(ugot.at[behind(rj, d)], UP + d - 1))
    keep = pltpu.make_async_copy(ugot, out_update, usem)
    keep.start()

    def write_out(s):
        return pltpu.make_async_copy(al.at[:, s], out_al.at[:, s], osem.at[s])

    def drain(s):
        ring_end(
            out(s, behind(rj, 1)), out(s, ahead(rj, 1)), out(s, ahead(rj, 2)), a_lower, a_upper,
            AL + s * 6,
        )
        write_out(s).start()

    each(0, 4, drain)
    each(0, 4, lambda s: ring_sent(out(s, rj), a_lower, a_upper, AL + s * 6))
    ring_sent(lb.at[:, x], q_lower, q_upper, LX)
    ring_sent(rb.at[:, rj], q_lower, q_upper, R4)
    left_here(fifteen, LL)

    @pl.when(diagonal)
    def _():
        left_here(fifteen, RR)

    @pl.when(jnp.logical_not(diagonal))
    def _():
        left_here(sixteen, RR)

    each(1, 4, lambda d: left_here(ubf.at[ahead(rj, d)], UP + d - 1))
    keep.wait()
    each(0, 4, lambda s: write_out(s).wait())


def finish(
    al_in, update_in, pair_in, rowv_in, al_out, pair_out, al, update, pair, rowv, result, sem, back
):
    inward = [
        pltpu.make_async_copy(update_in, update, sem.at[0]),
        pltpu.make_async_copy(pair_in, pair, sem.at[1]),
        pltpu.make_async_copy(rowv_in, rowv, sem.at[2]),
    ] + [pltpu.make_async_copy(al_in.at[k], al.at[k], sem.at[3 + k]) for k in range(4)]
    outward = [pltpu.make_async_copy(al.at[k], al_out.at[k], back.at[k]) for k in range(4)]
    outward.append(pltpu.make_async_copy(result, pair_out, back.at[4]))
    for copy in inward:
        copy.start()
    for k in range(3):
        inward[k].wait()
    scale = 1.0 / jnp.maximum(jnp.sum(rowv[...].astype(F32)), 1.0)
    result[...] = (
        pair[...].astype(F32) + update[...].reshape(1024, 128).astype(F32) * scale
    ).astype(BF)
    outward[4].start()
    for k in range(4):
        inward[3 + k].wait()
        outward[k].start()
    for copy in outward:
        copy.wait()


def on_device(
    homolog_embedding,
    pairwise_state,
    residue_mask,
    alignment_row_mask,
    focus_layer_scale,
    asking_projector,
    lookup_projector,
    content_projector,
    sigmoid_projector,
    gate_offset_bias,
    final_projector,
    pairwise_norm_gain,
    bias_weight,
    cross_layer_scale,
    first_cross_projector,
    second_cross_projector,
    outer_weight,
):
    hbm = pl.BlockSpec(memory_space=pl.ANY)
    gathered, update = pl.pallas_call(
        kernel,
        out_shape=(
            jax.ShapeDtypeStruct((4, 4, 128, 256), BF),
            jax.ShapeDtypeStruct((4, 256, 128), BF),
        ),
        in_specs=[hbm] * 17,
        out_specs=(hbm, hbm),
        scratch_shapes=[
            pltpu.VMEM((4, 128, 256), BF),
            pltpu.VMEM((1024, 128), BF),
            pltpu.VMEM((4, 128), jnp.int32),
            pltpu.SMEM((256,), jnp.int32),
            pltpu.VMEM((1, 256), F32),
            pltpu.VMEM((1, 256), F32),
            pltpu.VMEM((1, 128), F32),
            pltpu.VMEM((8, 128), BF),
            pltpu.VMEM((1, 256), F32),
            pltpu.VMEM((32, 256), BF),
            pltpu.VMEM((32, 256), BF),
            pltpu.VMEM((1024, 128), BF),
            pltpu.VMEM((4, 4, 128, 256), BF),
            pltpu.VMEM((2, 4, 64, 256), BF),
            pltpu.VMEM((4, 320, 256), BF),
            pltpu.VMEM((1024, 128), F32),
            pltpu.VMEM((64, 128), F32),
            pltpu.VMEM((2, 4, 4, 4, 32, 128), BF),
            pltpu.VMEM((256, 256), BF),
            pltpu.VMEM((768, 256), BF),
            pltpu.VMEM((4, 4, 128, 256), BF),
            pltpu.VMEM((4, 256, 128), BF),
            pltpu.VMEM((4, 4, 256, 128), BF),
            pltpu.VMEM((4, 256, 128), F32),
            pltpu.VMEM((4, 512, 256), F32),
            pltpu.VMEM((256, 128), F32),
            pltpu.VMEM((4, 128, 128), F32),
            pltpu.VMEM((512, 256), BF),
            pltpu.VMEM((4, 4, 128, 256), BF),
            pltpu.VMEM((128, 128), F32),
            pltpu.VMEM((4, 64, 128), F32),
            pltpu.VMEM((4, 64, 128), BF),
            pltpu.VMEM((4, 4, 32, 128), BF),
            pltpu.VMEM((4, 4, 32, 128), BF),
            pltpu.VMEM((128, 128), F32),
            pltpu.VMEM((8, 4, 4, 16, 128), BF),
            pltpu.VMEM((8, 4, 4, 16, 128), BF),
            pltpu.VMEM((2, 2, 256, 256), BF),
            pltpu.VMEM((4, 256, 128), F32),
            pltpu.VMEM((4, 256, 128), BF),
            pltpu.VMEM((4, 256, 128), BF),
            pltpu.SemaphoreType.DMA((COUNT,)),
            pltpu.SemaphoreType.DMA((COUNT,)),
            pltpu.SemaphoreType.DMA((17,)),
            pltpu.SemaphoreType.DMA((4,)),
            pltpu.SemaphoreType.DMA,
        ],
        compiler_params=pltpu.CompilerParams(
            collective_id=0, has_side_effects=True, vmem_limit_bytes=60 * 1024 * 1024
        ),
        cost_estimate=pl.CostEstimate(
            flops=4_000_000_000, bytes_accessed=4_000_000, transcendentals=2_000_000
        ),
    )(
        homolog_embedding,
        pairwise_state.reshape(1024, 128),
        residue_mask.reshape(4, 128),
        alignment_row_mask,
        focus_layer_scale.reshape(1, 256),
        asking_projector.T,
        lookup_projector.T,
        content_projector.T,
        sigmoid_projector.T,
        gate_offset_bias.reshape(1, 256),
        final_projector,
        pairwise_norm_gain.reshape(1, 128),
        bias_weight.T,
        cross_layer_scale.reshape(1, 256),
        first_cross_projector.T,
        second_cross_projector.T,
        outer_weight,
    )
    alignment_output, pair_rows = pl.pallas_call(
        finish,
        out_shape=(
            jax.ShapeDtypeStruct((4, 4, 128, 256), BF),
            jax.ShapeDtypeStruct((1024, 128), BF),
        ),
        in_specs=[hbm] * 4,
        out_specs=(hbm, hbm),
        scratch_shapes=[
            pltpu.VMEM((4, 4, 128, 256), BF),
            pltpu.VMEM((4, 256, 128), BF),
            pltpu.VMEM((1024, 128), BF),
            pltpu.VMEM((2, 128), jnp.int32),
            pltpu.VMEM((1024, 128), BF),
            pltpu.SemaphoreType.DMA((7,)),
            pltpu.SemaphoreType.DMA((5,)),
        ],
        compiler_params=pltpu.CompilerParams(vmem_limit_bytes=60 * 1024 * 1024),
    )(gathered, update, pairwise_state.reshape(1024, 128), alignment_row_mask.reshape(2, 128))
    return alignment_output.reshape(16, 128, 256), pair_rows.reshape(128, 8, 128)


def solution(mesh):
    placed = (
        P("seq", "ri", None),
        P("ri", ("seq", "rj"), None),
        P(),
        P(),
        P(),
        P(None, "rj"),
        P(None, "rj"),
        P(None, "rj"),
        P(None, "rj"),
        P(),
        P("rj", None),
        P(),
        P(),
        P(),
        P(),
        P(),
        P(),
    )
    return jax.shard_map(
        on_device,
        mesh=mesh,
        in_specs=placed,
        out_specs=(P("seq", "ri", None), P("ri", ("seq", "rj"), None)),
        check_vma=False,
    )
```

```python
import jax
import jax.numpy as jnp
from jax import lax
from jax.experimental import pallas as pl
from jax.experimental.pallas import tpu as pltpu
from jax.sharding import PartitionSpec as P

F32 = jnp.float32
BF = jnp.bfloat16
NT = (((1,), (1,)), ((), ()))

SIZES = (8, 8, 4, 4, 6, 1, 1, 6, 6, 24, 1, 1, 6, 6, 3)
RZ, XZ, XM, XF, WT, BA, BB, AX, BY, AL, LL, RR, LX, R4, UP = (
    sum(SIZES[:i]) for i in range(len(SIZES))
)
COUNT = sum(SIZES)


def nt(a, b):
    return lax.dot_general(a, b, NT, preferred_element_type=F32)


def mm(a, b):
    return jnp.dot(a, b, preferred_element_type=F32)


def norm(values, gain):
    centre = values - jnp.mean(values, -1, keepdims=True)
    spread = jnp.mean(centre * centre, -1, keepdims=True)
    return centre * lax.rsqrt(spread + 1e-5) * gain


def eye(n):
    row = lax.broadcasted_iota(jnp.int32, (n, n), 0)
    col = lax.broadcasted_iota(jnp.int32, (n, n), 1)
    return (row == col).astype(F32).astype(BF)


def kernel(
    hom, pair_in, resm_in, rows_in, fscale_in, wq, wk, wv, wg, gb_in, wo, pgain_in, bw_in,
    cscale_in, p1_in, p2_in, ow_in,
    out_al, out_update,
    xin, pair, resm, rows, fscale, gb, pgain, bw, cscale, p1, p2, ow,
    xn, relay, wbuf, pn, bt, bg, wkn, wqvg, kb, qt, vt, gate, biasb, gbt, cm, wst, al, right, sndf, snd, lraw, rraw, scr, lb, rb,
    bscr, ub, ubf, ugot,
    ssem, rsem, lsem, osem, usem,
):
    seq = lax.axis_index("seq")
    ri = lax.axis_index("ri")
    rj = lax.axis_index("rj")
    zl, x = lax.div(seq, 4), lax.rem(seq, 4)
    mate = ri + 1 - 2 * lax.rem(ri, 2)
    opp = lax.rem(ri + 2, 4)
    oppmate = lax.rem(mate + 2, 4)

    def ahead(v, d):
        return lax.rem(v + d, 4)

    def behind(v, d):
        return lax.rem(v + 4 - d, 4)

    plus_y, minus_y = {"rj": ahead(rj, 1)}, {"rj": behind(rj, 1)}
    plus_x, minus_x = {"seq": zl * 4 + ahead(x, 1)}, {"seq": zl * 4 + behind(x, 1)}
    core, z = lax.rem(ri, 2), lax.div(ri, 2) * 4 + zl

    def along_z(step):
        to = lax.rem(z + step, 8)
        return lax.div(to, 4) * 2 + core, {
            "seq": lax.rem(to, 4) * 4 + x,
            "ri": lax.div(to, 4) * 2 + core,
        }

    ri_up, up = along_z(2)
    ri_down, down = along_z(6)

    def seq_of(zz, xx):
        return zz * 4 + xx

    def in_zy(n):
        return {"seq": seq_of(ahead(zl, lax.div(n, 4)), x), "rj": ahead(rj, lax.rem(n, 4))}

    def in_zx(n):
        return {"seq": seq_of(ahead(zl, lax.div(n, 4)), ahead(x, lax.rem(n, 4)))}

    def right_to(n):
        return {"seq": seq_of(ri, lax.div(n, 4)), "ri": lax.rem(n, 4), "rj": x}

    def right_from(n):
        return {"seq": seq_of(lax.div(n, 4), rj), "ri": zl, "rj": lax.rem(n, 4)}

    def each(low, high, body):
        def step(n, carry):
            body(n)
            return carry

        lax.fori_loop(low, high, step, 0)

    diagonal = jnp.logical_and(zl == ri, x == rj)

    def to_self(n):
        return jnp.logical_and(diagonal, n == seq_of(x, ri))

    def from_self(n):
        return jnp.logical_and(diagonal, n == seq_of(zl, rj))


    def rcopy(src, dst, k, dev, send=None):
        return pltpu.make_async_remote_copy(
            src_ref=src,
            dst_ref=dst,
            send_sem=ssem.at[k if send is None else send],
            recv_sem=rsem.at[k],
            device_id=dev,
            device_id_type=pl.DeviceIdType.MESH,
        )

    def arrived(ref, k):
        pltpu.make_async_copy(ref, ref, rsem.at[k]).wait()

    def left_here(ref, k):
        pltpu.make_async_copy(ref, ref, ssem.at[k]).wait()

    def ring_start(own, lower, upper, k, plus, minus):
        for i, (part, dev) in enumerate(
            ((lower, plus), (upper, minus), (upper, plus), (lower, minus))
        ):
            rcopy(part(own), part(own), k + i, dev).start()

    def ring_pass(before, after, lower, upper, k, plus, minus):
        arrived(lower(before), k)
        rcopy(lower(before), lower(before), k + 4, plus).start()
        arrived(upper(after), k + 1)
        rcopy(upper(after), upper(after), k + 5, minus).start()

    def ring_end(before, after, far, lower, upper, k):
        arrived(upper(before), k + 2)
        arrived(lower(after), k + 3)
        arrived(lower(far), k + 4)
        arrived(upper(far), k + 5)

    def ring_sent(own, lower, upper, k):
        for i, part in enumerate((lower, upper, upper, lower, lower, upper)):
            left_here(part(own), k + i)

    def first(n):
        return lambda ref: ref.at[pl.ds(0, n)]

    def second(n):
        return lambda ref: ref.at[pl.ds(n, n)]

    inward = [
        (hom.at[pl.ds(rj * 4, 4)], xin),
        (fscale_in, fscale),
        (pair_in, pair),
        (pgain_in, pgain),
        (bw_in, bw),
        (wq, wbuf.at[rj, pl.ds(0, 64)]),
        (wk, wbuf.at[rj, pl.ds(64, 64)]),
        (wv, wbuf.at[rj, pl.ds(128, 64)]),
        (wg, wbuf.at[rj, pl.ds(192, 64)]),
        (wo, wbuf.at[rj, pl.ds(256, 64)]),
        (resm_in, resm),
        (rows_in, rows),
        (gb_in, gb),
        (cscale_in, cscale),
        (p1_in, p1),
        (p2_in, p2),
        (ow_in, ow),
    ]

    def local(k):
        return pltpu.make_async_copy(inward[k][0], inward[k][1], lsem.at[k])

    for k in range(len(inward)):
        local(k).start()

    barrier = pltpu.get_barrier_semaphore()

    def greet(dev):
        pl.semaphore_signal(barrier, inc=1, device_id=dev, device_id_type=pl.DeviceIdType.MESH)

    def greet_all(n):
        greet(in_zy(n))
        greet(in_zx(n))

    each(1, 16, greet_all)
    for dev in ({"ri": mate}, up, down):
        greet(dev)

    def greet_right(n):
        @pl.when(jnp.logical_not(from_self(n)))
        def _():
            greet(right_from(n))

    each(0, 16, greet_right)

    local(0).wait()
    local(1).wait()

    def norm_x(s, carry):
        xn[s, ri] = norm(xin[s].astype(F32), fscale[...]).astype(BF)
        return carry

    lax.fori_loop(0, 4, norm_x, 0)

    for k in range(2, 5):
        local(k).wait()
    pn[...] = norm(pair[...].astype(F32), pgain[...]).astype(BF).astype(F32)
    for j in range(8):
        tile = pn[pl.ds(j, 128, stride=8), :].astype(BF)
        bt[pl.ds(j, 8, stride=8), :] = nt(bw[...], tile)
    for half in range(2):
        bg[half, zl, x, rj] = bt[pl.ds(half * 32, 32), :].astype(BF)

    pl.semaphore_wait(barrier, 49 - diagonal.astype(jnp.int32))

    def send_x(s):
        rcopy(xn.at[s, ri, pl.ds(0, 64)], relay.at[0, s], RZ + s * 2, up).start()
        rcopy(xn.at[s, ri, pl.ds(64, 64)], relay.at[1, s], RZ + s * 2 + 1, down).start()

    def relay_x(s):
        arrived(relay.at[0, s], RZ + s * 2)
        rcopy(relay.at[0, s], xn.at[s, ri_down, pl.ds(0, 64)], XZ + s * 2, up).start()
        arrived(relay.at[1, s], RZ + s * 2 + 1)
        rcopy(relay.at[1, s], xn.at[s, ri_up, pl.ds(64, 64)], XZ + s * 2 + 1, down).start()

    def send_bias(n):
        rcopy(bg.at[0, zl, x, rj], bg.at[0, zl, x, rj], BA, in_zy(n)).start()
        rcopy(bg.at[1, zl, x, rj], bg.at[1, zl, x, rj], BB, in_zx(n)).start()

    each(1, 16, send_bias)
    for s in range(4):
        send_x(s)
    for s in range(4):
        rcopy(xn.at[s, ri], xn.at[s, ri], XM + s, {"ri": mate}).start()
    for k in range(5, 10):
        local(k).wait()
    w_lower, w_upper = first(160), second(160)
    ring_start(wbuf.at[rj], w_lower, w_upper, WT, plus_y, minus_y)
    for k in range(10, len(inward)):
        local(k).wait()

    row128 = lax.broadcasted_iota(jnp.int32, (128, 128), 0)
    col128 = lax.broadcasted_iota(jnp.int32, (128, 128), 1)
    ones = jnp.ones((128, 128), BF)
    for b in range(4):
        res = resm[pl.ds(b, 1), :].astype(F32)
        spread = jnp.where(row128 == col128, jnp.broadcast_to(res, (128, 128)), 0.0).astype(BF)
        cm[b] = mm(spread, ones)
    for b in range(2):
        gbt[pl.ds(b * 128, 128), :] = jnp.transpose(
            jnp.broadcast_to(gb[:, pl.ds(b * 128, 128)], (128, 128))
        )
    e128 = eye(128)
    for k in range(4):
        wst[pl.ds(k * 128, 128), :] = nt(e128, ow[pl.ds(k * 256, 256), :]).astype(BF)
    pick = (
        lax.broadcasted_iota(jnp.int32, (32, 128), 0)
        == lax.rem(lax.broadcasted_iota(jnp.int32, (32, 128), 1), 32)
    ).astype(F32).astype(BF)
    p1t = p1[...]
    p2r = jnp.concatenate([p2[...]] * 4, 0)

    fifteen, sixteen = bscr.at[0, 0, pl.ds(0, 240)], bscr.at[0, 0]
    arrived(fifteen, BA)
    arrived(fifteen, BB)
    b_lower, b_upper = first(2), second(2)
    ring_start(bg.at[0, :, x], b_lower, b_upper, AX, plus_x, minus_x)
    ring_start(bg.at[1, :, :, rj], b_lower, b_upper, BY, plus_y, minus_y)
    relay_x(0)
    relay_x(1)
    ring_pass(
        wbuf.at[behind(rj, 1)], wbuf.at[ahead(rj, 1)], w_lower, w_upper, WT, plus_y, minus_y
    )
    relay_x(2)
    relay_x(3)
    ring_pass(
        bg.at[0, :, behind(x, 1)], bg.at[0, :, ahead(x, 1)], b_lower, b_upper, AX, plus_x, minus_x
    )
    ring_pass(
        bg.at[1, :, :, behind(rj, 1)], bg.at[1, :, :, ahead(rj, 1)], b_lower, b_upper,
        BY, plus_y, minus_y,
    )

    ring_end(
        wbuf.at[behind(rj, 1)], wbuf.at[ahead(rj, 1)], wbuf.at[ahead(rj, 2)], w_lower, w_upper, WT
    )

    def weight(k):
        return wbuf[:, pl.ds(k * 64, 64), :].reshape(256, 256)

    wkn[...] = nt(eye(256), weight(1)).astype(BF)
    wqvg[0:256] = weight(0)
    wqvg[256:512] = weight(2)
    wqvg[512:768] = weight(3)

    def own_rows(s, carry):
        block = xn[s, ri]
        kb[s, ri] = mm(block, wkn[...]).astype(BF)
        three = nt(wqvg[...], block)
        qt[s] = (three[0:256] * 32 ** -0.5).astype(BF)
        vt[s, ri] = three[256:512].astype(BF)
        gate[s] = jax.nn.sigmoid(three[512:768] + gbt[...])
        return carry

    def other_rows(s, b):
        block = xn[s, b]
        kb[s, b] = mm(block, wkn[...]).astype(BF)
        vt[s, b] = nt(wqvg[256:512], block).astype(BF)

    lax.fori_loop(0, 4, own_rows, 0)

    def near_rows(s, carry):
        arrived(xn.at[s, mate], XM + s)
        other_rows(s, mate)
        return carry

    def far_rows(s, carry):
        arrived(xn.at[s, opp, pl.ds(0, 64)], XZ + s * 2)
        arrived(xn.at[s, opp, pl.ds(64, 64)], XZ + s * 2 + 1)
        rcopy(xn.at[s, opp], xn.at[s, opp], XF + s, {"ri": mate}).start()
        other_rows(s, opp)
        return carry

    def last_rows(s, carry):
        arrived(xn.at[s, oppmate], XF + s)
        other_rows(s, oppmate)
        return carry

    lax.fori_loop(0, 4, near_rows, 0)
    lax.fori_loop(0, 2, far_rows, 0)
    ring_end(
        bg.at[0, :, behind(x, 1)], bg.at[0, :, ahead(x, 1)], bg.at[0, :, ahead(x, 2)],
        b_lower, b_upper, AX,
    )
    ring_end(
        bg.at[1, :, :, behind(rj, 1)], bg.at[1, :, :, ahead(rj, 1)], bg.at[1, :, :, ahead(rj, 2)],
        b_lower, b_upper, BY,
    )

    keymask = (jnp.concatenate([cm[b] for b in range(4)], 0) - 1.0) * 1e9
    for hp in range(4):
        two = bg[hp // 2, :, :, :, pl.ds(hp % 2 * 16, 16), :].astype(F32).reshape(64, 2, 8, 128)
        for h in range(2):
            biasb[hp, :, pl.ds(h * 128, 128)] = (two[:, h].reshape(512, 128) + keymask).astype(F32)

    lane8 = lax.div(lax.broadcasted_iota(jnp.int32, (8, 128), 1), 32)

    def heads(s):
        key = kb[s].reshape(512, 256)
        value = jnp.concatenate([vt[s, b] for b in range(4)], 1)
        query = qt[s]
        parts = []
        for hp in range(4):
            g, r = hp // 2, hp % 2 * 2
            zero = jnp.zeros((32, 128), BF)
            pair_q = []
            for h in range(2):
                pieces = [zero] * 4
                pieces[r + h] = query[hp * 64 + h * 32 : hp * 64 + h * 32 + 32]
                pair_q.append(jnp.concatenate(pieces, 0))
            logits = mm(key[:, g * 128 : g * 128 + 128], jnp.concatenate(pair_q, 1)) + biasb[hp]
            low = logits - jnp.max(logits, 0, keepdims=True)
            probs = jnp.exp(low).astype(BF)
            summed = mm(
                jnp.concatenate([value[hp * 64 : hp * 64 + 64], jnp.ones((16, 512), BF)], 0), probs
            )
            scale = 1.0 / summed[64:65]
            parts.append(summed[0:32, 0:128] * scale[:, 0:128])
            parts.append(summed[32:64, 128:256] * scale[:, 128:256])
        return (jnp.concatenate(parts, 0) * gate[s]).astype(BF)

    def project(s, attended):
        attended = nt(e128, attended).astype(BF)
        result = (xin[s].astype(F32) + mm(attended, weight(4))).astype(BF)
        al[rj, s] = result
        on = norm(result.astype(F32), cscale[...])
        keep = cm[ri] * rows[seq * 16 + rj * 4 + s].astype(F32)
        on = (on * jnp.concatenate([keep, keep], 1)).astype(BF)
        left = nt(p1t, on)
        right[...] = nt(on, p2r)
        for y in range(4):
            ltile = jnp.zeros((8, 128), F32)
            rtile = jnp.zeros((8, 128), F32)
            for k in range(4):
                piece = left[k * 8 : k * 8 + 8]
                if k != y:
                    piece = pltpu.roll(piece, (32 * (k - y)) % 128, 1)
                ltile = jnp.where(lane8 == k, piece, ltile)
                rtile = jnp.where(lane8 == k, right[pl.ds(y * 32 + k, 8, stride=4), :], rtile)
            sndf[y, pl.ds(pl.multiple_of(s * 8, 8), 8), :] = ltile
            sndf[y, pl.ds(pl.multiple_of(32 + s * 8, 8), 8), :] = rtile

    def attend(s, before):
        last_rows(s, 0)
        attended = heads(s)
        project(lax.rem(s + 3, 4), before)

        @pl.when(s > 0)
        def _():
            start_out(s - 1)

        @pl.when(s < 2)
        def _():
            far_rows(s + 2, 0)

        return attended

    a_lower, a_upper = first(64), second(64)

    def out(s, source):
        return al.at[source, s]

    def start_out(s):
        for i, (part, dev) in enumerate(
            ((a_lower, plus_y), (a_upper, minus_y), (a_upper, plus_y), (a_lower, minus_y))
        ):
            rcopy(part(out(s, rj)), part(out(s, rj)), AL + s * 6 + i, dev).start()

    def pass_out(s):
        ring_pass(
            out(s, behind(rj, 1)), out(s, ahead(rj, 1)), a_lower, a_upper, AL + s * 6,
            plus_y, minus_y,
        )

    project(3, lax.fori_loop(0, 4, attend, jnp.zeros((256, 128), BF)))

    snd[...] = sndf[...].astype(BF)

    def send_sides(n):
        rcopy(
            snd.at[ahead(rj, lax.rem(n, 4)), pl.ds(0, 32)], lraw.at[zl, rj], LL, in_zy(n)
        ).start()

    each(1, 16, send_sides)

    def send_right(n):
        @pl.when(jnp.logical_not(to_self(n)))
        def _():
            rcopy(
                snd.at[lax.div(n, 4), pl.ds(32, 32)], rraw.at[zl, rj], RR, right_to(n)
            ).start()

    each(0, 16, send_right)
    each(0, 2, pass_out)
    start_out(3)
    lraw[zl, rj] = snd[rj, 0:32]

    @pl.when(diagonal)
    def _():
        rraw[zl, rj] = snd[x, 32:64]

    def drain_head(s):
        for half in range(2):
            left_here(relay.at[half, s], RZ + s * 2 + half)
            left_here(relay.at[half, s], XZ + s * 2 + half)
        left_here(xn.at[s, ri], XM + s)
        left_here(xn.at[s, opp], XF + s)

    each(0, 4, drain_head)
    left_here(fifteen, BA)
    left_here(fifteen, BB)
    ring_sent(wbuf.at[rj], w_lower, w_upper, WT)
    ring_sent(bg.at[0, :, x], b_lower, b_upper, AX)
    ring_sent(bg.at[1, :, :, rj], b_lower, b_upper, BY)

    def regroup(raw, buf, place):
        def step(t):
            block = raw[t].astype(F32)
            for y in range(4):
                for s in range(4):
                    scr[pl.ds(y * 4 + s, 8, stride=16), :] = block[y, s * 8 : s * 8 + 8]
            buf[:, place, t] = scr[...].astype(BF).reshape(8, 16, 128)

        each(0, 4, step)

    q_lower, q_upper = first(4), second(4)
    arrived(fifteen, LL)
    regroup(lraw, lb, x)
    ring_start(lb.at[:, x], q_lower, q_upper, LX, plus_x, minus_x)

    @pl.when(diagonal)
    def _():
        arrived(fifteen, RR)

    @pl.when(jnp.logical_not(diagonal))
    def _():
        arrived(sixteen, RR)

    regroup(rraw, rb, rj)
    ring_start(rb.at[:, rj], q_lower, q_upper, R4, plus_y, minus_y)
    ring_pass(
        lb.at[:, behind(x, 1)], lb.at[:, ahead(x, 1)], q_lower, q_upper, LX, plus_x, minus_x
    )
    ring_pass(
        rb.at[:, behind(rj, 1)], rb.at[:, ahead(rj, 1)], q_lower, q_upper, R4, plus_y, minus_y
    )
    each(2, 4, pass_out)
    ring_end(
        lb.at[:, behind(x, 1)], lb.at[:, ahead(x, 1)], lb.at[:, ahead(x, 2)], q_lower, q_upper, LX
    )
    ring_end(
        rb.at[:, behind(rj, 1)], rb.at[:, ahead(rj, 1)], rb.at[:, ahead(rj, 2)],
        q_lower, q_upper, R4,
    )

    lane128 = lax.div(lax.broadcasted_iota(jnp.int32, (128, 128), 1), 32)

    def product(peer, u):
        turned = nt(e128, rb[peer * 2 + u].reshape(256, 128)).astype(BF)
        for k in range(8):
            outer = mm(turned, lb[k].reshape(256, 128)).astype(BF)
            for j in range(4):
                bscr[u, j // 2, pl.ds(k * 32, 32), pl.ds((j % 2) * 128, 128)] = outer[
                    j * 32 : j * 32 + 32
                ]
        for jp in range(2):
            wide = mm(wst[...], bscr[u, jp])
            for half in range(2):
                c = half * 128
                mixed = wide[0:128, c : c + 128]
                for k in range(1, 4):
                    mixed = jnp.where(
                        lane128 == k, wide[k * 128 : k * 128 + 128, c : c + 128], mixed
                    )
                ub[peer, pl.ds(u * 4 + jp * 2 + half, 32, stride=8), :] = nt(
                    pick, mixed.astype(BF)
                )

    def in_order(t):
        return jnp.where(t == 0, 2, jnp.where(t == 1, 1, t + 1))

    def for_peer(t):
        d = in_order(t)
        peer = ahead(rj, d)
        for u in range(2):
            product(peer, u)
        ubf[peer] = ub[peer].astype(BF)

        @pl.when(t < 3)
        def _():
            update_copy(d).start()

    def update_copy(d):
        peer = ahead(rj, d)
        return rcopy(ubf.at[peer], ugot.at[rj], UP + d - 1, {"rj": peer})

    each(0, 4, for_peer)
    ugot[rj] = ubf[rj]
    each(1, 4, lambda d: arrived(ugot.at[behind(rj, d)], UP + d - 1))
    keep = pltpu.make_async_copy(ugot, out_update, usem)
    keep.start()

    def write_out(s):
        return pltpu.make_async_copy(al.at[:, s], out_al.at[:, s], osem.at[s])

    def drain(s):
        ring_end(
            out(s, behind(rj, 1)), out(s, ahead(rj, 1)), out(s, ahead(rj, 2)), a_lower, a_upper,
            AL + s * 6,
        )
        write_out(s).start()

    each(0, 4, drain)
    each(0, 4, lambda s: ring_sent(out(s, rj), a_lower, a_upper, AL + s * 6))
    ring_sent(lb.at[:, x], q_lower, q_upper, LX)
    ring_sent(rb.at[:, rj], q_lower, q_upper, R4)
    left_here(fifteen, LL)

    @pl.when(diagonal)
    def _():
        left_here(fifteen, RR)

    @pl.when(jnp.logical_not(diagonal))
    def _():
        left_here(sixteen, RR)

    each(1, 4, lambda d: left_here(ubf.at[ahead(rj, d)], UP + d - 1))
    keep.wait()
    each(0, 4, lambda s: write_out(s).wait())


def finish(
    al_in, update_in, pair_in, rowv_in, al_out, pair_out, al, update, pair, rowv, result, sem, back
):
    inward = [
        pltpu.make_async_copy(update_in, update, sem.at[0]),
        pltpu.make_async_copy(pair_in, pair, sem.at[1]),
        pltpu.make_async_copy(rowv_in, rowv, sem.at[2]),
    ] + [pltpu.make_async_copy(al_in.at[k], al.at[k], sem.at[3 + k]) for k in range(4)]
    outward = [pltpu.make_async_copy(al.at[k], al_out.at[k], back.at[k]) for k in range(4)]
    outward.append(pltpu.make_async_copy(result, pair_out, back.at[4]))
    for copy in inward:
        copy.start()
    for k in range(3):
        inward[k].wait()
    scale = 1.0 / jnp.maximum(jnp.sum(rowv[...].astype(F32)), 1.0)
    result[...] = (
        pair[...].astype(F32) + update[...].reshape(1024, 128).astype(F32) * scale
    ).astype(BF)
    outward[4].start()
    for k in range(4):
        inward[3 + k].wait()
        outward[k].start()
    for copy in outward:
        copy.wait()


def on_device(
    homolog_embedding,
    pairwise_state,
    residue_mask,
    alignment_row_mask,
    focus_layer_scale,
    asking_projector,
    lookup_projector,
    content_projector,
    sigmoid_projector,
    gate_offset_bias,
    final_projector,
    pairwise_norm_gain,
    bias_weight,
    cross_layer_scale,
    first_cross_projector,
    second_cross_projector,
    outer_weight,
):
    hbm = pl.BlockSpec(memory_space=pl.ANY)
    gathered, update = pl.pallas_call(
        kernel,
        out_shape=(
            jax.ShapeDtypeStruct((4, 4, 128, 256), BF),
            jax.ShapeDtypeStruct((4, 256, 128), BF),
        ),
        in_specs=[hbm] * 17,
        out_specs=(hbm, hbm),
        scratch_shapes=[
            pltpu.VMEM((4, 128, 256), BF),
            pltpu.VMEM((1024, 128), BF),
            pltpu.VMEM((4, 128), jnp.int32),
            pltpu.SMEM((256,), jnp.int32),
            pltpu.VMEM((1, 256), F32),
            pltpu.VMEM((1, 256), F32),
            pltpu.VMEM((1, 128), F32),
            pltpu.VMEM((8, 128), BF),
            pltpu.VMEM((1, 256), F32),
            pltpu.VMEM((32, 256), BF),
            pltpu.VMEM((32, 256), BF),
            pltpu.VMEM((1024, 128), BF),
            pltpu.VMEM((4, 4, 128, 256), BF),
            pltpu.VMEM((2, 4, 64, 256), BF),
            pltpu.VMEM((4, 320, 256), BF),
            pltpu.VMEM((1024, 128), F32),
            pltpu.VMEM((64, 128), F32),
            pltpu.VMEM((2, 4, 4, 4, 32, 128), BF),
            pltpu.VMEM((256, 256), BF),
            pltpu.VMEM((768, 256), BF),
            pltpu.VMEM((4, 4, 128, 256), BF),
            pltpu.VMEM((4, 256, 128), BF),
            pltpu.VMEM((4, 4, 256, 128), BF),
            pltpu.VMEM((4, 256, 128), F32),
            pltpu.VMEM((4, 512, 256), F32),
            pltpu.VMEM((256, 128), F32),
            pltpu.VMEM((4, 128, 128), F32),
            pltpu.VMEM((512, 256), BF),
            pltpu.VMEM((4, 4, 128, 256), BF),
            pltpu.VMEM((128, 128), F32),
            pltpu.VMEM((4, 64, 128), F32),
            pltpu.VMEM((4, 64, 128), BF),
            pltpu.VMEM((4, 4, 32, 128), BF),
            pltpu.VMEM((4, 4, 32, 128), BF),
            pltpu.VMEM((128, 128), F32),
            pltpu.VMEM((8, 4, 4, 16, 128), BF),
            pltpu.VMEM((8, 4, 4, 16, 128), BF),
            pltpu.VMEM((2, 2, 256, 256), BF),
            pltpu.VMEM((4, 256, 128), F32),
            pltpu.VMEM((4, 256, 128), BF),
            pltpu.VMEM((4, 256, 128), BF),
            pltpu.SemaphoreType.DMA((COUNT,)),
            pltpu.SemaphoreType.DMA((COUNT,)),
            pltpu.SemaphoreType.DMA((17,)),
            pltpu.SemaphoreType.DMA((4,)),
            pltpu.SemaphoreType.DMA,
        ],
        compiler_params=pltpu.CompilerParams(
            collective_id=0, has_side_effects=True, vmem_limit_bytes=60 * 1024 * 1024
        ),
        cost_estimate=pl.CostEstimate(
            flops=4_000_000_000, bytes_accessed=4_000_000, transcendentals=2_000_000
        ),
    )(
        homolog_embedding,
        pairwise_state.reshape(1024, 128),
        residue_mask.reshape(4, 128),
        alignment_row_mask,
        focus_layer_scale.reshape(1, 256),
        asking_projector.T,
        lookup_projector.T,
        content_projector.T,
        sigmoid_projector.T,
        gate_offset_bias.reshape(1, 256),
        final_projector,
        pairwise_norm_gain.reshape(1, 128),
        bias_weight.T,
        cross_layer_scale.reshape(1, 256),
        first_cross_projector.T,
        second_cross_projector.T,
        outer_weight,
    )
    alignment_output, pair_rows = pl.pallas_call(
        finish,
        out_shape=(
            jax.ShapeDtypeStruct((4, 4, 128, 256), BF),
            jax.ShapeDtypeStruct((1024, 128), BF),
        ),
        in_specs=[hbm] * 4,
        out_specs=(hbm, hbm),
        scratch_shapes=[
            pltpu.VMEM((4, 4, 128, 256), BF),
            pltpu.VMEM((4, 256, 128), BF),
            pltpu.VMEM((1024, 128), BF),
            pltpu.VMEM((2, 128), jnp.int32),
            pltpu.VMEM((1024, 128), BF),
            pltpu.SemaphoreType.DMA((7,)),
            pltpu.SemaphoreType.DMA((5,)),
        ],
        compiler_params=pltpu.CompilerParams(vmem_limit_bytes=60 * 1024 * 1024),
    )(gathered, update, pairwise_state.reshape(1024, 128), alignment_row_mask.reshape(2, 128))
    return alignment_output.reshape(16, 128, 256), pair_rows.reshape(128, 8, 128)


def solution(mesh):
    placed = (
        P("seq", "ri", None),
        P("ri", ("seq", "rj"), None),
        P(),
        P(),
        P(),
        P(None, "rj"),
        P(None, "rj"),
        P(None, "rj"),
        P(None, "rj"),
        P(),
        P("rj", None),
        P(),
        P(),
        P(),
        P(),
        P(),
        P(),
    )
    return jax.shard_map(
        on_device,
        mesh=mesh,
        in_specs=placed,
        out_specs=(P("seq", "ri", None), P("ri", ("seq", "rj"), None)),
        check_vma=False,
    )
```

```python
import jax
import jax.numpy as jnp
from jax import lax
from jax.experimental import pallas as pl
from jax.experimental.pallas import tpu as pltpu
from jax.sharding import PartitionSpec as P

F32 = jnp.float32
BF = jnp.bfloat16
NT = (((1,), (1,)), ((), ()))

SIZES = (8, 8, 4, 4, 6, 1, 1, 6, 6, 24, 1, 1, 6, 6, 3)
RZ, XZ, XM, XF, WT, BA, BB, AX, BY, AL, LL, RR, LX, R4, UP = (
    sum(SIZES[:i]) for i in range(len(SIZES))
)
COUNT = sum(SIZES)


def nt(a, b):
    return lax.dot_general(a, b, NT, preferred_element_type=F32)


def mm(a, b):
    return jnp.dot(a, b, preferred_element_type=F32)


def norm(values, gain):
    centre = values - jnp.mean(values, -1, keepdims=True)
    spread = jnp.mean(centre * centre, -1, keepdims=True)
    return centre * lax.rsqrt(spread + 1e-5) * gain


def eye(n):
    row = lax.broadcasted_iota(jnp.int32, (n, n), 0)
    col = lax.broadcasted_iota(jnp.int32, (n, n), 1)
    return (row == col).astype(F32).astype(BF)


def kernel(
    hom, pair_in, resm_in, rows_in, fscale_in, wq, wk, wv, wg, gb_in, wo, pgain_in, bw_in,
    cscale_in, p1_in, p2_in, ow_in,
    out_al, out_update,
    xin, pair, resm, rows, fscale, gb, pgain, bw, cscale, p1, p2, ow,
    xn, relay, wbuf, pn, bt, bg, wkn, wqvg, kb, qt, vt, gate, biasb, gbt, cm, wst, al, right, sndf, snd, lraw, rraw, scr, lb, rb,
    bscr, ub, ubf, ugot,
    ssem, rsem, lsem, osem, usem,
):
    seq = lax.axis_index("seq")
    ri = lax.axis_index("ri")
    rj = lax.axis_index("rj")
    zl, x = lax.div(seq, 4), lax.rem(seq, 4)
    mate = ri + 1 - 2 * lax.rem(ri, 2)
    opp = lax.rem(ri + 2, 4)
    oppmate = lax.rem(mate + 2, 4)

    def ahead(v, d):
        return lax.rem(v + d, 4)

    def behind(v, d):
        return lax.rem(v + 4 - d, 4)

    plus_y, minus_y = {"rj": ahead(rj, 1)}, {"rj": behind(rj, 1)}
    plus_x, minus_x = {"seq": zl * 4 + ahead(x, 1)}, {"seq": zl * 4 + behind(x, 1)}
    core, z = lax.rem(ri, 2), lax.div(ri, 2) * 4 + zl

    def along_z(step):
        to = lax.rem(z + step, 8)
        return lax.div(to, 4) * 2 + core, {
            "seq": lax.rem(to, 4) * 4 + x,
            "ri": lax.div(to, 4) * 2 + core,
        }

    ri_up, up = along_z(2)
    ri_down, down = along_z(6)

    def seq_of(zz, xx):
        return zz * 4 + xx

    def in_zy(n):
        return {"seq": seq_of(ahead(zl, lax.div(n, 4)), x), "rj": ahead(rj, lax.rem(n, 4))}

    def in_zx(n):
        return {"seq": seq_of(ahead(zl, lax.div(n, 4)), ahead(x, lax.rem(n, 4)))}

    def right_to(n):
        return {"seq": seq_of(ri, lax.div(n, 4)), "ri": lax.rem(n, 4), "rj": x}

    def right_from(n):
        return {"seq": seq_of(lax.div(n, 4), rj), "ri": zl, "rj": lax.rem(n, 4)}

    def each(low, high, body):
        def step(n, carry):
            body(n)
            return carry

        lax.fori_loop(low, high, step, 0)

    diagonal = jnp.logical_and(zl == ri, x == rj)

    def to_self(n):
        return jnp.logical_and(diagonal, n == seq_of(x, ri))

    def from_self(n):
        return jnp.logical_and(diagonal, n == seq_of(zl, rj))


    def rcopy(src, dst, k, dev, send=None):
        return pltpu.make_async_remote_copy(
            src_ref=src,
            dst_ref=dst,
            send_sem=ssem.at[k if send is None else send],
            recv_sem=rsem.at[k],
            device_id=dev,
            device_id_type=pl.DeviceIdType.MESH,
        )

    def arrived(ref, k):
        pltpu.make_async_copy(ref, ref, rsem.at[k]).wait()

    def left_here(ref, k):
        pltpu.make_async_copy(ref, ref, ssem.at[k]).wait()

    def ring_start(own, lower, upper, k, plus, minus):
        for i, (part, dev) in enumerate(
            ((lower, plus), (upper, minus), (upper, plus), (lower, minus))
        ):
            rcopy(part(own), part(own), k + i, dev).start()

    def ring_pass(before, after, lower, upper, k, plus, minus):
        arrived(lower(before), k)
        rcopy(lower(before), lower(before), k + 4, plus).start()
        arrived(upper(after), k + 1)
        rcopy(upper(after), upper(after), k + 5, minus).start()

    def ring_end(before, after, far, lower, upper, k):
        arrived(upper(before), k + 2)
        arrived(lower(after), k + 3)
        arrived(lower(far), k + 4)
        arrived(upper(far), k + 5)

    def ring_sent(own, lower, upper, k):
        for i, part in enumerate((lower, upper, upper, lower, lower, upper)):
            left_here(part(own), k + i)

    def first(n):
        return lambda ref: ref.at[pl.ds(0, n)]

    def second(n):
        return lambda ref: ref.at[pl.ds(n, n)]

    inward = [
        (hom.at[pl.ds(rj * 4, 4)], xin),
        (fscale_in, fscale),
        (pair_in, pair),
        (pgain_in, pgain),
        (bw_in, bw),
        (wq, wbuf.at[rj, pl.ds(0, 64)]),
        (wk, wbuf.at[rj, pl.ds(64, 64)]),
        (wv, wbuf.at[rj, pl.ds(128, 64)]),
        (wg, wbuf.at[rj, pl.ds(192, 64)]),
        (wo, wbuf.at[rj, pl.ds(256, 64)]),
        (resm_in, resm),
        (rows_in, rows),
        (gb_in, gb),
        (cscale_in, cscale),
        (p1_in, p1),
        (p2_in, p2),
        (ow_in, ow),
    ]

    def local(k):
        return pltpu.make_async_copy(inward[k][0], inward[k][1], lsem.at[k])

    for k in range(len(inward)):
        local(k).start()

    barrier = pltpu.get_barrier_semaphore()

    def greet(dev):
        pl.semaphore_signal(barrier, inc=1, device_id=dev, device_id_type=pl.DeviceIdType.MESH)

    def greet_all(n):
        greet(in_zy(n))
        greet(in_zx(n))

    each(1, 16, greet_all)
    for dev in ({"ri": mate}, up, down):
        greet(dev)

    def greet_right(n):
        @pl.when(jnp.logical_not(from_self(n)))
        def _():
            greet(right_from(n))

    each(0, 16, greet_right)

    local(0).wait()
    local(1).wait()

    def norm_x(s, carry):
        xn[s, ri] = norm(xin[s].astype(F32), fscale[...]).astype(BF)
        return carry

    lax.fori_loop(0, 4, norm_x, 0)

    for k in range(2, 5):
        local(k).wait()
    pn[...] = norm(pair[...].astype(F32), pgain[...]).astype(BF).astype(F32)
    for j in range(8):
        tile = pn[pl.ds(j, 128, stride=8), :].astype(BF)
        bt[pl.ds(j, 8, stride=8), :] = nt(bw[...], tile)
    for half in range(2):
        bg[half, zl, x, rj] = bt[pl.ds(half * 32, 32), :].astype(BF)

    pl.semaphore_wait(barrier, 49 - diagonal.astype(jnp.int32))

    def send_x(s):
        rcopy(xn.at[s, ri, pl.ds(0, 64)], relay.at[0, s], RZ + s * 2, up).start()
        rcopy(xn.at[s, ri, pl.ds(64, 64)], relay.at[1, s], RZ + s * 2 + 1, down).start()

    def relay_x(s):
        arrived(relay.at[0, s], RZ + s * 2)
        rcopy(relay.at[0, s], xn.at[s, ri_down, pl.ds(0, 64)], XZ + s * 2, up).start()
        arrived(relay.at[1, s], RZ + s * 2 + 1)
        rcopy(relay.at[1, s], xn.at[s, ri_up, pl.ds(64, 64)], XZ + s * 2 + 1, down).start()

    def send_bias(n):
        rcopy(bg.at[0, zl, x, rj], bg.at[0, zl, x, rj], BA, in_zy(n)).start()
        rcopy(bg.at[1, zl, x, rj], bg.at[1, zl, x, rj], BB, in_zx(n)).start()

    each(1, 16, send_bias)
    for s in range(4):
        send_x(s)
    for s in range(4):
        rcopy(xn.at[s, ri], xn.at[s, ri], XM + s, {"ri": mate}).start()
    for k in range(5, 10):
        local(k).wait()
    w_lower, w_upper = first(160), second(160)
    ring_start(wbuf.at[rj], w_lower, w_upper, WT, plus_y, minus_y)
    for k in range(10, len(inward)):
        local(k).wait()

    row128 = lax.broadcasted_iota(jnp.int32, (128, 128), 0)
    col128 = lax.broadcasted_iota(jnp.int32, (128, 128), 1)
    ones = jnp.ones((128, 128), BF)
    for b in range(4):
        res = resm[pl.ds(b, 1), :].astype(F32)
        spread = jnp.where(row128 == col128, jnp.broadcast_to(res, (128, 128)), 0.0).astype(BF)
        cm[b] = mm(spread, ones)
    for b in range(2):
        gbt[pl.ds(b * 128, 128), :] = jnp.transpose(
            jnp.broadcast_to(gb[:, pl.ds(b * 128, 128)], (128, 128))
        )
    e128 = eye(128)
    for k in range(4):
        wst[pl.ds(k * 128, 128), :] = nt(e128, ow[pl.ds(k * 256, 256), :]).astype(BF)
    pick = (
        lax.broadcasted_iota(jnp.int32, (32, 128), 0)
        == lax.rem(lax.broadcasted_iota(jnp.int32, (32, 128), 1), 32)
    ).astype(F32).astype(BF)
    p1t = p1[...]
    p2r = jnp.concatenate([p2[...]] * 4, 0)

    fifteen, sixteen = bscr.at[0, 0, pl.ds(0, 240)], bscr.at[0, 0]
    arrived(fifteen, BA)
    arrived(fifteen, BB)
    b_lower, b_upper = first(2), second(2)
    ring_start(bg.at[0, :, x], b_lower, b_upper, AX, plus_x, minus_x)
    ring_start(bg.at[1, :, :, rj], b_lower, b_upper, BY, plus_y, minus_y)
    relay_x(0)
    relay_x(1)
    ring_pass(
        wbuf.at[behind(rj, 1)], wbuf.at[ahead(rj, 1)], w_lower, w_upper, WT, plus_y, minus_y
    )
    relay_x(2)
    relay_x(3)
    ring_pass(
        bg.at[0, :, behind(x, 1)], bg.at[0, :, ahead(x, 1)], b_lower, b_upper, AX, plus_x, minus_x
    )
    ring_pass(
        bg.at[1, :, :, behind(rj, 1)], bg.at[1, :, :, ahead(rj, 1)], b_lower, b_upper,
        BY, plus_y, minus_y,
    )

    ring_end(
        wbuf.at[behind(rj, 1)], wbuf.at[ahead(rj, 1)], wbuf.at[ahead(rj, 2)], w_lower, w_upper, WT
    )

    def weight(k):
        return wbuf[:, pl.ds(k * 64, 64), :].reshape(256, 256)

    wkn[...] = nt(eye(256), weight(1)).astype(BF)
    wqvg[0:256] = weight(0)
    wqvg[256:512] = weight(2)
    wqvg[512:768] = weight(3)

    def own_rows(s, carry):
        block = xn[s, ri]
        kb[s, ri] = mm(block, wkn[...]).astype(BF)
        three = nt(wqvg[...], block)
        qt[s] = (three[0:256] * 32 ** -0.5).astype(BF)
        vt[s, ri] = three[256:512].astype(BF)
        gate[s] = jax.nn.sigmoid(three[512:768] + gbt[...])
        return carry

    def other_rows(s, b):
        block = xn[s, b]
        kb[s, b] = mm(block, wkn[...]).astype(BF)
        vt[s, b] = nt(wqvg[256:512], block).astype(BF)

    lax.fori_loop(0, 4, own_rows, 0)

    def near_rows(s, carry):
        arrived(xn.at[s, mate], XM + s)
        other_rows(s, mate)
        return carry

    def far_rows(s, carry):
        arrived(xn.at[s, opp, pl.ds(0, 64)], XZ + s * 2)
        arrived(xn.at[s, opp, pl.ds(64, 64)], XZ + s * 2 + 1)
        rcopy(xn.at[s, opp], xn.at[s, opp], XF + s, {"ri": mate}).start()
        other_rows(s, opp)
        return carry

    def last_rows(s, carry):
        arrived(xn.at[s, oppmate], XF + s)
        other_rows(s, oppmate)
        return carry

    lax.fori_loop(0, 4, near_rows, 0)
    lax.fori_loop(0, 2, far_rows, 0)
    ring_end(
        bg.at[0, :, behind(x, 1)], bg.at[0, :, ahead(x, 1)], bg.at[0, :, ahead(x, 2)],
        b_lower, b_upper, AX,
    )
    ring_end(
        bg.at[1, :, :, behind(rj, 1)], bg.at[1, :, :, ahead(rj, 1)], bg.at[1, :, :, ahead(rj, 2)],
        b_lower, b_upper, BY,
    )

    keymask = (jnp.concatenate([cm[b] for b in range(4)], 0) - 1.0) * 1e9
    for hp in range(4):
        two = bg[hp // 2, :, :, :, pl.ds(hp % 2 * 16, 16), :].astype(F32).reshape(64, 2, 8, 128)
        for h in range(2):
            biasb[hp, :, pl.ds(h * 128, 128)] = (two[:, h].reshape(512, 128) + keymask).astype(F32)

    lane8 = lax.div(lax.broadcasted_iota(jnp.int32, (8, 128), 1), 32)

    def heads(s):
        key = kb[s].reshape(512, 256)
        value = jnp.concatenate([vt[s, b] for b in range(4)], 1)
        query = qt[s]
        parts = []
        for hp in range(4):
            g, r = hp // 2, hp % 2 * 2
            zero = jnp.zeros((32, 128), BF)
            pair_q = []
            for h in range(2):
                pieces = [zero] * 4
                pieces[r + h] = query[hp * 64 + h * 32 : hp * 64 + h * 32 + 32]
                pair_q.append(jnp.concatenate(pieces, 0))
            logits = mm(key[:, g * 128 : g * 128 + 128], jnp.concatenate(pair_q, 1)) + biasb[hp]
            low = logits - jnp.max(logits, 0, keepdims=True)
            probs = jnp.exp(low).astype(BF)
            summed = mm(
                jnp.concatenate([value[hp * 64 : hp * 64 + 64], jnp.ones((16, 512), BF)], 0), probs
            )
            scale = 1.0 / summed[64:65]
            parts.append(summed[0:32, 0:128] * scale[:, 0:128])
            parts.append(summed[32:64, 128:256] * scale[:, 128:256])
        return (jnp.concatenate(parts, 0) * gate[s]).astype(BF)

    def project(s, attended):
        attended = nt(e128, attended).astype(BF)
        result = (xin[s].astype(F32) + mm(attended, weight(4))).astype(BF)
        al[rj, s] = result
        on = norm(result.astype(F32), cscale[...])
        keep = cm[ri] * rows[seq * 16 + rj * 4 + s].astype(F32)
        on = (on * jnp.concatenate([keep, keep], 1)).astype(BF)
        left = nt(p1t, on)
        right[...] = nt(on, p2r)
        for y in range(4):
            ltile = jnp.zeros((8, 128), F32)
            rtile = jnp.zeros((8, 128), F32)
            for k in range(4):
                piece = left[k * 8 : k * 8 + 8]
                if k != y:
                    piece = pltpu.roll(piece, (32 * (k - y)) % 128, 1)
                ltile = jnp.where(lane8 == k, piece, ltile)
                rtile = jnp.where(lane8 == k, right[pl.ds(y * 32 + k, 8, stride=4), :], rtile)
            sndf[y, pl.ds(pl.multiple_of(s * 8, 8), 8), :] = ltile
            sndf[y, pl.ds(pl.multiple_of(32 + s * 8, 8), 8), :] = rtile

    def attend(s, before):
        last_rows(s, 0)
        attended = heads(s)
        project(lax.rem(s + 3, 4), before)

        @pl.when(jnp.logical_and(s > 0, s < 3))
        def _():
            start_out(s - 1)

        @pl.when(s < 2)
        def _():
            far_rows(s + 2, 0)

        return attended

    a_lower, a_upper = first(64), second(64)

    def out(s, source):
        return al.at[source, s]

    def start_out(s):
        for i, (part, dev) in enumerate(
            ((a_lower, plus_y), (a_upper, minus_y), (a_upper, plus_y), (a_lower, minus_y))
        ):
            rcopy(part(out(s, rj)), part(out(s, rj)), AL + s * 6 + i, dev).start()

    def pass_out(s):
        ring_pass(
            out(s, behind(rj, 1)), out(s, ahead(rj, 1)), a_lower, a_upper, AL + s * 6,
            plus_y, minus_y,
        )

    project(3, lax.fori_loop(0, 4, attend, jnp.zeros((256, 128), BF)))

    snd[...] = sndf[...].astype(BF)

    def send_sides(n):
        rcopy(
            snd.at[ahead(rj, lax.rem(n, 4)), pl.ds(0, 32)], lraw.at[zl, rj], LL, in_zy(n)
        ).start()

    each(1, 16, send_sides)

    def send_right(n):
        @pl.when(jnp.logical_not(to_self(n)))
        def _():
            rcopy(
                snd.at[lax.div(n, 4), pl.ds(32, 32)], rraw.at[zl, rj], RR, right_to(n)
            ).start()

    each(0, 16, send_right)
    lraw[zl, rj] = snd[rj, 0:32]

    @pl.when(diagonal)
    def _():
        rraw[zl, rj] = snd[x, 32:64]

    def drain_head(s):
        for half in range(2):
            left_here(relay.at[half, s], RZ + s * 2 + half)
            left_here(relay.at[half, s], XZ + s * 2 + half)
        left_here(xn.at[s, ri], XM + s)
        left_here(xn.at[s, opp], XF + s)

    each(0, 4, drain_head)
    left_here(fifteen, BA)
    left_here(fifteen, BB)
    ring_sent(wbuf.at[rj], w_lower, w_upper, WT)
    ring_sent(bg.at[0, :, x], b_lower, b_upper, AX)
    ring_sent(bg.at[1, :, :, rj], b_lower, b_upper, BY)

    def regroup(raw, buf, place):
        def step(t):
            block = raw[t].astype(F32)
            for y in range(4):
                for s in range(4):
                    scr[pl.ds(y * 4 + s, 8, stride=16), :] = block[y, s * 8 : s * 8 + 8]
            buf[:, place, t] = scr[...].astype(BF).reshape(8, 16, 128)

        each(0, 4, step)

    q_lower, q_upper = first(4), second(4)
    arrived(fifteen, LL)
    regroup(lraw, lb, x)
    ring_start(lb.at[:, x], q_lower, q_upper, LX, plus_x, minus_x)

    @pl.when(diagonal)
    def _():
        arrived(fifteen, RR)

    @pl.when(jnp.logical_not(diagonal))
    def _():
        arrived(sixteen, RR)

    regroup(rraw, rb, rj)
    ring_start(rb.at[:, rj], q_lower, q_upper, R4, plus_y, minus_y)
    ring_pass(
        lb.at[:, behind(x, 1)], lb.at[:, ahead(x, 1)], q_lower, q_upper, LX, plus_x, minus_x
    )
    ring_pass(
        rb.at[:, behind(rj, 1)], rb.at[:, ahead(rj, 1)], q_lower, q_upper, R4, plus_y, minus_y
    )
    each(2, 4, start_out)
    each(0, 2, pass_out)
    ring_end(
        lb.at[:, behind(x, 1)], lb.at[:, ahead(x, 1)], lb.at[:, ahead(x, 2)], q_lower, q_upper, LX
    )
    ring_end(
        rb.at[:, behind(rj, 1)], rb.at[:, ahead(rj, 1)], rb.at[:, ahead(rj, 2)],
        q_lower, q_upper, R4,
    )

    lane128 = lax.div(lax.broadcasted_iota(jnp.int32, (128, 128), 1), 32)

    def product(peer, u):
        turned = nt(e128, rb[peer * 2 + u].reshape(256, 128)).astype(BF)
        for k in range(8):
            outer = mm(turned, lb[k].reshape(256, 128)).astype(BF)
            for j in range(4):
                bscr[u, j // 2, pl.ds(k * 32, 32), pl.ds((j % 2) * 128, 128)] = outer[
                    j * 32 : j * 32 + 32
                ]
        for jp in range(2):
            wide = mm(wst[...], bscr[u, jp])
            for half in range(2):
                c = half * 128
                mixed = wide[0:128, c : c + 128]
                for k in range(1, 4):
                    mixed = jnp.where(
                        lane128 == k, wide[k * 128 : k * 128 + 128, c : c + 128], mixed
                    )
                ub[peer, pl.ds(u * 4 + jp * 2 + half, 32, stride=8), :] = nt(
                    pick, mixed.astype(BF)
                )

    def write_out(s):
        return pltpu.make_async_copy(al.at[:, s], out_al.at[:, s], osem.at[s])

    def drain(s):
        ring_end(
            out(s, behind(rj, 1)), out(s, ahead(rj, 1)), out(s, ahead(rj, 2)), a_lower, a_upper,
            AL + s * 6,
        )
        write_out(s).start()

    def in_order(t):
        return jnp.where(t == 0, 2, jnp.where(t == 1, 1, t + 1))

    def for_peer(t):
        d = in_order(t)
        peer = ahead(rj, d)
        for u in range(2):
            product(peer, u)
        ubf[peer] = ub[peer].astype(BF)

        @pl.when(t < 3)
        def _():
            update_copy(d).start()

        @pl.when(t == 1)
        def _():
            each(2, 4, pass_out)

        @pl.when(t == 2)
        def _():
            each(0, 2, drain)

    def update_copy(d):
        peer = ahead(rj, d)
        return rcopy(ubf.at[peer], ugot.at[rj], UP + d - 1, {"rj": peer})

    each(0, 4, for_peer)
    ugot[rj] = ubf[rj]
    each(1, 4, lambda d: arrived(ugot.at[behind(rj, d)], UP + d - 1))
    keep = pltpu.make_async_copy(ugot, out_update, usem)
    keep.start()

    each(2, 4, drain)
    each(0, 4, lambda s: ring_sent(out(s, rj), a_lower, a_upper, AL + s * 6))
    ring_sent(lb.at[:, x], q_lower, q_upper, LX)
    ring_sent(rb.at[:, rj], q_lower, q_upper, R4)
    left_here(fifteen, LL)

    @pl.when(diagonal)
    def _():
        left_here(fifteen, RR)

    @pl.when(jnp.logical_not(diagonal))
    def _():
        left_here(sixteen, RR)

    each(1, 4, lambda d: left_here(ubf.at[ahead(rj, d)], UP + d - 1))
    keep.wait()
    each(0, 4, lambda s: write_out(s).wait())


def finish(
    al_in, update_in, pair_in, rowv_in, al_out, pair_out, al, update, pair, rowv, result, sem, back
):
    inward = [
        pltpu.make_async_copy(update_in, update, sem.at[0]),
        pltpu.make_async_copy(pair_in, pair, sem.at[1]),
        pltpu.make_async_copy(rowv_in, rowv, sem.at[2]),
    ] + [pltpu.make_async_copy(al_in.at[k], al.at[k], sem.at[3 + k]) for k in range(4)]
    outward = [pltpu.make_async_copy(al.at[k], al_out.at[k], back.at[k]) for k in range(4)]
    outward.append(pltpu.make_async_copy(result, pair_out, back.at[4]))
    for copy in inward:
        copy.start()
    for k in range(3):
        inward[k].wait()
    scale = 1.0 / jnp.maximum(jnp.sum(rowv[...].astype(F32)), 1.0)
    result[...] = (
        pair[...].astype(F32) + update[...].reshape(1024, 128).astype(F32) * scale
    ).astype(BF)
    outward[4].start()
    for k in range(4):
        inward[3 + k].wait()
        outward[k].start()
    for copy in outward:
        copy.wait()


def on_device(
    homolog_embedding,
    pairwise_state,
    residue_mask,
    alignment_row_mask,
    focus_layer_scale,
    asking_projector,
    lookup_projector,
    content_projector,
    sigmoid_projector,
    gate_offset_bias,
    final_projector,
    pairwise_norm_gain,
    bias_weight,
    cross_layer_scale,
    first_cross_projector,
    second_cross_projector,
    outer_weight,
):
    hbm = pl.BlockSpec(memory_space=pl.ANY)
    gathered, update = pl.pallas_call(
        kernel,
        out_shape=(
            jax.ShapeDtypeStruct((4, 4, 128, 256), BF),
            jax.ShapeDtypeStruct((4, 256, 128), BF),
        ),
        in_specs=[hbm] * 17,
        out_specs=(hbm, hbm),
        scratch_shapes=[
            pltpu.VMEM((4, 128, 256), BF),
            pltpu.VMEM((1024, 128), BF),
            pltpu.VMEM((4, 128), jnp.int32),
            pltpu.SMEM((256,), jnp.int32),
            pltpu.VMEM((1, 256), F32),
            pltpu.VMEM((1, 256), F32),
            pltpu.VMEM((1, 128), F32),
            pltpu.VMEM((8, 128), BF),
            pltpu.VMEM((1, 256), F32),
            pltpu.VMEM((32, 256), BF),
            pltpu.VMEM((32, 256), BF),
            pltpu.VMEM((1024, 128), BF),
            pltpu.VMEM((4, 4, 128, 256), BF),
            pltpu.VMEM((2, 4, 64, 256), BF),
            pltpu.VMEM((4, 320, 256), BF),
            pltpu.VMEM((1024, 128), F32),
            pltpu.VMEM((64, 128), F32),
            pltpu.VMEM((2, 4, 4, 4, 32, 128), BF),
            pltpu.VMEM((256, 256), BF),
            pltpu.VMEM((768, 256), BF),
            pltpu.VMEM((4, 4, 128, 256), BF),
            pltpu.VMEM((4, 256, 128), BF),
            pltpu.VMEM((4, 4, 256, 128), BF),
            pltpu.VMEM((4, 256, 128), F32),
            pltpu.VMEM((4, 512, 256), F32),
            pltpu.VMEM((256, 128), F32),
            pltpu.VMEM((4, 128, 128), F32),
            pltpu.VMEM((512, 256), BF),
            pltpu.VMEM((4, 4, 128, 256), BF),
            pltpu.VMEM((128, 128), F32),
            pltpu.VMEM((4, 64, 128), F32),
            pltpu.VMEM((4, 64, 128), BF),
            pltpu.VMEM((4, 4, 32, 128), BF),
            pltpu.VMEM((4, 4, 32, 128), BF),
            pltpu.VMEM((128, 128), F32),
            pltpu.VMEM((8, 4, 4, 16, 128), BF),
            pltpu.VMEM((8, 4, 4, 16, 128), BF),
            pltpu.VMEM((2, 2, 256, 256), BF),
            pltpu.VMEM((4, 256, 128), F32),
            pltpu.VMEM((4, 256, 128), BF),
            pltpu.VMEM((4, 256, 128), BF),
            pltpu.SemaphoreType.DMA((COUNT,)),
            pltpu.SemaphoreType.DMA((COUNT,)),
            pltpu.SemaphoreType.DMA((17,)),
            pltpu.SemaphoreType.DMA((4,)),
            pltpu.SemaphoreType.DMA,
        ],
        compiler_params=pltpu.CompilerParams(
            collective_id=0, has_side_effects=True, vmem_limit_bytes=60 * 1024 * 1024
        ),
        cost_estimate=pl.CostEstimate(
            flops=4_000_000_000, bytes_accessed=4_000_000, transcendentals=2_000_000
        ),
    )(
        homolog_embedding,
        pairwise_state.reshape(1024, 128),
        residue_mask.reshape(4, 128),
        alignment_row_mask,
        focus_layer_scale.reshape(1, 256),
        asking_projector.T,
        lookup_projector.T,
        content_projector.T,
        sigmoid_projector.T,
        gate_offset_bias.reshape(1, 256),
        final_projector,
        pairwise_norm_gain.reshape(1, 128),
        bias_weight.T,
        cross_layer_scale.reshape(1, 256),
        first_cross_projector.T,
        second_cross_projector.T,
        outer_weight,
    )
    alignment_output, pair_rows = pl.pallas_call(
        finish,
        out_shape=(
            jax.ShapeDtypeStruct((4, 4, 128, 256), BF),
            jax.ShapeDtypeStruct((1024, 128), BF),
        ),
        in_specs=[hbm] * 4,
        out_specs=(hbm, hbm),
        scratch_shapes=[
            pltpu.VMEM((4, 4, 128, 256), BF),
            pltpu.VMEM((4, 256, 128), BF),
            pltpu.VMEM((1024, 128), BF),
            pltpu.VMEM((2, 128), jnp.int32),
            pltpu.VMEM((1024, 128), BF),
            pltpu.SemaphoreType.DMA((7,)),
            pltpu.SemaphoreType.DMA((5,)),
        ],
        compiler_params=pltpu.CompilerParams(vmem_limit_bytes=60 * 1024 * 1024),
    )(gathered, update, pairwise_state.reshape(1024, 128), alignment_row_mask.reshape(2, 128))
    return alignment_output.reshape(16, 128, 256), pair_rows.reshape(128, 8, 128)


def solution(mesh):
    placed = (
        P("seq", "ri", None),
        P("ri", ("seq", "rj"), None),
        P(),
        P(),
        P(),
        P(None, "rj"),
        P(None, "rj"),
        P(None, "rj"),
        P(None, "rj"),
        P(),
        P("rj", None),
        P(),
        P(),
        P(),
        P(),
        P(),
        P(),
    )
    return jax.shard_map(
        on_device,
        mesh=mesh,
        in_specs=placed,
        out_specs=(P("seq", "ri", None), P("ri", ("seq", "rj"), None)),
        check_vma=False,
    )
```

```python
import jax
import jax.numpy as jnp
from jax import lax
from jax.experimental import pallas as pl
from jax.experimental.pallas import tpu as pltpu
from jax.sharding import PartitionSpec as P

F32 = jnp.float32
BF = jnp.bfloat16
NT = (((1,), (1,)), ((), ()))

SIZES = (8, 8, 4, 4, 6, 1, 1, 6, 6, 24, 1, 1, 6, 6, 3, 3)
RZ, XZ, XM, XF, WT, BA, BB, AX, BY, AL, LL, RR, LX, R4, UP, WM = (
    sum(SIZES[:i]) for i in range(len(SIZES))
)
COUNT = sum(SIZES)


def nt(a, b):
    return lax.dot_general(a, b, NT, preferred_element_type=F32)


def mm(a, b):
    return jnp.dot(a, b, preferred_element_type=F32)


def norm(values, gain):
    centre = values - jnp.mean(values, -1, keepdims=True)
    spread = jnp.mean(centre * centre, -1, keepdims=True)
    return centre * lax.rsqrt(spread + 1e-5) * gain


def eye(n):
    row = lax.broadcasted_iota(jnp.int32, (n, n), 0)
    col = lax.broadcasted_iota(jnp.int32, (n, n), 1)
    return (row == col).astype(F32).astype(BF)


def kernel(
    hom, pair_in, resm_in, rows_in, fscale_in, wq, wk, wv, wg, gb_in, wo, pgain_in, bw_in,
    cscale_in, p1_in, p2_in, ow_in,
    out_al, out_update,
    xin, pair, resm, rows, fscale, gb, pgain, bw, cscale, p1, p2, ow,
    xn, relay, wbuf, pn, bt, bg, wkn, wqvg, kb, qt, vt, gate, biasb, gbt, cm, wst, al, right, sndf, snd, lraw, rraw, scr, lb, rb,
    bscr, ub, ubf, ugot,
    ssem, rsem, lsem, osem, usem,
):
    seq = lax.axis_index("seq")
    ri = lax.axis_index("ri")
    rj = lax.axis_index("rj")
    zl, x = lax.div(seq, 4), lax.rem(seq, 4)
    mate = ri + 1 - 2 * lax.rem(ri, 2)
    opp = lax.rem(ri + 2, 4)
    oppmate = lax.rem(mate + 2, 4)

    def ahead(v, d):
        return lax.rem(v + d, 4)

    def behind(v, d):
        return lax.rem(v + 4 - d, 4)

    plus_y, minus_y = {"rj": ahead(rj, 1)}, {"rj": behind(rj, 1)}
    plus_x, minus_x = {"seq": zl * 4 + ahead(x, 1)}, {"seq": zl * 4 + behind(x, 1)}
    core, z = lax.rem(ri, 2), lax.div(ri, 2) * 4 + zl

    def along_z(step):
        to = lax.rem(z + step, 8)
        return lax.div(to, 4) * 2 + core, {
            "seq": lax.rem(to, 4) * 4 + x,
            "ri": lax.div(to, 4) * 2 + core,
        }

    ri_up, up = along_z(2)
    ri_down, down = along_z(6)

    def seq_of(zz, xx):
        return zz * 4 + xx

    def in_zy(n):
        return {"seq": seq_of(ahead(zl, lax.div(n, 4)), x), "rj": ahead(rj, lax.rem(n, 4))}

    def in_zx(n):
        return {"seq": seq_of(ahead(zl, lax.div(n, 4)), ahead(x, lax.rem(n, 4)))}

    def right_to(n):
        return {"seq": seq_of(ri, lax.div(n, 4)), "ri": lax.rem(n, 4), "rj": x}

    def right_from(n):
        return {"seq": seq_of(lax.div(n, 4), rj), "ri": zl, "rj": lax.rem(n, 4)}

    def each(low, high, body):
        def step(n, carry):
            body(n)
            return carry

        lax.fori_loop(low, high, step, 0)

    diagonal = jnp.logical_and(zl == ri, x == rj)

    def to_self(n):
        return jnp.logical_and(diagonal, n == seq_of(x, ri))

    def from_self(n):
        return jnp.logical_and(diagonal, n == seq_of(zl, rj))


    def rcopy(src, dst, k, dev, send=None):
        return pltpu.make_async_remote_copy(
            src_ref=src,
            dst_ref=dst,
            send_sem=ssem.at[k if send is None else send],
            recv_sem=rsem.at[k],
            device_id=dev,
            device_id_type=pl.DeviceIdType.MESH,
        )

    def arrived(ref, k):
        pltpu.make_async_copy(ref, ref, rsem.at[k]).wait()

    def left_here(ref, k):
        pltpu.make_async_copy(ref, ref, ssem.at[k]).wait()

    def ring_start(own, lower, upper, k, plus, minus):
        for i, (part, dev) in enumerate(
            ((lower, plus), (upper, minus), (upper, plus), (lower, minus))
        ):
            rcopy(part(own), part(own), k + i, dev).start()

    def ring_pass(before, after, lower, upper, k, plus, minus):
        arrived(lower(before), k)
        rcopy(lower(before), lower(before), k + 4, plus).start()
        arrived(upper(after), k + 1)
        rcopy(upper(after), upper(after), k + 5, minus).start()

    def ring_end(before, after, far, lower, upper, k):
        arrived(upper(before), k + 2)
        arrived(lower(after), k + 3)
        arrived(lower(far), k + 4)
        arrived(upper(far), k + 5)

    def ring_sent(own, lower, upper, k):
        for i, part in enumerate((lower, upper, upper, lower, lower, upper)):
            left_here(part(own), k + i)

    def first(n):
        return lambda ref: ref.at[pl.ds(0, n)]

    def second(n):
        return lambda ref: ref.at[pl.ds(n, n)]

    inward = [
        (hom.at[pl.ds(rj * 4, 4)], xin),
        (fscale_in, fscale),
        (pair_in, pair),
        (pgain_in, pgain),
        (bw_in, bw),
        (wq, wbuf.at[rj, pl.ds(0, 64)]),
        (wk, wbuf.at[rj, pl.ds(64, 64)]),
        (wv, wbuf.at[rj, pl.ds(128, 64)]),
        (wg, wbuf.at[rj, pl.ds(192, 64)]),
        (wo, wbuf.at[rj, pl.ds(256, 64)]),
        (resm_in, resm),
        (rows_in, rows),
        (gb_in, gb),
        (cscale_in, cscale),
        (p1_in, p1),
        (p2_in, p2),
        (ow_in, ow),
    ]

    def local(k):
        return pltpu.make_async_copy(inward[k][0], inward[k][1], lsem.at[k])

    for k in range(len(inward)):
        local(k).start()

    barrier = pltpu.get_barrier_semaphore()

    def greet(dev):
        pl.semaphore_signal(barrier, inc=1, device_id=dev, device_id_type=pl.DeviceIdType.MESH)

    def greet_all(n):
        greet(in_zy(n))
        greet(in_zx(n))

    each(1, 16, greet_all)
    for dev in ({"ri": mate}, up, down):
        greet(dev)

    def greet_right(n):
        @pl.when(jnp.logical_not(from_self(n)))
        def _():
            greet(right_from(n))

    each(0, 16, greet_right)

    local(0).wait()
    local(1).wait()

    def norm_x(s, carry):
        xn[s, ri] = norm(xin[s].astype(F32), fscale[...]).astype(BF)
        return carry

    lax.fori_loop(0, 4, norm_x, 0)

    for k in range(2, 5):
        local(k).wait()
    pn[...] = norm(pair[...].astype(F32), pgain[...]).astype(BF).astype(F32)
    for j in range(8):
        tile = pn[pl.ds(j, 128, stride=8), :].astype(BF)
        bt[pl.ds(j, 8, stride=8), :] = nt(bw[...], tile)
    for half in range(2):
        bg[half, zl, x, rj] = bt[pl.ds(half * 32, 32), :].astype(BF)

    pl.semaphore_wait(barrier, 49 - diagonal.astype(jnp.int32))

    def send_x(s):
        rcopy(xn.at[s, ri, pl.ds(0, 64)], relay.at[0, s], RZ + s * 2, up).start()
        rcopy(xn.at[s, ri, pl.ds(64, 64)], relay.at[1, s], RZ + s * 2 + 1, down).start()

    def relay_x(s):
        arrived(relay.at[0, s], RZ + s * 2)
        rcopy(relay.at[0, s], xn.at[s, ri_down, pl.ds(0, 64)], XZ + s * 2, up).start()
        arrived(relay.at[1, s], RZ + s * 2 + 1)
        rcopy(relay.at[1, s], xn.at[s, ri_up, pl.ds(64, 64)], XZ + s * 2 + 1, down).start()

    def send_bias(n):
        rcopy(bg.at[0, zl, x, rj], bg.at[0, zl, x, rj], BA, in_zy(n)).start()
        rcopy(bg.at[1, zl, x, rj], bg.at[1, zl, x, rj], BB, in_zx(n)).start()

    each(1, 16, send_bias)
    for s in range(2):
        send_x(s)
    for k in range(5, 10):
        local(k).wait()
    w_row = pl.multiple_of(core * 160, 16)
    w_other = pl.multiple_of(160 - core * 160, 16)
    w_lower, w_upper = first(80), second(80)

    def w_half(y):
        return wbuf.at[y, pl.ds(w_row, 160)]

    ring_start(w_half(rj), w_lower, w_upper, WT, plus_y, minus_y)
    for k in range(10, len(inward)):
        local(k).wait()

    row128 = lax.broadcasted_iota(jnp.int32, (128, 128), 0)
    col128 = lax.broadcasted_iota(jnp.int32, (128, 128), 1)
    ones = jnp.ones((128, 128), BF)
    for b in range(4):
        res = resm[pl.ds(b, 1), :].astype(F32)
        spread = jnp.where(row128 == col128, jnp.broadcast_to(res, (128, 128)), 0.0).astype(BF)
        cm[b] = mm(spread, ones)
    for b in range(2):
        gbt[pl.ds(b * 128, 128), :] = jnp.transpose(
            jnp.broadcast_to(gb[:, pl.ds(b * 128, 128)], (128, 128))
        )
    e128 = eye(128)
    for k in range(4):
        wst[pl.ds(k * 128, 128), :] = nt(e128, ow[pl.ds(k * 256, 256), :]).astype(BF)
    pick = (
        lax.broadcasted_iota(jnp.int32, (32, 128), 0)
        == lax.rem(lax.broadcasted_iota(jnp.int32, (32, 128), 1), 32)
    ).astype(F32).astype(BF)
    p1t = p1[...]
    p2r = jnp.concatenate([p2[...]] * 4, 0)

    fifteen, sixteen = bscr.at[0, 0, pl.ds(0, 240)], bscr.at[0, 0]
    arrived(fifteen, BA)
    arrived(fifteen, BB)
    b_lower, b_upper = first(2), second(2)
    ring_start(bg.at[0, :, x], b_lower, b_upper, AX, plus_x, minus_x)
    ring_start(bg.at[1, :, :, rj], b_lower, b_upper, BY, plus_y, minus_y)
    for s in range(2, 4):
        send_x(s)
    for s in range(4):
        rcopy(xn.at[s, ri], xn.at[s, ri], XM + s, {"ri": mate}).start()
    relay_x(0)
    relay_x(1)
    ring_pass(w_half(behind(rj, 1)), w_half(ahead(rj, 1)), w_lower, w_upper, WT, plus_y, minus_y)
    ring_pass(
        bg.at[0, :, behind(x, 1)], bg.at[0, :, ahead(x, 1)], b_lower, b_upper, AX, plus_x, minus_x
    )
    ring_pass(
        bg.at[1, :, :, behind(rj, 1)], bg.at[1, :, :, ahead(rj, 1)], b_lower, b_upper,
        BY, plus_y, minus_y,
    )

    relay_x(2)
    relay_x(3)

    ring_end(
        w_half(behind(rj, 1)), w_half(ahead(rj, 1)), w_half(ahead(rj, 2)), w_lower, w_upper, WT
    )
    for d in (1, 2, 3):
        y = ahead(rj, d)
        rcopy(w_half(y), w_half(y), WM + d - 1, {"ri": mate}).start()
    for d in (1, 2, 3):
        arrived(wbuf.at[ahead(rj, d), pl.ds(w_other, 160)], WM + d - 1)

    def weight(k):
        return wbuf[:, pl.ds(k * 64, 64), :].reshape(256, 256)

    wkn[...] = nt(eye(256), weight(1)).astype(BF)
    wqvg[0:256] = weight(0)
    wqvg[256:512] = weight(2)
    wqvg[512:768] = weight(3)

    def own_rows(s, carry):
        block = xn[s, ri]
        kb[s, ri] = mm(block, wkn[...]).astype(BF)
        three = nt(wqvg[...], block)
        qt[s] = (three[0:256] * 32 ** -0.5).astype(BF)
        vt[s, ri] = three[256:512].astype(BF)
        gate[s] = jax.nn.sigmoid(three[512:768] + gbt[...])
        return carry

    def other_rows(s, b):
        block = xn[s, b]
        kb[s, b] = mm(block, wkn[...]).astype(BF)
        vt[s, b] = nt(wqvg[256:512], block).astype(BF)

    lax.fori_loop(0, 4, own_rows, 0)

    def near_rows(s, carry):
        arrived(xn.at[s, mate], XM + s)
        other_rows(s, mate)
        return carry

    def far_rows(s, carry):
        arrived(xn.at[s, opp, pl.ds(0, 64)], XZ + s * 2)
        arrived(xn.at[s, opp, pl.ds(64, 64)], XZ + s * 2 + 1)
        rcopy(xn.at[s, opp], xn.at[s, opp], XF + s, {"ri": mate}).start()
        other_rows(s, opp)
        return carry

    def last_rows(s, carry):
        arrived(xn.at[s, oppmate], XF + s)
        other_rows(s, oppmate)
        return carry

    lax.fori_loop(0, 4, near_rows, 0)
    lax.fori_loop(0, 2, far_rows, 0)
    ring_end(
        bg.at[0, :, behind(x, 1)], bg.at[0, :, ahead(x, 1)], bg.at[0, :, ahead(x, 2)],
        b_lower, b_upper, AX,
    )
    ring_end(
        bg.at[1, :, :, behind(rj, 1)], bg.at[1, :, :, ahead(rj, 1)], bg.at[1, :, :, ahead(rj, 2)],
        b_lower, b_upper, BY,
    )

    keymask = (jnp.concatenate([cm[b] for b in range(4)], 0) - 1.0) * 1e9
    for hp in range(4):
        two = bg[hp // 2, :, :, :, pl.ds(hp % 2 * 16, 16), :].astype(F32).reshape(64, 2, 8, 128)
        for h in range(2):
            biasb[hp, :, pl.ds(h * 128, 128)] = (two[:, h].reshape(512, 128) + keymask).astype(F32)

    lane8 = lax.div(lax.broadcasted_iota(jnp.int32, (8, 128), 1), 32)

    def heads(s):
        key = kb[s].reshape(512, 256)
        value = jnp.concatenate([vt[s, b] for b in range(4)], 1)
        query = qt[s]
        parts = []
        for hp in range(4):
            g, r = hp // 2, hp % 2 * 2
            zero = jnp.zeros((32, 128), BF)
            pair_q = []
            for h in range(2):
                pieces = [zero] * 4
                pieces[r + h] = query[hp * 64 + h * 32 : hp * 64 + h * 32 + 32]
                pair_q.append(jnp.concatenate(pieces, 0))
            logits = mm(key[:, g * 128 : g * 128 + 128], jnp.concatenate(pair_q, 1)) + biasb[hp]
            low = logits - jnp.max(logits, 0, keepdims=True)
            probs = jnp.exp(low).astype(BF)
            summed = mm(
                jnp.concatenate([value[hp * 64 : hp * 64 + 64], jnp.ones((16, 512), BF)], 0), probs
            )
            scale = 1.0 / summed[64:65]
            parts.append(summed[0:32, 0:128] * scale[:, 0:128])
            parts.append(summed[32:64, 128:256] * scale[:, 128:256])
        return (jnp.concatenate(parts, 0) * gate[s]).astype(BF)

    def project(s, attended):
        attended = nt(e128, attended).astype(BF)
        result = (xin[s].astype(F32) + mm(attended, weight(4))).astype(BF)
        al[rj, s] = result
        on = norm(result.astype(F32), cscale[...])
        keep = cm[ri] * rows[seq * 16 + rj * 4 + s].astype(F32)
        on = (on * jnp.concatenate([keep, keep], 1)).astype(BF)
        left = nt(p1t, on)
        right[...] = nt(on, p2r)
        for y in range(4):
            ltile = jnp.zeros((8, 128), F32)
            rtile = jnp.zeros((8, 128), F32)
            for k in range(4):
                piece = left[k * 8 : k * 8 + 8]
                if k != y:
                    piece = pltpu.roll(piece, (32 * (k - y)) % 128, 1)
                ltile = jnp.where(lane8 == k, piece, ltile)
                rtile = jnp.where(lane8 == k, right[pl.ds(y * 32 + k, 8, stride=4), :], rtile)
            sndf[y, pl.ds(pl.multiple_of(s * 8, 8), 8), :] = ltile
            sndf[y, pl.ds(pl.multiple_of(32 + s * 8, 8), 8), :] = rtile

    def attend(s, before):
        last_rows(s, 0)
        attended = heads(s)
        project(lax.rem(s + 3, 4), before)

        @pl.when(s > 0)
        def _():
            start_out(s - 1)

        @pl.when(s < 2)
        def _():
            far_rows(s + 2, 0)

        return attended

    a_lower, a_upper = first(64), second(64)

    def out(s, source):
        return al.at[source, s]

    def start_out(s):
        for i, (part, dev) in enumerate(
            ((a_lower, plus_y), (a_upper, minus_y), (a_upper, plus_y), (a_lower, minus_y))
        ):
            rcopy(part(out(s, rj)), part(out(s, rj)), AL + s * 6 + i, dev).start()

    def pass_out(s):
        ring_pass(
            out(s, behind(rj, 1)), out(s, ahead(rj, 1)), a_lower, a_upper, AL + s * 6,
            plus_y, minus_y,
        )

    project(3, lax.fori_loop(0, 4, attend, jnp.zeros((256, 128), BF)))

    snd[...] = sndf[...].astype(BF)

    def send_sides(n):
        rcopy(
            snd.at[ahead(rj, lax.rem(n, 4)), pl.ds(0, 32)], lraw.at[zl, rj], LL, in_zy(n)
        ).start()

    each(1, 16, send_sides)

    def send_right(n):
        @pl.when(jnp.logical_not(to_self(n)))
        def _():
            rcopy(
                snd.at[lax.div(n, 4), pl.ds(32, 32)], rraw.at[zl, rj], RR, right_to(n)
            ).start()

    each(0, 16, send_right)
    each(0, 2, pass_out)
    start_out(3)
    lraw[zl, rj] = snd[rj, 0:32]

    @pl.when(diagonal)
    def _():
        rraw[zl, rj] = snd[x, 32:64]

    def drain_head(s):
        for half in range(2):
            left_here(relay.at[half, s], RZ + s * 2 + half)
            left_here(relay.at[half, s], XZ + s * 2 + half)
        left_here(xn.at[s, ri], XM + s)
        left_here(xn.at[s, opp], XF + s)

    each(0, 4, drain_head)
    left_here(fifteen, BA)
    left_here(fifteen, BB)
    ring_sent(w_half(rj), w_lower, w_upper, WT)
    for d in (1, 2, 3):
        left_here(w_half(ahead(rj, d)), WM + d - 1)
    ring_sent(bg.at[0, :, x], b_lower, b_upper, AX)
    ring_sent(bg.at[1, :, :, rj], b_lower, b_upper, BY)

    def regroup(raw, buf, place):
        def step(t):
            block = raw[t].astype(F32)
            for y in range(4):
                for s in range(4):
                    scr[pl.ds(y * 4 + s, 8, stride=16), :] = block[y, s * 8 : s * 8 + 8]
            buf[:, place, t] = scr[...].astype(BF).reshape(8, 16, 128)

        each(0, 4, step)

    q_lower, q_upper = first(4), second(4)
    arrived(fifteen, LL)
    regroup(lraw, lb, x)
    ring_start(lb.at[:, x], q_lower, q_upper, LX, plus_x, minus_x)

    @pl.when(diagonal)
    def _():
        arrived(fifteen, RR)

    @pl.when(jnp.logical_not(diagonal))
    def _():
        arrived(sixteen, RR)

    regroup(rraw, rb, rj)
    ring_start(rb.at[:, rj], q_lower, q_upper, R4, plus_y, minus_y)
    ring_pass(
        lb.at[:, behind(x, 1)], lb.at[:, ahead(x, 1)], q_lower, q_upper, LX, plus_x, minus_x
    )
    ring_pass(
        rb.at[:, behind(rj, 1)], rb.at[:, ahead(rj, 1)], q_lower, q_upper, R4, plus_y, minus_y
    )
    each(2, 4, pass_out)
    ring_end(
        lb.at[:, behind(x, 1)], lb.at[:, ahead(x, 1)], lb.at[:, ahead(x, 2)], q_lower, q_upper, LX
    )
    ring_end(
        rb.at[:, behind(rj, 1)], rb.at[:, ahead(rj, 1)], rb.at[:, ahead(rj, 2)],
        q_lower, q_upper, R4,
    )

    lane128 = lax.div(lax.broadcasted_iota(jnp.int32, (128, 128), 1), 32)

    def product(peer, u):
        turned = nt(e128, rb[peer * 2 + u].reshape(256, 128)).astype(BF)
        for k in range(8):
            outer = mm(turned, lb[k].reshape(256, 128)).astype(BF)
            for j in range(4):
                bscr[u, j // 2, pl.ds(k * 32, 32), pl.ds((j % 2) * 128, 128)] = outer[
                    j * 32 : j * 32 + 32
                ]
        for jp in range(2):
            wide = mm(wst[...], bscr[u, jp])
            for half in range(2):
                c = half * 128
                mixed = wide[0:128, c : c + 128]
                for k in range(1, 4):
                    mixed = jnp.where(
                        lane128 == k, wide[k * 128 : k * 128 + 128, c : c + 128], mixed
                    )
                ub[peer, pl.ds(u * 4 + jp * 2 + half, 32, stride=8), :] = nt(
                    pick, mixed.astype(BF)
                )

    def in_order(t):
        return jnp.where(t == 0, 2, jnp.where(t == 1, 1, t + 1))

    def for_peer(t):
        d = in_order(t)
        peer = ahead(rj, d)
        for u in range(2):
            product(peer, u)
        ubf[peer] = ub[peer].astype(BF)

        @pl.when(t < 3)
        def _():
            update_copy(d).start()

    def update_copy(d):
        peer = ahead(rj, d)
        return rcopy(ubf.at[peer], ugot.at[rj], UP + d - 1, {"rj": peer})

    each(0, 4, for_peer)
    ugot[rj] = ubf[rj]
    each(1, 4, lambda d: arrived(ugot.at[behind(rj, d)], UP + d - 1))
    keep = pltpu.make_async_copy(ugot, out_update, usem)
    keep.start()

    def write_out(s):
        return pltpu.make_async_copy(al.at[:, s], out_al.at[:, s], osem.at[s])

    def drain(s):
        ring_end(
            out(s, behind(rj, 1)), out(s, ahead(rj, 1)), out(s, ahead(rj, 2)), a_lower, a_upper,
            AL + s * 6,
        )
        write_out(s).start()

    each(0, 4, drain)
    each(0, 4, lambda s: ring_sent(out(s, rj), a_lower, a_upper, AL + s * 6))
    ring_sent(lb.at[:, x], q_lower, q_upper, LX)
    ring_sent(rb.at[:, rj], q_lower, q_upper, R4)
    left_here(fifteen, LL)

    @pl.when(diagonal)
    def _():
        left_here(fifteen, RR)

    @pl.when(jnp.logical_not(diagonal))
    def _():
        left_here(sixteen, RR)

    each(1, 4, lambda d: left_here(ubf.at[ahead(rj, d)], UP + d - 1))
    keep.wait()
    each(0, 4, lambda s: write_out(s).wait())


def finish(
    al_in, update_in, pair_in, rowv_in, al_out, pair_out, al, update, pair, rowv, result, sem, back
):
    inward = [
        pltpu.make_async_copy(update_in, update, sem.at[0]),
        pltpu.make_async_copy(pair_in, pair, sem.at[1]),
        pltpu.make_async_copy(rowv_in, rowv, sem.at[2]),
    ] + [pltpu.make_async_copy(al_in.at[k], al.at[k], sem.at[3 + k]) for k in range(4)]
    outward = [pltpu.make_async_copy(al.at[k], al_out.at[k], back.at[k]) for k in range(4)]
    outward.append(pltpu.make_async_copy(result, pair_out, back.at[4]))
    for copy in inward:
        copy.start()
    for k in range(3):
        inward[k].wait()
    scale = 1.0 / jnp.maximum(jnp.sum(rowv[...].astype(F32)), 1.0)
    result[...] = (
        pair[...].astype(F32) + update[...].reshape(1024, 128).astype(F32) * scale
    ).astype(BF)
    outward[4].start()
    for k in range(4):
        inward[3 + k].wait()
        outward[k].start()
    for copy in outward:
        copy.wait()


def on_device(
    homolog_embedding,
    pairwise_state,
    residue_mask,
    alignment_row_mask,
    focus_layer_scale,
    asking_projector,
    lookup_projector,
    content_projector,
    sigmoid_projector,
    gate_offset_bias,
    final_projector,
    pairwise_norm_gain,
    bias_weight,
    cross_layer_scale,
    first_cross_projector,
    second_cross_projector,
    outer_weight,
):
    hbm = pl.BlockSpec(memory_space=pl.ANY)
    gathered, update = pl.pallas_call(
        kernel,
        out_shape=(
            jax.ShapeDtypeStruct((4, 4, 128, 256), BF),
            jax.ShapeDtypeStruct((4, 256, 128), BF),
        ),
        in_specs=[hbm] * 17,
        out_specs=(hbm, hbm),
        scratch_shapes=[
            pltpu.VMEM((4, 128, 256), BF),
            pltpu.VMEM((1024, 128), BF),
            pltpu.VMEM((4, 128), jnp.int32),
            pltpu.SMEM((256,), jnp.int32),
            pltpu.VMEM((1, 256), F32),
            pltpu.VMEM((1, 256), F32),
            pltpu.VMEM((1, 128), F32),
            pltpu.VMEM((8, 128), BF),
            pltpu.VMEM((1, 256), F32),
            pltpu.VMEM((32, 256), BF),
            pltpu.VMEM((32, 256), BF),
            pltpu.VMEM((1024, 128), BF),
            pltpu.VMEM((4, 4, 128, 256), BF),
            pltpu.VMEM((2, 4, 64, 256), BF),
            pltpu.VMEM((4, 320, 256), BF),
            pltpu.VMEM((1024, 128), F32),
            pltpu.VMEM((64, 128), F32),
            pltpu.VMEM((2, 4, 4, 4, 32, 128), BF),
            pltpu.VMEM((256, 256), BF),
            pltpu.VMEM((768, 256), BF),
            pltpu.VMEM((4, 4, 128, 256), BF),
            pltpu.VMEM((4, 256, 128), BF),
            pltpu.VMEM((4, 4, 256, 128), BF),
            pltpu.VMEM((4, 256, 128), F32),
            pltpu.VMEM((4, 512, 256), F32),
            pltpu.VMEM((256, 128), F32),
            pltpu.VMEM((4, 128, 128), F32),
            pltpu.VMEM((512, 256), BF),
            pltpu.VMEM((4, 4, 128, 256), BF),
            pltpu.VMEM((128, 128), F32),
            pltpu.VMEM((4, 64, 128), F32),
            pltpu.VMEM((4, 64, 128), BF),
            pltpu.VMEM((4, 4, 32, 128), BF),
            pltpu.VMEM((4, 4, 32, 128), BF),
            pltpu.VMEM((128, 128), F32),
            pltpu.VMEM((8, 4, 4, 16, 128), BF),
            pltpu.VMEM((8, 4, 4, 16, 128), BF),
            pltpu.VMEM((2, 2, 256, 256), BF),
            pltpu.VMEM((4, 256, 128), F32),
            pltpu.VMEM((4, 256, 128), BF),
            pltpu.VMEM((4, 256, 128), BF),
            pltpu.SemaphoreType.DMA((COUNT,)),
            pltpu.SemaphoreType.DMA((COUNT,)),
            pltpu.SemaphoreType.DMA((17,)),
            pltpu.SemaphoreType.DMA((4,)),
            pltpu.SemaphoreType.DMA,
        ],
        compiler_params=pltpu.CompilerParams(
            collective_id=0, has_side_effects=True, vmem_limit_bytes=60 * 1024 * 1024
        ),
        cost_estimate=pl.CostEstimate(
            flops=4_000_000_000, bytes_accessed=4_000_000, transcendentals=2_000_000
        ),
    )(
        homolog_embedding,
        pairwise_state.reshape(1024, 128),
        residue_mask.reshape(4, 128),
        alignment_row_mask,
        focus_layer_scale.reshape(1, 256),
        asking_projector.T,
        lookup_projector.T,
        content_projector.T,
        sigmoid_projector.T,
        gate_offset_bias.reshape(1, 256),
        final_projector,
        pairwise_norm_gain.reshape(1, 128),
        bias_weight.T,
        cross_layer_scale.reshape(1, 256),
        first_cross_projector.T,
        second_cross_projector.T,
        outer_weight,
    )
    alignment_output, pair_rows = pl.pallas_call(
        finish,
        out_shape=(
            jax.ShapeDtypeStruct((4, 4, 128, 256), BF),
            jax.ShapeDtypeStruct((1024, 128), BF),
        ),
        in_specs=[hbm] * 4,
        out_specs=(hbm, hbm),
        scratch_shapes=[
            pltpu.VMEM((4, 4, 128, 256), BF),
            pltpu.VMEM((4, 256, 128), BF),
            pltpu.VMEM((1024, 128), BF),
            pltpu.VMEM((2, 128), jnp.int32),
            pltpu.VMEM((1024, 128), BF),
            pltpu.SemaphoreType.DMA((7,)),
            pltpu.SemaphoreType.DMA((5,)),
        ],
        compiler_params=pltpu.CompilerParams(vmem_limit_bytes=60 * 1024 * 1024),
    )(gathered, update, pairwise_state.reshape(1024, 128), alignment_row_mask.reshape(2, 128))
    return alignment_output.reshape(16, 128, 256), pair_rows.reshape(128, 8, 128)


def solution(mesh):
    placed = (
        P("seq", "ri", None),
        P("ri", ("seq", "rj"), None),
        P(),
        P(),
        P(),
        P(None, "rj"),
        P(None, "rj"),
        P(None, "rj"),
        P(None, "rj"),
        P(),
        P("rj", None),
        P(),
        P(),
        P(),
        P(),
        P(),
        P(),
    )
    return jax.shard_map(
        on_device,
        mesh=mesh,
        in_specs=placed,
        out_specs=(P("seq", "ri", None), P("ri", ("seq", "rj"), None)),
        check_vma=False,
    )
```
